32 devices in a mesh: dp: 8 (over z, y), seq: 4 (over x, core).
Axes of the slice: x: 2, y: 2, z: 4, core: 2. Of those that a mesh axis runs over, the one named last changes fastest.
Arguments:
- target: bfloat16 [8, 2048, 512], P('dp', 'seq'), may hold values from -6 to 6
- memory: bfloat16 [8, 2048, 512], P('dp', 'seq'), may hold values from -6 to 6
- cotangent: bfloat16 [8, 2048, 512], P('dp', 'seq'), may hold values from -6 to 6
- target_segments: int32 [8, 2048], P('dp'), may hold values from 0 to 7, as said below
- source_segments: int32 [8, 2048], P('dp'), may hold values from 0 to 7, as said below
- target_lengths: int32 [8], P('dp'), may hold values from 1 to 2048, as said below
- source_lengths: int32 [8], P('dp'), may hold values from 1 to 2048, as said below
- self_inproj: bfloat16 [512, 1536], replicated, may hold values from -0.25 to 0.25
- self_outproj: bfloat16 [512, 512], replicated, may hold values from -2 to 2
- cross_query: bfloat16 [512, 512], replicated, may hold values from -0.25 to 0.25
- cross_keyval: bfloat16 [512, 1024], replicated, may hold values from -0.25 to 0.25
- cross_outproj: bfloat16 [512, 512], replicated, may hold values from -2 to 2
- ffn_expand: bfloat16 [512, 2048], replicated, may hold values from -0.25 to 0.25
- ffn_reduce: bfloat16 [2048, 512], replicated, may hold values from -0.125 to 0.125
- expand_bias: bfloat16 [1, 2048], replicated, may hold values from -1.796875 to 1.796875
- proj_bias: bfloat16 [7, 512], replicated, may hold values from -0.59765625 to 0.59765625
- norm_gain: bfloat16 [3, 512], replicated, may hold values from 0.5 to 1.5
- norm_shift: bfloat16 [3, 512], replicated, may hold values from -1.1953125 to 1.1953125
Outputs:
- layer_out: bfloat16 [8, 2048, 512], P('dp', 'seq')
- target_grad: float32 [8, 2048, 512], P('dp', 'seq')
- memory_grad: float32 [8, 2048, 512], P('dp', 'seq')
- grad_self_inproj: float32 [512, 1536], P(None, 'seq')
- grad_self_outproj: float32 [512, 512], P(None, 'seq')
- grad_cross_query: float32 [512, 512], P(None, 'seq')
- grad_cross_keyval: float32 [512, 1024], P(None, 'seq')
- grad_cross_outproj: float32 [512, 512], P(None, 'seq')
- grad_ffn_expand: float32 [512, 2048], P(None, 'seq')
- grad_ffn_reduce: float32 [2048, 512], P(None, 'seq')
- grad_expand_bias: float32 [1, 2048], P(None, 'seq')
- grad_proj_bias: float32 [7, 512], P(None, 'seq')
- grad_norm_gain: float32 [3, 512], P(None, 'seq')
- grad_norm_shift: float32 [3, 512], P(None, 'seq')
The draws below stay inside these ranges and needn't reach their ends.
Inputs may be any that keep to these rules, and one draw needn't show every extreme that they name: `target_segments`: within a row the numbers never fall along the positions, and every number from 0 to 7 occurs both below the row's target length here and below its source length in source_segments. `source_segments`: within a row the numbers never fall along the positions, and every number from 0 to 7 occurs below the row's source length. `target_lengths`: positions of a row from this number on are padding. `source_lengths`: positions of a row from this number on are padding.
All inputs are finite; a program needn't handle non-finite values.
Results may differ from the reference program's by a relative error of at most 0.025.
Values may be sent and summed in bfloat16 or wider, within the bound.
No kernel may reach another device: no remote copies, remote signals or barrier semaphores. Data moves between devices by JAX's collectives and lax.ppermute only.
A program may use at most 192 MiB of HBM per device.

```python
import jax
import jax.numpy as jnp
from jax import lax

D = 512
HEADS = 8
HEAD_DIM = 64
FF = 2048
LEN_DEV = 512
ROW_LEN = 2048
ROWS = 8
N_SEQ = 4


def packing(key, constant):
    key = jax.random.fold_in(key, constant)
    shard_len = LEN_DEV
    full_length = LEN_DEV * N_SEQ
    lead_step = max(shard_len // 8, 1)
    tail_step = max(shard_len // 16, 1)
    leading = jnp.cumsum(jax.random.randint(jax.random.fold_in(key, 1), (ROWS, 3), 0, lead_step) + 1, axis=1)
    long_end = full_length - shard_len // 2 - jax.random.randint(jax.random.fold_in(key, 2), (ROWS, 1), 0, lead_step)
    trailing = long_end + jnp.cumsum(jax.random.randint(jax.random.fold_in(key, 3), (ROWS, 3), 0, tail_step) + 1, axis=1)
    lengths = trailing[:, 2] + 1 + jax.random.randint(jax.random.fold_in(key, 4), (ROWS,), 0, tail_step)
    bounds = jnp.concatenate([leading, long_end, trailing], axis=1)
    positions = jnp.arange(full_length, dtype=jnp.int32)
    segments = jnp.sum((positions[None, :, None] >= bounds[:, None, :]).astype(jnp.int32), axis=2)
    return (segments.astype(jnp.int32), lengths.astype(jnp.int32))


def draw_target_segments(key, part):
    return packing(key, 11)[0]


def draw_target_lengths(key, part):
    return packing(key, 11)[1]


def draw_source_segments(key, part):
    return packing(key, 12)[0]


def draw_source_lengths(key, part):
    return packing(key, 12)[1]


def level_of(rng, dims, split, low, largest):
    def one(axis_at, blocks):
        heights = jax.random.uniform(jax.random.fold_in(jax.random.fold_in(rng, 6), axis_at), (blocks,), jnp.float32, low / len(split), largest / len(split))
        return jnp.repeat(jnp.exp(heights), dims[axis_at] // blocks).reshape((-1,) + (1,) * (len(dims) - axis_at - 1))

    factor_of = one(*split[0])
    for cut in split[1:]:
        factor_of = factor_of * one(*cut)
    return factor_of


def noise(stream_key, dims, scale, most, pieces=(), kind=jnp.bfloat16):
    entries = jax.random.normal(stream_key, dims, jnp.float32) * scale
    if len(pieces) > 0:
        entries = level_of(stream_key, dims, pieces, -0.22, 0.18) * entries
    return jnp.clip(entries, min=-most, max=most).astype(kind)


def setup_inputs(seed: int = 0) -> dict:
    streams_of = jax.random.split(jax.random.key(seed), 19)
    return {
        "target": noise(streams_of[0], (ROWS, ROW_LEN, D), 1.0, 6.0, ((0, 8), (1, 4))),
        "memory": noise(streams_of[1], (ROWS, ROW_LEN, D), 1.0, 6.0, ((0, 8), (1, 4))),
        "cotangent": noise(streams_of[2], (ROWS, ROW_LEN, D), 1.0, 6.0, ((0, 8), (1, 4))),
        "target_segments": draw_target_segments(jax.random.fold_in(streams_of[18], 71), 0),
        "source_segments": draw_source_segments(jax.random.fold_in(streams_of[18], 71), 0),
        "target_lengths": draw_target_lengths(jax.random.fold_in(streams_of[18], 71), 0),
        "source_lengths": draw_source_lengths(jax.random.fold_in(streams_of[18], 71), 0),
        "self_inproj": noise(streams_of[7], (D, 3 * D), D ** -0.5, 0.25),
        "self_outproj": noise(streams_of[8], (D, D), (D // 64) ** -0.5, 2.0),
        "cross_query": noise(streams_of[9], (D, D), D ** -0.5, 0.25),
        "cross_keyval": noise(streams_of[10], (D, 2 * D), D ** -0.5, 0.25),
        "cross_outproj": noise(streams_of[11], (D, D), (D // 64) ** -0.5, 2.0),
        "ffn_expand": noise(streams_of[12], (D, FF), D ** -0.5, 0.25),
        "ffn_reduce": noise(streams_of[13], (FF, D), FF ** -0.5, 0.125),
        "expand_bias": noise(streams_of[14], (1, FF), 0.3, 1.796875),
        "proj_bias": noise(streams_of[15], (7, D), 0.1, 0.59765625),
        "norm_gain": jnp.clip(1.0 + 0.1 * jax.random.normal(streams_of[16], (3, D), jnp.float32), 0.5, 1.5).astype(jnp.bfloat16),
        "norm_shift": noise(streams_of[17], (3, D), 0.2, 1.1953125),
    }


EPSILON = 1e-05
NEGATIVE = -1e+30
HIGHEST = lax.Precision.HIGHEST

@jax.custom_vjp
def low(v):
    return lax.optimization_barrier(v.astype(jnp.bfloat16)).astype(jnp.float32)

@jax.custom_vjp
def low_back(v):
    return v

def low_keep(v):
    return (low(v), None)

def low_pass(kept, grad):
    return (grad,)

def back_keep(v):
    return (v, None)

def back_low(kept, grad):
    return (low(grad),)
low.defvjp(low_keep, low_pass)
low_back.defvjp(back_keep, back_low)

def both_ways(value):
    return low(low_back(value))

def layer_norm(hidden, gain_row, shift_row):
    center = hidden - lax.optimization_barrier(jnp.mean(hidden, axis=-1, keepdims=True))
    spread = lax.rsqrt(lax.optimization_barrier(jnp.mean(center * center, axis=-1, keepdims=True)) + EPSILON)
    return center * spread * gain_row + shift_row

def linear(inputs, matrix):
    return jnp.dot(inputs, matrix, precision=HIGHEST)

def attention(queries, key_rows, value_rows, visible):
    length = queries.shape[0]
    query_heads = queries.reshape(length, HEADS, HEAD_DIM)
    key_heads = key_rows.reshape(key_rows.shape[0], HEADS, HEAD_DIM)
    value_heads = value_rows.reshape(value_rows.shape[0], HEADS, HEAD_DIM)
    scores = jnp.einsum('qhd,khd->hqk', query_heads, key_heads, precision=HIGHEST) * HEAD_DIM ** (-0.5)
    scores = jnp.where(visible[None], low_back(scores), NEGATIVE)
    shares = low(jax.nn.softmax(scores, axis=-1))
    mixed = jnp.einsum('hqk,khd->qhd', shares, value_heads, precision=HIGHEST)
    return both_ways(mixed.reshape(length, HEADS * HEAD_DIM))

def one_row(weight_set, row_inputs):
    self_inproj, self_outproj, cross_query, cross_keyval, cross_outproj, ffn_expand, ffn_reduce, expand_bias, proj_bias, norm_gain, norm_shift = weight_set
    target_row, memory_row, target_ids, source_ids, target_count, source_count = row_inputs
    model_dim = target_row.shape[-1]
    positions = jnp.arange(target_row.shape[0], dtype=jnp.int32)
    self_visible = (target_ids[:, None] == target_ids[None, :]) & (positions[None, :] <= positions[:, None]) & (positions[None, :] < target_count)
    cross_visible = (target_ids[:, None] == source_ids[None, :]) & (positions[None, :] < source_count)
    self_queries = both_ways(linear(target_row, self_inproj[:, :model_dim]) + proj_bias[0])
    self_keys = both_ways(linear(target_row, self_inproj[:, model_dim:2 * model_dim]))
    self_values = both_ways(linear(target_row, self_inproj[:, 2 * model_dim:]) + proj_bias[1])
    self_mixed = attention(self_queries, self_keys, self_values, self_visible)
    first_branch = low_back(linear(self_mixed, self_outproj) + proj_bias[2])
    first_norm = layer_norm(target_row + first_branch, norm_gain[0], norm_shift[0])
    cross_queries = both_ways(linear(low(first_norm), cross_query) + proj_bias[3])
    memory_keys = both_ways(linear(memory_row, cross_keyval[:, :model_dim]))
    memory_values = both_ways(linear(memory_row, cross_keyval[:, model_dim:]) + proj_bias[4])
    cross_mixed = attention(cross_queries, memory_keys, memory_values, cross_visible)
    second_branch = low_back(linear(cross_mixed, cross_outproj) + proj_bias[5])
    second_norm = layer_norm(first_norm + second_branch, norm_gain[1], norm_shift[1])
    expanded = low_back(linear(low(second_norm), ffn_expand) + expand_bias[0])
    activated = low(jax.nn.gelu(expanded))
    third_branch = low_back(linear(activated, ffn_reduce) + proj_bias[6])
    return layer_norm(second_norm + third_branch, norm_gain[2], norm_shift[2])

def reference(target, memory, cotangent, target_segments, source_segments, target_lengths, source_lengths, self_inproj, self_outproj, cross_query, cross_keyval, cross_outproj, ffn_expand, ffn_reduce, expand_bias, proj_bias, norm_gain, norm_shift):
    weights = tuple((matrix.astype(jnp.float32) for matrix in (self_inproj, self_outproj, cross_query, cross_keyval, cross_outproj, ffn_expand, ffn_reduce, expand_bias, proj_bias, norm_gain, norm_shift)))

    def forward(target_float, memory_float, weight_set):

        def per_row(row_inputs):
            return one_row(weight_set, row_inputs)
        return lax.map(jax.checkpoint(per_row), (target_float, memory_float, target_segments, source_segments, target_lengths, source_lengths))
    result, backward = jax.vjp(forward, target.astype(jnp.float32), memory.astype(jnp.float32), weights)
    positions = jnp.arange(target.shape[1], dtype=jnp.int32)
    row_valid = (positions[None, :] < target_lengths[:, None]).astype(jnp.float32)
    target_grad, memory_grad, weight_grads = backward(cotangent.astype(jnp.float32) * row_valid[:, :, None])
    return (result.astype(jnp.bfloat16), target_grad, memory_grad, weight_grads[0], weight_grads[1], weight_grads[2], weight_grads[3], weight_grads[4], weight_grads[5], weight_grads[6], weight_grads[7], weight_grads[8], weight_grads[9], weight_grads[10])
```

```python
import functools
import jax
import jax.numpy as jnp
from jax import lax
from jax.experimental import pallas as pl
from jax.experimental.pallas import tpu as pltpu
from jax.sharding import PartitionSpec as P

BF16 = jnp.bfloat16
F32 = jnp.float32
EPSILON = 1e-05
BK = 256
RT = 256
NT = (((1,), (1,)), ((), ()))
NN = (((1,), (0,)), ((), ()))
TN = (((0,), (0,)), ((), ()))


def dot(a, b, dims=NN):
    return lax.dot_general(a, b, dims, preferred_element_type=F32)


class Held:
    def __init__(self, copy, ref):
        self.copy, self.ref, self.waited = copy, ref, False

    def get(self):
        if not self.waited:
            self.copy.wait()
            self.waited = True
        return self.ref


class Result:
    def __init__(self, copy, ref):
        self.copy, self.ref, self.started = copy, ref, False

    def send(self):
        self.copy.start()
        self.started = True


def call(body, rng, ins, outs, scratch, deps=(), flops=10**9, vmem=24):
    arrays, columns = [], []
    for x in ins:
        x, cut = x if isinstance(x, tuple) else (x, None)
        arrays.append(x)
        columns.append(cut)
    shapes = []
    for x, cut in zip(arrays, columns):
        shapes.append(x.shape if cut is None else x.shape[:-1] + (cut.size,))
    n_in, n_dep, n_out, n_scr = len(ins), len(deps), len(outs), len(scratch)

    def kernel(rng_ref, *refs):
        hbm_in, refs = refs[:n_in], refs[n_in + n_dep :]
        hbm_out, refs = refs[:n_out], refs[n_out:]
        vm_in, refs = refs[:n_in], refs[n_in:]
        vm_out, refs = refs[:n_out], refs[n_out:]
        scr, refs = refs[:n_scr], refs[n_scr:]
        sem_in, sem_out = refs
        held = []
        for i, (src, dst, cut) in enumerate(zip(hbm_in, vm_in, columns)):
            if cut is not None:
                src = src.at[(slice(None),) * (len(src.shape) - 1) + (cut,)]
            copy = pltpu.make_async_copy(src, dst, sem_in.at[i])
            copy.start()
            held.append(Held(copy, dst))
        results = [
            Result(pltpu.make_async_copy(src, dst, sem_out.at[i]), src)
            for i, (src, dst) in enumerate(zip(vm_out, hbm_out))
        ]
        body(rng_ref, held, results, *scr)
        for x in held:
            x.get()
        for x in results:
            if not x.started:
                x.send()
        for x in results:
            x.copy.wait()

    hbm = pl.BlockSpec(memory_space=pltpu.HBM)
    return pl.pallas_call(
        kernel,
        out_shape=tuple(pltpu.HBM(s, d) for s, d in outs),
        in_specs=[pl.BlockSpec(memory_space=pltpu.SMEM)] + [hbm] * (n_in + n_dep),
        out_specs=(hbm,) * n_out,
        scratch_shapes=[pltpu.VMEM(s, x.dtype) for s, x in zip(shapes, arrays)]
        + [pltpu.VMEM(s, d) for s, d in outs]
        + [pltpu.VMEM(s, d) for s, d in scratch]
        + [pltpu.SemaphoreType.DMA((n_in,)), pltpu.SemaphoreType.DMA((n_out,))],
        compiler_params=pltpu.CompilerParams(vmem_limit_bytes=vmem * 2**20),
        cost_estimate=pl.CostEstimate(flops=flops, bytes_accessed=2**20, transcendentals=0),
    )(rng, *[pltpu.with_memory_space_constraint(x, pltpu.HBM) for x in (*arrays, *deps)])


LO0, HI0, LO1, HI1, SHARD, VALID = range(6)


def half_masks():
    lane = lax.broadcasted_iota(jnp.int32, (1, 128), 1)
    return (lane < 64, lane >= 64), lane % 64


def relative_offset(block, shard, per_shard):
    owner = lax.div(block, per_shard)
    return pl.multiple_of(((owner ^ shard) * per_shard + lax.rem(block, per_shard)) * BK, BK)


def triangle(transposed):
    a = lax.broadcasted_iota(jnp.int32, (BK, BK), 0)
    b = lax.broadcasted_iota(jnp.int32, (BK, BK), 1)
    return a <= b if transposed else b <= a


def attend(rng, q_ref, fq_ref, k_ref, v_ref, fk_ref, o_ref, lse_ref, qh, s_scr, mx, acc, causal):
    length, width = q_ref.shape
    per = length // BK
    shard = rng[SHARD]
    conds, _ = half_masks()
    heads = [(j, h) for j in range(2) for h in range(2)]
    for g in range(width // 256):
        for half in range(length // RT):
            rows = slice(half * RT, (half + 1) * RT)
            fq = fq_ref[rows]
            for i, (j, h) in enumerate(heads):
                c = g * 256 + j * 128
                qh[i] = jnp.where(conds[h], q_ref[rows, c : c + 128], fq)
                mx[i] = jnp.full((RT, 128), -3e38, F32)
                acc[i] = jnp.zeros((RT, 128), F32)

            def scores(off, slot, diagonal, g=g):
                fk = fk_ref[pl.ds(off, BK), :]
                for i, (j, h) in enumerate(heads):
                    c = g * 256 + j * 128
                    kh = jnp.where(conds[h], k_ref[pl.ds(off, BK), c : c + 128], fk)
                    s = dot(qh[i], kh, NT)
                    if diagonal:
                        s = jnp.where(triangle(False), s, -1e30)
                    s_scr[i, slot] = s
                    m = mx[i]
                    for t in range(0, BK, 128):
                        m = jnp.maximum(m, s[:, t : t + 128])
                    mx[i] = m

            def values(off, slot, g=g):
                for i, (j, h) in enumerate(heads):
                    c = g * 256 + j * 128
                    vp = v_ref[pl.ds(off, BK), c : c + 128]
                    vh = jnp.where(conds[h], vp, jnp.ones_like(vp))
                    m = mx[i]
                    p = jnp.concatenate(
                        [
                            jnp.exp(s_scr[i, slot, :, t : t + 128] - m).astype(BF16)
                            for t in range(0, BK, 128)
                        ],
                        axis=1,
                    )
                    acc[i] += dot(p, vh)

            lo = rng[LO0 + 2 * half]
            hi = shard * per + half if causal else rng[HI0 + 2 * half]

            def first(kb, carry):
                scores(relative_offset(kb, shard, per), kb, False)
                return carry

            def second(kb, carry):
                values(relative_offset(kb, shard, per), kb)
                return carry

            lax.fori_loop(lo, hi, first, 0)
            if causal:
                scores(half * BK, hi, True)
            for i in range(4):
                mx[i] = jnp.broadcast_to(jnp.max(mx[i], axis=-1, keepdims=True), (RT, 128))
            lax.fori_loop(lo, hi, second, 0)
            if causal:
                values(half * BK, hi)
            for j in range(2):
                c = g * 256 + j * 128
                a, b = 2 * j, 2 * j + 1
                num = jnp.where(conds[0], acc[a], acc[b])
                den = jnp.where(conds[0], acc[b], acc[a])
                o_ref[rows, c : c + 128] = (num / pltpu.roll(den, 64, 1)).astype(BF16)
                lse_ref[2 * g + j, rows] = jnp.where(conds[0], mx[b], mx[a]) + jnp.log(den)


def attend_scratch(length, full):
    return [
        ((4, RT, 128), BF16),
        ((4, full // BK, RT, BK), F32),
        ((4, RT, 128), F32),
        ((4, RT, 128), F32),
    ]


def attend_back(rng, q, fq, logsum, do, o, k_ref, v_ref, fk_ref, dkv_ref, qh, doh, qm, dom, dq_scr, causal):
    length = q.shape[0]
    per = length // BK
    shard = rng[SHARD]
    conds, l64 = half_masks()
    prod = do.astype(F32) * o.astype(F32)
    delta = jnp.where(
        conds[0],
        jnp.sum(jnp.where(conds[1], prod, 0.0), axis=-1, keepdims=True),
        jnp.sum(jnp.where(conds[0], prod, 0.0), axis=-1, keepdims=True),
    )

    def negated_parts(x):
        high = x.astype(BF16).astype(F32)
        rest = x - high
        mid = rest.astype(BF16).astype(F32)
        low = rest - mid
        return -jnp.where(
            l64 == 8, high, jnp.where(l64 == 9, mid, jnp.where(l64 == 10, low, 0.0))
        )

    fl = (negated_parts(logsum) + fq.astype(F32)).astype(BF16)
    fd = negated_parts(delta).astype(BF16)
    zero = jnp.zeros_like(q)
    for h in range(2):
        qh[h] = jnp.where(conds[h], q, fl)
        doh[h] = jnp.where(conds[h], do, fd)
        qm[h] = jnp.where(conds[h], q, zero)
        dom[h] = jnp.where(conds[h], do, zero)
    dq_scr[...] = jnp.zeros_like(dq_scr)
    ones = jnp.where((l64 >= 8) & (l64 <= 10), 1.0, 0.0).astype(BF16)

    def block(off, halves, diagonal=None):
        kp = k_ref[pl.ds(off, BK), :]
        vp = v_ref[pl.ds(off, BK), :]
        fk = fk_ref[pl.ds(off, BK), :]
        ones_block = jnp.broadcast_to(ones, vp.shape)
        dk = jnp.zeros((BK, 128), F32)
        dv = jnp.zeros((BK, 128), F32)
        for h in range(2):
            kh = jnp.where(conds[h], kp, fk)
            vh = jnp.where(conds[h], vp, ones_block)
            kt = jnp.where(conds[h], kp, jnp.zeros_like(kp)).T
            for half in halves:
                r = half * RT
                s = dot(kh, qh[h, r : r + RT], NT)
                if diagonal == half:
                    s = jnp.where(triangle(True), s, -1e30)
                p = jnp.exp(s)
                dp = dot(vh, doh[h, r : r + RT], NT)
                ds = (p * dp).astype(BF16)
                dv += dot(p.astype(BF16), dom[h, r : r + RT])
                dk += dot(ds, qm[h, r : r + RT])
                dq_scr[:, r : r + RT] += dot(kt, ds)
        dkv_ref[pl.ds(off, BK), 0:128] = dk.astype(BF16)
        dkv_ref[pl.ds(off, BK), 128:256] = dv.astype(BF16)

    def sweep(lo, hi, halves):
        def step(kb, carry):
            block(relative_offset(kb, shard, per), halves)
            return carry

        lax.fori_loop(lo, hi, step, 0)

    lo0, lo1 = rng[LO0], rng[LO1]
    if causal:
        own = shard * per
        sweep(lo0, jnp.minimum(lo1, own), (0,))
        sweep(lo1, own, (0, 1))
        block(0, (0, 1), 0)
        block(BK, (1,), 1)
    else:
        hi0, hi1 = rng[HI0], rng[HI1]
        sweep(lo0, jnp.minimum(lo1, hi0), (0,))
        sweep(lo1, hi0, (0, 1))
        sweep(jnp.maximum(hi0, lo1), hi1, (1,))
    return dq_scr[...].T * 0.125


def norm_rows(hidden):
    center = hidden - jnp.mean(hidden, axis=-1, keepdims=True)
    spread = lax.rsqrt(jnp.mean(center * center, axis=-1, keepdims=True) + EPSILON)
    return center * spread, spread


def norm_rows_back(upstream, normed, spread, gain):
    scaled = upstream * gain
    return spread * (
        scaled
        - jnp.mean(scaled, axis=-1, keepdims=True)
        - normed * jnp.mean(scaled * normed, axis=-1, keepdims=True)
    )


def put_block(keep_ref, send_ref, m, rows, value):
    def keep():
        keep_ref[m // 2, rows] = value

    def send():
        send_ref[m // 2, rows] = value

    pl.when(m % 2 == 0)(keep)
    pl.when(m % 2 == 1)(send)


def row_of(ref, i):
    return ref[i : i + 1, :].astype(F32)


def self_body(rng, held, results, qh, s_scr, mx, acc):
    x0, win, pb, x1, x2, x3, fq, fk, wout, wq, gain, shift = held
    q, k, v, o, lse, a, n_out, r_out, q2_out = results
    length, width = x0.ref.shape
    shard = rng[SHARD]
    eighth = jnp.asarray(0.125, BF16)
    x_ref, win_ref, pb_ref = x0.get(), win.get(), pb.get()
    for r in range(0, length, RT):
        rows = slice(r, r + RT)
        q.ref[rows] = (dot(x_ref[rows], win_ref[:, :width]) + row_of(pb_ref, 0)).astype(BF16) * eighth
    q.send()
    for m, x in enumerate((x0, x1, x2, x3)):
        x_m = x.get()

        def fill(m=m, x_m=x_m):
            for r in range(0, length, RT):
                x = x_m[r : r + RT]
                rows = slice(m * length + r, m * length + r + RT)
                k.ref[rows] = dot(x, win_ref[:, width : 2 * width]).astype(BF16)
                v.ref[rows] = (dot(x, win_ref[:, 2 * width :]) + row_of(pb_ref, 1)).astype(BF16)

        if m == 0:
            fill()
        else:
            pl.when((shard ^ m) < shard)(fill)
    k.send()
    v.send()
    attend(rng, q.ref, fq.get(), k.ref, v.ref, fk.get(), o.ref, lse.ref, qh, s_scr, mx, acc, True)
    o.send()
    lse.send()
    wout_ref, wq_ref, gain_ref, shift_ref = wout.get(), wq.get(), gain.get(), shift.get()
    for r in range(0, length, RT):
        rows = slice(r, r + RT)
        h = x_ref[rows].astype(F32) + dot(o.ref[rows], wout_ref[...]) + row_of(pb_ref, 2)
        n, spread = norm_rows(h)
        a_new = n * row_of(gain_ref, 0) + row_of(shift_ref, 0)
        n_out.ref[rows] = n
        r_out.ref[rows] = jnp.broadcast_to(spread, (RT, 128))
        a.ref[rows] = a_new
        q2 = dot(a_new.astype(BF16), wq_ref[...]) + row_of(pb_ref, 3)
        q2_out.ref[rows] = q2.astype(BF16) * eighth


def self_forward(rng, parts, fq, fk, win, wout, wq, pb, gain, shift):
    length, width = parts[0].shape
    full = len(parts) * length
    return call(
        self_body,
        rng,
        [parts[0], win, pb, *parts[1:], fq, fk, wout, wq, gain, shift],
        [
            ((length, width), BF16), ((full, width), BF16), ((full, width), BF16),
            ((length, width), BF16), ((width // 128, length, 128), F32), ((length, width), F32),
            ((length, width), F32), ((length, 128), F32), ((length, width), BF16),
        ],
        attend_scratch(length, full),
        flops=14 * 10**9,
        vmem=40,
    )


GELU_A = 0.7978845608028654
GELU_B = 0.044715


def cross_body(rng, held, results, qh, s_scr, mx, acc, n1, r1, a2, a2t, act, gp, y_scr, dy_scr):
    wkv, pb, y0, y1, y2, y3, q, fq, fk, wout, a1, gain, shift, w1, w2, eb, cot = held
    k, v, o, lse, out, do, dh, keep_a, send_a, keep_b, send_b, deb, small = results
    length, width = q.ref.shape
    shard = rng[SHARD]
    wkv_ref, pb_ref = wkv.get(), pb.get()
    for m, y in enumerate((y0, y1, y2, y3)):
        y_ref = y.get()
        for r in range(0, length, RT):
            x = y_ref[r : r + RT]
            rows = slice(m * length + r, m * length + r + RT)
            k.ref[rows] = dot(x, wkv_ref[:, :width]).astype(BF16)
            v.ref[rows] = (dot(x, wkv_ref[:, width:]) + row_of(pb_ref, 4)).astype(BF16)
    k.send()
    v.send()
    attend(rng, q.get(), fq.get(), k.ref, v.ref, fk.get(), o.ref, lse.ref, qh, s_scr, mx, acc, False)
    o.send()
    lse.send()
    wout_ref, a1_ref, gain_ref, shift_ref = wout.get(), a1.get(), gain.get(), shift.get()
    for r in range(0, length, RT):
        rows = slice(r, r + RT)
        n, spread = norm_rows(a1_ref[rows] + dot(o.ref[rows], wout_ref[...]) + row_of(pb_ref, 5))
        n1[rows] = n
        r1[rows] = jnp.broadcast_to(spread, (RT, 128))
        a2[rows] = n * row_of(gain_ref, 1) + row_of(shift_ref, 1)
        y_scr[rows] = jnp.zeros((RT, width), F32)
    a2t[...] = a2[...].astype(BF16).T
    w1_ref, w2_ref, eb_ref, cot_ref = w1.get(), w2.get(), eb.get(), cot.get()
    chunks = w1_ref.shape[1] // width

    def expand(c, carry):
        cols = pl.ds(pl.multiple_of(c * width, width), width)
        for r in range(0, length, RT):
            rows = slice(r, r + RT)
            u = dot(a2[rows].astype(BF16), w1_ref[:, cols]) + eb_ref[0:1, cols].astype(F32)
            square = u * u
            t = jnp.tanh(GELU_A * (u + GELU_B * u * square))
            half = 0.5 * (1.0 + t)
            act_low = (u * half).astype(BF16)
            act[c, rows] = act_low
            gp[c, rows] = half + 0.5 * u * (1.0 - t * t) * (GELU_A + 3.0 * GELU_A * GELU_B * square)
            y_scr[rows] += dot(act_low, w2_ref[cols, :])
        return carry

    lax.fori_loop(0, chunks, expand, 0)
    zero = jnp.zeros((1, width), F32)
    db5, db6, dg1, ds1, dg2, ds2 = (zero,) * 6
    for r in range(0, length, RT):
        rows = slice(r, r + RT)
        n, spread = norm_rows(a2[rows] + y_scr[rows] + row_of(pb_ref, 6))
        out.ref[rows] = (n * row_of(gain_ref, 2) + row_of(shift_ref, 2)).astype(BF16)
        position = shard * length + r + lax.broadcasted_iota(jnp.int32, (RT, 1), 0)
        g = jnp.where(position < rng[VALID], cot_ref[rows].astype(F32), 0.0)
        dg2 += jnp.sum(g * n, axis=0, keepdims=True)
        ds2 += jnp.sum(g, axis=0, keepdims=True)
        dh3 = norm_rows_back(g, n, spread, row_of(gain_ref, 2))
        dy3 = dh3.astype(BF16)
        db6 += jnp.sum(dy3.astype(F32), axis=0, keepdims=True)
        dy_scr[rows] = dy3
        y_scr[rows] = dh3
    out.send()

    parts = width // 128

    def contract(c, carry):
        cols = pl.ds(pl.multiple_of(c * width, width), width)
        total = jnp.zeros((1, width), F32)
        dus = []
        for r in range(0, length, RT):
            rows = slice(r, r + RT)
            du = (gp[c, rows] * dot(dy_scr[rows], w2_ref[cols, :], NT)).astype(BF16)
            total += jnp.sum(du.astype(F32), axis=0, keepdims=True)
            y_scr[rows] += dot(du, w1_ref[:, cols], NT)
            dus.append(du)
        deb.ref[0:1, cols] = total
        du = jnp.concatenate(dus, axis=0)
        g1 = dot(a2t[...], du)
        for j in range(parts):
            put_block(
                keep_b.ref, send_b.ref, c ^ shard, slice(j * width, (j + 1) * width),
                g1[:, j * 128 : (j + 1) * 128].astype(BF16),
            )
        g2 = dot(act[c], dy_scr[...], TN)
        at = pl.ds(pl.multiple_of(c * width, width), width)
        for b in range(4):
            put_block(
                keep_a.ref, send_a.ref, shard ^ b, at, g2[:, b * 128 : (b + 1) * 128].astype(BF16)
            )
        return carry

    lax.fori_loop(0, chunks, contract, 0)
    keep_a.send()
    send_a.send()
    for r in range(0, length, RT):
        rows = slice(r, r + RT)
        up = y_scr[rows]
        n = n1[rows]
        dg1 += jnp.sum(up * n, axis=0, keepdims=True)
        ds1 += jnp.sum(up, axis=0, keepdims=True)
        dh2 = norm_rows_back(up, n, r1[rows, 0:1], row_of(gain_ref, 1))
        dh.ref[rows] = dh2
        dy2 = dh2.astype(BF16)
        dy_scr[rows] = dy2
        db5 += jnp.sum(dy2.astype(F32), axis=0, keepdims=True)
        do.ref[rows] = dot(dy2, wout_ref[...], NT).astype(BF16)
    dh.send()
    do.send()
    g3 = dot(o.ref[...], dy_scr[...], TN)
    for b in range(4):
        put_block(
            keep_b.ref, send_b.ref, shard ^ b, slice(parts * width, (parts + 1) * width),
            g3[:, b * 128 : (b + 1) * 128].astype(BF16),
        )
    for i, value in enumerate((db5, db6, dg1, dg2, ds1, ds2)):
        small.ref[i : i + 1, :] = value
    small.ref[6:8, :] = jnp.zeros((2, width), F32)


def cross_forward(rng, parts, fq, fk, q, a1, cot, wkv, wout, w1, w2, eb, pb, gain, shift):
    length, width = q.shape
    full, inner = len(parts) * length, w1.shape[1]
    return call(
        cross_body,
        rng,
        [wkv, pb, *parts, q, fq, fk, wout, a1, gain, shift, w1, w2, eb, cot],
        [
            ((full, width), BF16), ((full, width), BF16), ((length, width), BF16),
            ((width // 128, length, 128), F32), ((length, width), BF16), ((length, width), BF16),
            ((length, width), F32), ((2, inner, 128), BF16), ((2, inner, 128), BF16),
            ((2, inner + width, 128), BF16), ((2, inner + width, 128), BF16), ((1, inner), F32),
            ((8, width), F32),
        ],
        attend_scratch(length, full)
        + [
            ((length, width), F32), ((length, 128), F32), ((length, width), F32), ((width, length), BF16),
            ((inner // width, length, width), BF16), ((inner // width, length, width), F32),
            ((length, width), F32), ((length, width), BF16),
        ],
        flops=30 * 10**9,
        vmem=60,
    )


def back_body(rng, held, results, qh, doh, qm, dom, dq_scr, w_scr, c_scr, *, causal):
    q, fq, lse, do, o, fk, k, v, xq, x0, x1, x2, x3 = held
    dq_out, dkv, w, small = results
    length = q.ref.shape[0]
    shard = rng[SHARD]
    dkv.ref[...] = jnp.zeros_like(dkv.ref)
    dq = attend_back(
        rng, q.get()[...], fq.get()[...], lse.get()[0], do.get()[...], o.get()[...], k.get(), v.get(),
        fk.get(), dkv.ref, qh, doh, qm, dom, dq_scr, causal,
    ).astype(BF16)
    dkv.send()
    dq_out.ref[...] = dq
    dq_out.send()
    w.ref[0] = dot(xq.get()[...], dq, TN).astype(BF16)
    w_scr[...] = jnp.zeros_like(w_scr)
    c_scr[...] = jnp.zeros_like(c_scr)
    for m, x in enumerate((x0, x1, x2, x3)):
        x_ref = x.get()

        def more(m=m, x_ref=x_ref):
            part = dkv.ref[m * length : (m + 1) * length, :]
            w_scr[...] += dot(x_ref[...], part, TN)
            c_scr[...] += jnp.sum(part[:, 128:].astype(F32), axis=0, keepdims=True)

        if causal and m:
            pl.when((shard ^ m) < shard)(more)
        else:
            more()
    w.ref[1] = w_scr[:, :128].astype(BF16)
    w.ref[2] = w_scr[:, 128:].astype(BF16)
    small.ref[0:1, :] = jnp.sum(dq.astype(F32), axis=0, keepdims=True)
    small.ref[1:2, :] = c_scr[0:1]
    small.ref[2:8, :] = jnp.zeros((6, 128), F32)


def attend_backward(rng, p, q, fq, lse, do, o, fk, k, v, xq, parts, causal, deps):
    length, width = q.shape
    full = k.shape[0]
    cut = pl.ds(p * 128, 128)
    return call(
        functools.partial(back_body, causal=causal),
        rng,
        [(q, cut), fq, lse[p : p + 1], (do, cut), (o, cut), fk, (k, cut), (v, cut), xq, *parts],
        [((length, 128), BF16), ((full, 256), BF16), ((3, width, 128), BF16), ((8, 128), F32)],
        [((2, length, 128), BF16)] * 4 + [((128, length), F32), ((width, 256), F32), ((8, 128), F32)],
        deps=deps,
        flops=9 * 10**9,
    )


def middle_body(rng, held, results, dy_scr):
    dq0, dq1, dq2, dq3, wq, dh2, n0, r0, gain, wout, o, u0, u1, u2, u3 = held
    dh, do, keep, send, small = results
    length, width = dh2.ref.shape
    pairs = width // 128
    shard = rng[SHARD]
    zero = jnp.zeros((1, width), F32)
    db2, dg0, ds0 = zero, zero, zero
    dq_refs = [x.get() for x in (dq0, dq1, dq2, dq3)]
    wq_ref, dh2_ref, n_ref, r_ref, gain_ref, wout_ref = (x.get() for x in (wq, dh2, n0, r0, gain, wout))
    for r in range(0, length, RT):
        rows = slice(r, r + RT)
        up = dh2_ref[rows] + dot(jnp.concatenate([d[rows] for d in dq_refs], axis=1), wq_ref[...], NT)
        n = n_ref[rows]
        dg0 += jnp.sum(up * n, axis=0, keepdims=True)
        ds0 += jnp.sum(up, axis=0, keepdims=True)
        new = norm_rows_back(up, n, r_ref[rows, 0:1], row_of(gain_ref, 0))
        dh.ref[rows] = new
        dy = new.astype(BF16)
        dy_scr[rows] = dy
        db2 += jnp.sum(dy.astype(F32), axis=0, keepdims=True)
        do.ref[rows] = dot(dy, wout_ref[...], NT).astype(BF16)
    dh.send()
    do.send()
    g = dot(o.get()[...], dy_scr[...], TN)
    for b in range(4):
        put_block(keep.ref, send.ref, shard ^ b, slice(0, width), g[:, b * 128 : (b + 1) * 128].astype(BF16))
    units = [x.get() for x in (u0, u1, u2, u3)]
    for b in range(4):
        put_block(keep.ref, send.ref, shard ^ b, slice(width, 2 * width), units[b][0])
    for i in range(2 * pairs):
        b, at = i // 2, 2 + i % 2
        put_block(
            keep.ref, send.ref, shard ^ b, slice(at * width, (at + 1) * width), units[i % pairs][1 + i // pairs]
        )
    for i, value in enumerate((db2, dg0, ds0)):
        small.ref[i : i + 1, :] = value
    small.ref[3:8, :] = jnp.zeros((5, width), F32)


def middle(rng, dqs, units, dh2, n, r, o, wq, wout, gain):
    length, width = dh2.shape
    return call(
        middle_body,
        rng,
        [*dqs, wq, dh2, n, r, gain, wout, o, *units],
        [
            ((length, width), F32), ((length, width), BF16), ((2, 4 * width, 128), BF16),
            ((2, 4 * width, 128), BF16), ((8, width), F32),
        ],
        [((length, width), BF16)],
        flops=3 * 10**9,
    )


def spread_body(rng, held, results, *, causal, offset):
    keep, send = results
    length, width = keep.ref.shape[1:]
    shard = rng[SHARD]
    refs = [x.get() for x in held]
    w_ref, parts = refs[0], refs[1:]
    for m in (1, 3, 0, 2):
        ref = (keep.ref, send.ref)[m % 2]

        def fill(m=m, ref=ref):
            for r in range(0, length, RT):
                rows = slice(m * length + r, m * length + r + RT)
                dk = jnp.concatenate([d[rows, :128] for d in parts], axis=1)
                dv = jnp.concatenate([d[rows, 128:] for d in parts], axis=1)
                total = dot(dk, w_ref[:, offset : offset + width], NT)
                total += dot(dv, w_ref[:, offset + width : offset + 2 * width], NT)
                ref[m // 2, r : r + RT] = total.astype(BF16)

        def clear(m=m, ref=ref):
            ref[m // 2] = jnp.zeros((length, width), BF16)

        if causal and m:
            pl.when((shard ^ m) < shard)(fill)
            pl.when((shard ^ m) > shard)(clear)
        else:
            fill()
        if m == 3:
            send.send()


def spread_keys(rng, dkvs, w, length, causal, offset, deps):
    width = w.shape[0]
    return call(
        functools.partial(spread_body, causal=causal, offset=offset),
        rng,
        [w, *dkvs],
        [((2, length, width), BF16), ((2, length, width), BF16)],
        [],
        deps=deps,
        flops=2 * 10**9,
    )


def pack_body(rng, held, results):
    keep, send = results
    refs = [x.get() for x in held]
    units, own, other = refs[0:4], refs[4:8], refs[8:12]
    s0_ref, s2_ref, deb_ref = refs[12:]
    width = units[0].shape[1]
    pairs = width // 128
    shard = rng[SHARD]
    for i in range(3 * pairs):
        b, at = i // 3, i % 3
        put_block(
            keep.ref, send.ref, shard ^ b, slice(at * width, (at + 1) * width), units[i % pairs][i // pairs]
        )
    base = 3 * width
    pad = keep.ref.shape[1] - base
    for b in range(4):
        cols = slice(b * 128, (b + 1) * 128)
        rows = [deb_ref[0:1, b * width + j * 128 : b * width + (j + 1) * 128] for j in range(pairs)]
        rows += [own[b][0:1], own[b][1:2], s0_ref[0:1, cols], other[b][0:1], other[b][1:2]]
        rows += [s2_ref[0:1, cols], s2_ref[1:2, cols]]
        rows += [s0_ref[1:2, cols], s2_ref[2:3, cols], s2_ref[3:4, cols]]
        rows += [s0_ref[2:3, cols], s2_ref[4:5, cols], s2_ref[5:6, cols]]
        rows.append(jnp.zeros((pad - len(rows), 128), F32))
        put_block(
            keep.ref, send.ref, shard ^ b, slice(base, base + pad), jnp.concatenate(rows, axis=0).astype(BF16)
        )


def pack_tail(rng, units, self_small, cross_small, s0, s2, deb, unit):
    rows = 3 * units[0].shape[1] + unit
    return call(
        pack_body,
        rng,
        [*units, *self_small, *cross_small, s0, s2, deb],
        [((2, rows, 128), BF16), ((2, rows, 128), BF16)],
        [],
    )


def partner(x, axis, mask):
    n = lax.axis_size(axis)
    return lax.ppermute(x, axis, [(i, i ^ mask) for i in range(n)])


def gather_relative(x):
    across = partner(x, "seq", 2)
    return [x, partner(x, "seq", 1), across, partner(across, "seq", 1)]


def add(a, b):
    return (a.astype(F32) + b.astype(F32)).astype(BF16)


def after(x, *deps):
    return lax.optimization_barrier((x, *deps))[0]


def half_of(x, bit):
    half = x.shape[0] // 2
    return lax.dynamic_slice_in_dim(x, bit * half, half, 0)


def dp_bit(j):
    return (lax.axis_index("dp") >> j) & 1


def fold_send(x, j):
    return partner(half_of(x, 1 - dp_bit(j)), "dp", 1 << j)


def fold(x, j):
    return add(half_of(x, dp_bit(j)), fold_send(x, j))


def unfold_join(x, other, j):
    return jnp.where(dp_bit(j) == 0, jnp.concatenate([x, other]), jnp.concatenate([other, x]))


def unfold(x, j):
    return unfold_join(x, partner(x, "dp", 1 << j), j)


def dp_groups(split):
    n = lax.axis_size("dp")
    if split == 0:
        return [[i, i + 1] for i in range(0, n, 2)]
    rest = [0]
    while len(rest) < n // 2:
        rest = [i * 2 for i in rest] + [i * 2 + 1 for i in rest]
        rest = sorted(rest, key=lambda i: bin(i + 2 * n)[:2:-1])
    return [[2 * i + b for i in rest] for b in range(2)]


def group_fold(x, split):
    return lax.psum_scatter(x, "dp", axis_index_groups=dp_groups(split), scatter_dimension=0, tiled=True)


def group_unfold(x, split):
    return lax.all_gather(x, "dp", axis_index_groups=dp_groups(split), axis=0, tiled=True)


def query_features(segments):
    f = lax.broadcasted_iota(jnp.int32, (1, 128), 1) % 64
    return (segments[:, None] == f).astype(BF16)


def key_features(segments, positions, length):
    f = lax.broadcasted_iota(jnp.int32, (1, 128), 1) % 64
    seen = (segments[:, None] == f) & (positions[:, None] < length)
    return jnp.where(
        f < 8, jnp.where(seen, 0.0, -1e30), jnp.where(f < 11, 1.0, 0.0)
    ).astype(BF16)


def ranges(own, segments, count, shard, valid):
    values = []
    for half in range(2):
        first, last = own[half * RT], own[half * RT + RT - 1]
        lo = jnp.sum((segments < first).astype(jnp.int32)) // BK
        end = jnp.minimum(jnp.sum((segments <= last).astype(jnp.int32)), count)
        values += [lo, (end + BK - 1) // BK]
    return jnp.stack(values + [shard, valid])


def local(
    target, memory, cotangent, target_segments, source_segments, target_lengths, source_lengths,
    self_inproj, self_outproj, cross_query, cross_keyval, cross_outproj, ffn_expand, ffn_reduce,
    expand_bias, proj_bias, norm_gain, norm_shift,
):
    target, memory, cotangent = target[0], memory[0], cotangent[0]
    target_segments, source_segments = target_segments[0], source_segments[0]
    target_length, source_length = target_lengths[0], source_lengths[0]
    length, width = target.shape
    pairs = width // 128
    shards = lax.axis_size("seq")
    bits = lax.axis_size("dp").bit_length() - 1
    shard = lax.axis_index("seq").astype(jnp.int32)

    target_parts = gather_relative(target)
    memory_parts = gather_relative(memory)

    order = shard ^ jnp.arange(shards, dtype=jnp.int32)
    positions = (order[:, None] * length + jnp.arange(length, dtype=jnp.int32)[None]).reshape(-1)
    target_rel = jnp.take(target_segments.reshape(shards, length), order, axis=0).reshape(-1)
    source_rel = jnp.take(source_segments.reshape(shards, length), order, axis=0).reshape(-1)
    own = target_rel[:length]
    fq = query_features(own)
    self_fk = key_features(target_rel, positions, target_length)
    cross_fk = key_features(source_rel, positions, source_length)
    self_rng = ranges(own, target_segments, target_length, shard, target_length)
    cross_rng = ranges(own, source_segments, source_length, shard, target_length)

    q1, k1, v1, o1, lse1, a1, n0, r0, q2 = self_forward(
        self_rng, target_parts, fq, self_fk, self_inproj, self_outproj, cross_query, proj_bias,
        norm_gain, norm_shift,
    )
    a1_low = a1.astype(BF16)
    k2, v2, o2, lse2, layer_out, do2, dh2, keep1, send1, keep2, send2, deb, small2 = cross_forward(
        cross_rng, memory_parts, fq, cross_fk, q2, a1, cotangent, cross_keyval, cross_outproj,
        ffn_expand, ffn_reduce, expand_bias, proj_bias, norm_gain, norm_shift,
    )

    def cross_back(p, deps):
        return attend_backward(
            cross_rng, p, q2, fq, lse2, do2, o2, cross_fk, k2, v2, a1_low, memory_parts, False, deps
        )

    def self_back(p, deps):
        return attend_backward(
            self_rng, p, q1, fq, lse1, do1, o1, self_fk, k1, v1, target, target_parts, True, deps
        )

    got1 = partner(send1, "seq", 1)
    got2 = partner(send2, "seq", 1)
    c0 = cross_back(0, [])
    got1, got2 = after(got1, c0[0]), after(got2, c0[0])
    far1 = add(keep1[1], got1[1])
    near1 = add(keep1[0], got1[0])
    two2 = add(keep2, got2).reshape(2, 2, -1, 128).transpose(1, 0, 2, 3).reshape(-1, 128)
    get1 = partner(far1, "seq", 2)
    y2 = group_fold(two2, 0)
    c1 = cross_back(1, [far1, two2, c0[0]])
    c2 = cross_back(2, [c1[0]])
    get1, y2 = after(get1, c2[0]), after(y2, c2[0])
    x1 = add(near1, get1)
    y1 = group_fold(x1, 0)
    y2 = y2.reshape(2, -1, 128)
    get2 = partner(y2[1], "seq", 2)
    c3 = cross_back(3, [x1, y2, c2[0]])
    get2 = after(get2, c3[0])
    x2 = add(y2[0], get2)
    z2 = group_fold(x2, 1)
    cross = (c0, c1, c2, c3)
    dh1, do1, keep3, send3, small0 = middle(
        self_rng, [c[0] for c in cross], [c[2] for c in cross], dh2, n0, r0, o1, cross_query,
        self_outproj, norm_gain,
    )
    y1 = after(y1, do1)
    z1 = group_fold(y1, 1)
    got3 = partner(send3, "seq", 1)
    mem_keep, mem_send = spread_keys(cross_rng, [c[1] for c in cross], cross_keyval, length, False, 0, [do1, x2])
    got3 = after(got3, mem_keep)
    two3 = add(keep3, got3)
    get3 = partner(two3[1], "seq", 2)
    mem_got = partner(mem_send, "seq", 1)
    s0 = self_back(0, [two3, mem_keep])
    mem_got, get3 = after(mem_got, s0[0]), after(get3, s0[0])
    mem_two = add(mem_keep, mem_got)
    x3 = add(two3[0], get3)
    mem_get = partner(mem_two[1], "seq", 2)
    send_y3 = fold_send(x3, 0)
    s1 = self_back(1, [x3, mem_two, s0[0]])
    send_y3, z1, z2 = after(send_y3, s1[0]), after(z1, s1[0]), after(z2, s1[0])
    y3 = add(half_of(x3, dp_bit(0)), send_y3)
    z3 = lax.psum(y3, "dp", axis_index_groups=dp_groups(1))
    w = jnp.concatenate([z1, z2])
    other = partner(w, "dp", 1 << (bits - 1))
    s2 = self_back(2, [y3, w, s1[0]])
    other, mem_get = after(other, s2[0]), after(mem_get, s2[0])
    w = unfold_join(w, other, bits - 1)
    memory_grad = mem_two[0].astype(F32) + mem_get.astype(F32)
    other = partner(w, "dp", 1 << (bits - 2))
    s3 = self_back(3, [w, memory_grad, s2[0]])
    selfs = (s0, s1, s2, s3)
    keep4, send4 = pack_tail(
        self_rng, [s[2] for s in selfs], [s[3] for s in selfs], [c[3] for c in cross], small0, small2, deb,
        16 * lax.axis_size("dp"),
    )
    got4 = partner(send4, "seq", 1)
    tgt_keep, tgt_send = spread_keys(
        self_rng, [s[1] for s in selfs], self_inproj, length, True, width, [keep4]
    )
    got4, other, z3 = after(got4, tgt_keep), after(other, tgt_keep), after(z3, tgt_keep)
    w = unfold_join(w, other, bits - 2)
    for j in reversed(range(1, bits - 2)):
        w = unfold(w, j)
    w = group_unfold(w, 0)
    two4 = add(keep4, got4)
    sum4 = add(two4[0], partner(two4[1], "seq", 2))
    tgt_got = partner(tgt_send, "seq", 1)
    tgt_two = add(tgt_keep, tgt_got)
    tgt_get = partner(tgt_two[1], "seq", 2)
    dq1 = jnp.concatenate([s[0] for s in selfs], axis=1)
    target_grad = dh1 + dot(dq1, self_inproj[:, :width], NT) + (tgt_two[0].astype(F32) + tgt_get.astype(F32))
    for j in range(bits):
        sum4 = fold(sum4, j)
    for j in reversed(range(bits)):
        sum4 = unfold(sum4, j)
    sum3 = unfold(z3, 0)
    shards_of = 2 ** (bits - 1)
    w = w.reshape(2 * shards_of, -1, 128)
    cut = z1.shape[0]
    sum1 = w[:, :cut].reshape(-1, 128)
    sum2 = w[:, cut:].reshape(-1, 128)

    def take(x, at, rows, cols):
        n = cols // 128
        x = x[at : at + n * rows].reshape(n, rows, 128).transpose(1, 0, 2)
        return x.reshape(rows, cols).astype(F32)

    base = 3 * width
    tail = sum4[base:].astype(F32)
    return (
        layer_out[None],
        target_grad[None],
        memory_grad[None],
        take(sum4, 0, width, 3 * 128),
        take(sum3, 0, width, 128),
        take(sum3, width, width, 128),
        take(sum3, 2 * width, width, 256),
        take(sum2, pairs * width, width, 128),
        take(sum2, 0, width, 512),
        take(sum1, 0, sum1.shape[0], 128),
        tail[0:4].reshape(1, 512),
        tail[4:11],
        tail[11:14],
        tail[14:17],
    )


def solution(mesh):
    rows, shard = P("dp", "seq", None), P(None, "seq")
    in_specs = (rows, rows, rows, P("dp", None), P("dp", None), P("dp"), P("dp")) + (P(),) * 11
    out_specs = (rows, rows, rows) + (shard,) * 11
    return jax.shard_map(local, mesh=mesh, in_specs=in_specs, out_specs=out_specs, check_vma=False)
```

```python
import functools
import jax
import jax.numpy as jnp
from jax import lax
from jax.experimental import pallas as pl
from jax.experimental.pallas import tpu as pltpu
from jax.sharding import PartitionSpec as P

BF16 = jnp.bfloat16
F32 = jnp.float32
EPSILON = 1e-05
BK = 256
RT = 256
NT = (((1,), (1,)), ((), ()))
NN = (((1,), (0,)), ((), ()))
TN = (((0,), (0,)), ((), ()))


def dot(a, b, dims=NN):
    return lax.dot_general(a, b, dims, preferred_element_type=F32)


class Held:
    def __init__(self, copy, ref):
        self.copy, self.ref, self.waited = copy, ref, False

    def get(self):
        if not self.waited:
            self.copy.wait()
            self.waited = True
        return self.ref


class Result:
    def __init__(self, copy, ref):
        self.copy, self.ref, self.started = copy, ref, False

    def send(self):
        self.copy.start()
        self.started = True


def call(body, rng, ins, outs, scratch, flops=10**9, vmem=24):
    arrays, columns = [], []
    for x in ins:
        x, cut = x if isinstance(x, tuple) else (x, None)
        arrays.append(x)
        columns.append(cut)
    shapes = []
    for x, cut in zip(arrays, columns):
        shapes.append(x.shape if cut is None else x.shape[:-1] + (cut.size,))
    n_in, n_out, n_scr = len(ins), len(outs), len(scratch)

    def kernel(rng_ref, *refs):
        hbm_in, refs = refs[:n_in], refs[n_in:]
        hbm_out, refs = refs[:n_out], refs[n_out:]
        vm_in, refs = refs[:n_in], refs[n_in:]
        vm_out, refs = refs[:n_out], refs[n_out:]
        scr, refs = refs[:n_scr], refs[n_scr:]
        sem_in, sem_out = refs
        held = []
        for i, (src, dst, cut) in enumerate(zip(hbm_in, vm_in, columns)):
            if cut is not None:
                src = src.at[(slice(None),) * (len(src.shape) - 1) + (cut,)]
            copy = pltpu.make_async_copy(src, dst, sem_in.at[i])
            copy.start()
            held.append(Held(copy, dst))
        results = [
            Result(pltpu.make_async_copy(src, dst, sem_out.at[i]), src)
            for i, (src, dst) in enumerate(zip(vm_out, hbm_out))
        ]
        body(rng_ref, held, results, *scr)
        for x in held:
            x.get()
        for x in results:
            if not x.started:
                x.send()
        for x in results:
            x.copy.wait()

    hbm = pl.BlockSpec(memory_space=pltpu.HBM)
    return pl.pallas_call(
        kernel,
        out_shape=tuple(pltpu.HBM(s, d) for s, d in outs),
        in_specs=[pl.BlockSpec(memory_space=pltpu.SMEM)] + [hbm] * n_in,
        out_specs=(hbm,) * n_out,
        scratch_shapes=[pltpu.VMEM(s, x.dtype) for s, x in zip(shapes, arrays)]
        + [pltpu.VMEM(s, d) for s, d in outs]
        + [pltpu.VMEM(s, d) for s, d in scratch]
        + [pltpu.SemaphoreType.DMA((n_in,)), pltpu.SemaphoreType.DMA((n_out,))],
        compiler_params=pltpu.CompilerParams(vmem_limit_bytes=vmem * 2**20),
        cost_estimate=pl.CostEstimate(flops=flops, bytes_accessed=2**20, transcendentals=0),
    )(rng, *[pltpu.with_memory_space_constraint(x, pltpu.HBM) for x in arrays])


LO0, HI0, LO1, HI1, SHARD, VALID = range(6)


def prepare_body(
    info, lengths, t_smem, t_ref, s_ref, self_rng, cross_rng, fq_ref, self_fk, cross_fk
):
    length = fq_ref.shape[0]
    shard = info[0]
    valid, count = lengths[0], lengths[1]
    full = t_ref.shape[1]
    t_row, s_row = t_ref[...], s_ref[...]

    def number(mask):
        return jnp.sum(jnp.where(mask, 1.0, 0.0)).astype(jnp.int32)

    for half in range(2):
        first = t_smem[0, shard * length + half * RT]
        last = t_smem[0, shard * length + half * RT + RT - 1]
        self_rng[LO0 + 2 * half] = lax.div(number(t_row < first), BK)
        self_rng[HI0 + 2 * half] = 0
        cross_rng[LO0 + 2 * half] = lax.div(number(s_row < first), BK)
        end = jnp.minimum(number(s_row <= last), count)
        cross_rng[HI0 + 2 * half] = lax.div(end + BK - 1, BK)
    for ref in (self_rng, cross_rng):
        ref[SHARD] = shard
        ref[VALID] = valid
        ref[6] = 0
        ref[7] = 0
    f = lax.broadcasted_iota(jnp.int32, (128, 128), 1) % 64

    def column(ref, at):
        return jnp.broadcast_to(ref[0:1, pl.ds(pl.multiple_of(at, 128), 128)], (128, 128)).T

    row = lax.broadcasted_iota(jnp.int32, (128, 128), 0)
    for m in range(full // length):
        for t in range(0, length, 128):
            at = (shard ^ m) * length + t
            for ref, total, out in ((t_ref, valid, self_fk), (s_ref, count, cross_fk)):
                seg = column(ref, at)
                seen = (seg == f) & (row + at < total)
                feature = jnp.where(
                    f < 8, jnp.where(seen, 0.0, -1e30), jnp.where(f < 11, 1.0, 0.0)
                )
                out[m * length + t : m * length + t + 128] = feature.astype(BF16)
                if m == 0 and out is self_fk:
                    fq_ref[t : t + 128] = jnp.where(seg == f, 1.0, 0.0).astype(BF16)


def prepare(shard, target_length, source_length, target_segments, source_segments, length):
    full = target_segments.shape[1]
    sd = jax.ShapeDtypeStruct
    smem, vm = pl.BlockSpec(memory_space=pltpu.SMEM), pl.BlockSpec(memory_space=pltpu.VMEM)
    return pl.pallas_call(
        prepare_body,
        out_shape=(
            sd((8,), jnp.int32), sd((8,), jnp.int32), sd((length, 128), BF16), sd((full, 128), BF16),
            sd((full, 128), BF16),
        ),
        in_specs=[smem, smem, smem, vm, vm],
        out_specs=(smem, smem, vm, vm, vm),
    )(
        shard.reshape(1), jnp.concatenate([target_length, source_length]), target_segments,
        target_segments, source_segments,
    )


def half_masks():
    lane = lax.broadcasted_iota(jnp.int32, (1, 128), 1)
    return (lane < 64, lane >= 64), lane % 64


def relative_offset(block, shard, per_shard):
    owner = lax.div(block, per_shard)
    return pl.multiple_of(((owner ^ shard) * per_shard + lax.rem(block, per_shard)) * BK, BK)


def triangle(transposed):
    a = lax.broadcasted_iota(jnp.int32, (BK, BK), 0)
    b = lax.broadcasted_iota(jnp.int32, (BK, BK), 1)
    return a <= b if transposed else b <= a


def attend(rng, q_ref, fq_ref, k_ref, v_ref, fk_ref, o_ref, lse_ref, qh, s_scr, mx, acc, causal):
    length, width = q_ref.shape
    per = length // BK
    shard = rng[SHARD]
    conds, _ = half_masks()
    heads = [(j, h) for j in range(2) for h in range(2)]
    for g in range(width // 256):
        for half in range(length // RT):
            rows = slice(half * RT, (half + 1) * RT)
            fq = fq_ref[rows]
            for i, (j, h) in enumerate(heads):
                c = g * 256 + j * 128
                qh[i] = jnp.where(conds[h], q_ref[rows, c : c + 128], fq)
                mx[i] = jnp.full((RT, 128), -3e38, F32)
                acc[i] = jnp.zeros((RT, 128), F32)

            def scores(off, slot, diagonal, g=g):
                fk = fk_ref[pl.ds(off, BK), :]
                for i, (j, h) in enumerate(heads):
                    c = g * 256 + j * 128
                    kh = jnp.where(conds[h], k_ref[pl.ds(off, BK), c : c + 128], fk)
                    s = dot(qh[i], kh, NT)
                    if diagonal:
                        s = jnp.where(triangle(False), s, -1e30)
                    s_scr[i, slot] = s
                    m = mx[i]
                    for t in range(0, BK, 128):
                        m = jnp.maximum(m, s[:, t : t + 128])
                    mx[i] = m

            def values(off, slot, g=g):
                for i, (j, h) in enumerate(heads):
                    c = g * 256 + j * 128
                    vp = v_ref[pl.ds(off, BK), c : c + 128]
                    vh = jnp.where(conds[h], vp, jnp.ones_like(vp))
                    m = mx[i]
                    p = jnp.concatenate(
                        [
                            jnp.exp(s_scr[i, slot, :, t : t + 128] - m).astype(BF16)
                            for t in range(0, BK, 128)
                        ],
                        axis=1,
                    )
                    acc[i] += dot(p, vh)

            lo = rng[LO0 + 2 * half]
            hi = shard * per + half if causal else rng[HI0 + 2 * half]

            def first(kb, carry):
                scores(relative_offset(kb, shard, per), kb, False)
                return carry

            def second(kb, carry):
                values(relative_offset(kb, shard, per), kb)
                return carry

            lax.fori_loop(lo, hi, first, 0)
            if causal:
                scores(half * BK, hi, True)
            for i in range(4):
                mx[i] = jnp.broadcast_to(jnp.max(mx[i], axis=-1, keepdims=True), (RT, 128))
            lax.fori_loop(lo, hi, second, 0)
            if causal:
                values(half * BK, hi)
            for j in range(2):
                c = g * 256 + j * 128
                a, b = 2 * j, 2 * j + 1
                num = jnp.where(conds[0], acc[a], acc[b])
                den = jnp.where(conds[0], acc[b], acc[a])
                o_ref[rows, c : c + 128] = (num / pltpu.roll(den, 64, 1)).astype(BF16)
                lse_ref[2 * g + j, rows] = jnp.where(conds[0], mx[b], mx[a]) + jnp.log(den)


def attend_scratch(length, full):
    return [
        ((4, RT, 128), BF16),
        ((4, full // BK, RT, BK), F32),
        ((4, RT, 128), F32),
        ((4, RT, 128), F32),
    ]


def attend_back(rng, q, fq, logsum, do, o, k_ref, v_ref, fk_ref, dkv_ref, qh, doh, qm, dom, dq_scr, causal):
    length = q.shape[0]
    per = length // BK
    shard = rng[SHARD]
    conds, l64 = half_masks()
    prod = do.astype(F32) * o.astype(F32)
    delta = jnp.where(
        conds[0],
        jnp.sum(jnp.where(conds[1], prod, 0.0), axis=-1, keepdims=True),
        jnp.sum(jnp.where(conds[0], prod, 0.0), axis=-1, keepdims=True),
    )

    def negated_parts(x):
        high = x.astype(BF16).astype(F32)
        rest = x - high
        mid = rest.astype(BF16).astype(F32)
        low = rest - mid
        return -jnp.where(
            l64 == 8, high, jnp.where(l64 == 9, mid, jnp.where(l64 == 10, low, 0.0))
        )

    fl = (negated_parts(logsum) + fq.astype(F32)).astype(BF16)
    fd = negated_parts(delta).astype(BF16)
    zero = jnp.zeros_like(q)
    for h in range(2):
        qh[h] = jnp.where(conds[h], q, fl)
        doh[h] = jnp.where(conds[h], do, fd)
        qm[h] = jnp.where(conds[h], q, zero)
        dom[h] = jnp.where(conds[h], do, zero)
    dq_scr[...] = jnp.zeros_like(dq_scr)
    ones = jnp.where((l64 >= 8) & (l64 <= 10), 1.0, 0.0).astype(BF16)

    def block(off, halves, diagonal=None):
        kp = k_ref[pl.ds(off, BK), :]
        vp = v_ref[pl.ds(off, BK), :]
        fk = fk_ref[pl.ds(off, BK), :]
        ones_block = jnp.broadcast_to(ones, vp.shape)
        dk = jnp.zeros((BK, 128), F32)
        dv = jnp.zeros((BK, 128), F32)
        for h in range(2):
            kh = jnp.where(conds[h], kp, fk)
            vh = jnp.where(conds[h], vp, ones_block)
            kt = jnp.where(conds[h], kp, jnp.zeros_like(kp)).T
            for half in halves:
                r = half * RT
                s = dot(kh, qh[h, r : r + RT], NT)
                if diagonal == half:
                    s = jnp.where(triangle(True), s, -1e30)
                p = jnp.exp(s)
                dp = dot(vh, doh[h, r : r + RT], NT)
                ds = (p * dp).astype(BF16)
                dv += dot(p.astype(BF16), dom[h, r : r + RT])
                dk += dot(ds, qm[h, r : r + RT])
                dq_scr[:, r : r + RT] += dot(kt, ds)
        dkv_ref[pl.ds(off, BK), 0:128] = dk.astype(BF16)
        dkv_ref[pl.ds(off, BK), 128:256] = dv.astype(BF16)

    def sweep(lo, hi, halves):
        def step(kb, carry):
            block(relative_offset(kb, shard, per), halves)
            return carry

        lax.fori_loop(lo, hi, step, 0)

    lo0, lo1 = rng[LO0], rng[LO1]
    if causal:
        own = shard * per
        sweep(lo0, jnp.minimum(lo1, own), (0,))
        sweep(lo1, own, (0, 1))
        block(0, (0, 1), 0)
        block(BK, (1,), 1)
    else:
        hi0, hi1 = rng[HI0], rng[HI1]
        sweep(lo0, jnp.minimum(lo1, hi0), (0,))
        sweep(lo1, hi0, (0, 1))
        sweep(jnp.maximum(hi0, lo1), hi1, (1,))
    return dq_scr[...].T * 0.125


def norm_rows(hidden):
    center = hidden - jnp.mean(hidden, axis=-1, keepdims=True)
    spread = lax.rsqrt(jnp.mean(center * center, axis=-1, keepdims=True) + EPSILON)
    return center * spread, spread


def norm_rows_back(upstream, normed, spread, gain):
    scaled = upstream * gain
    return spread * (
        scaled
        - jnp.mean(scaled, axis=-1, keepdims=True)
        - normed * jnp.mean(scaled * normed, axis=-1, keepdims=True)
    )


def put_block(keep_ref, send_ref, m, rows, value):
    def keep():
        keep_ref[m // 2, rows] = value

    def send():
        send_ref[m // 2, rows] = value

    pl.when(m % 2 == 0)(keep)
    pl.when(m % 2 == 1)(send)


def row_of(ref, i):
    return ref[i : i + 1, :].astype(F32)


def self_body(rng, held, results, qh, s_scr, mx, acc):
    x0, win, pb, x1, x2, x3, fq, fk, wout, wq, gain, shift = held
    q, k, v, o, lse, a, n_out, r_out, q2_out = results
    length, width = x0.ref.shape
    shard = rng[SHARD]
    eighth = jnp.asarray(0.125, BF16)
    x_ref, win_ref, pb_ref = x0.get(), win.get(), pb.get()
    for r in range(0, length, RT):
        rows = slice(r, r + RT)
        q.ref[rows] = (dot(x_ref[rows], win_ref[:, :width]) + row_of(pb_ref, 0)).astype(BF16) * eighth
    q.send()
    for m, x in enumerate((x0, x1, x2, x3)):
        x_m = x.get()

        def fill(m=m, x_m=x_m):
            for r in range(0, length, RT):
                x = x_m[r : r + RT]
                rows = slice(m * length + r, m * length + r + RT)
                k.ref[rows] = dot(x, win_ref[:, width : 2 * width]).astype(BF16)
                v.ref[rows] = (dot(x, win_ref[:, 2 * width :]) + row_of(pb_ref, 1)).astype(BF16)

        if m == 0:
            fill()
        else:
            pl.when((shard ^ m) < shard)(fill)
    k.send()
    v.send()
    attend(rng, q.ref, fq.get(), k.ref, v.ref, fk.get(), o.ref, lse.ref, qh, s_scr, mx, acc, True)
    o.send()
    lse.send()
    wout_ref, wq_ref, gain_ref, shift_ref = wout.get(), wq.get(), gain.get(), shift.get()
    for r in range(0, length, RT):
        rows = slice(r, r + RT)
        h = x_ref[rows].astype(F32) + dot(o.ref[rows], wout_ref[...]) + row_of(pb_ref, 2)
        n, spread = norm_rows(h)
        a_new = n * row_of(gain_ref, 0) + row_of(shift_ref, 0)
        n_out.ref[rows] = n
        r_out.ref[rows] = jnp.broadcast_to(spread, (RT, 128))
        a.ref[rows] = a_new
        q2 = dot(a_new.astype(BF16), wq_ref[...]) + row_of(pb_ref, 3)
        q2_out.ref[rows] = q2.astype(BF16) * eighth


def self_forward(rng, parts, fq, fk, win, wout, wq, pb, gain, shift):
    length, width = parts[0].shape
    full = len(parts) * length
    return call(
        self_body,
        rng,
        [parts[0], win, pb, *parts[1:], fq, fk, wout, wq, gain, shift],
        [
            ((length, width), BF16), ((full, width), BF16), ((full, width), BF16),
            ((length, width), BF16), ((width // 128, length, 128), F32), ((length, width), F32),
            ((length, width), F32), ((length, 128), F32), ((length, width), BF16),
        ],
        attend_scratch(length, full),
        flops=14 * 10**9,
        vmem=40,
    )


GELU_A = 0.7978845608028654
GELU_B = 0.044715


def cross_body(rng, held, results, qh, s_scr, mx, acc, n1, r1, a2, a2t, act, gp, y_scr, dy_scr):
    wkv, pb, y0, y1, y2, y3, q, fq, fk, wout, a1, gain, shift, w1, w2, eb, cot = held
    k, v, o, lse, out, do, dh, keep, send, deb, small = results
    length, width = q.ref.shape
    shard = rng[SHARD]
    wkv_ref, pb_ref = wkv.get(), pb.get()
    for m, y in enumerate((y0, y1, y2, y3)):
        y_ref = y.get()
        for r in range(0, length, RT):
            x = y_ref[r : r + RT]
            rows = slice(m * length + r, m * length + r + RT)
            k.ref[rows] = dot(x, wkv_ref[:, :width]).astype(BF16)
            v.ref[rows] = (dot(x, wkv_ref[:, width:]) + row_of(pb_ref, 4)).astype(BF16)
    k.send()
    v.send()
    attend(rng, q.get(), fq.get(), k.ref, v.ref, fk.get(), o.ref, lse.ref, qh, s_scr, mx, acc, False)
    o.send()
    lse.send()
    wout_ref, a1_ref, gain_ref, shift_ref = wout.get(), a1.get(), gain.get(), shift.get()
    for r in range(0, length, RT):
        rows = slice(r, r + RT)
        n, spread = norm_rows(a1_ref[rows] + dot(o.ref[rows], wout_ref[...]) + row_of(pb_ref, 5))
        n1[rows] = n
        r1[rows] = jnp.broadcast_to(spread, (RT, 128))
        a2[rows] = n * row_of(gain_ref, 1) + row_of(shift_ref, 1)
        y_scr[rows] = jnp.zeros((RT, width), F32)
    a2t[...] = a2[...].astype(BF16).T
    w1_ref, w2_ref, eb_ref, cot_ref = w1.get(), w2.get(), eb.get(), cot.get()
    inner = w1_ref.shape[1]
    chunks = inner // width

    def expand(c, carry):
        cols = pl.ds(pl.multiple_of(c * width, width), width)
        for r in range(0, length, RT):
            rows = slice(r, r + RT)
            u = dot(a2[rows].astype(BF16), w1_ref[:, cols]) + eb_ref[0:1, cols].astype(F32)
            square = u * u
            t = jnp.tanh(GELU_A * (u + GELU_B * u * square))
            half = 0.5 * (1.0 + t)
            act_low = (u * half).astype(BF16)
            act[c, rows] = act_low
            gp[c, rows] = half + 0.5 * u * (1.0 - t * t) * (GELU_A + 3.0 * GELU_A * GELU_B * square)
            y_scr[rows] += dot(act_low, w2_ref[cols, :])
        return carry

    lax.fori_loop(0, chunks, expand, 0)
    zero = jnp.zeros((1, width), F32)
    db5, db6, dg1, ds1, dg2, ds2 = (zero,) * 6
    for r in range(0, length, RT):
        rows = slice(r, r + RT)
        n, spread = norm_rows(a2[rows] + y_scr[rows] + row_of(pb_ref, 6))
        out.ref[rows] = (n * row_of(gain_ref, 2) + row_of(shift_ref, 2)).astype(BF16)
        position = shard * length + r + lax.broadcasted_iota(jnp.int32, (RT, 1), 0)
        g = jnp.where(position < rng[VALID], cot_ref[rows].astype(F32), 0.0)
        dg2 += jnp.sum(g * n, axis=0, keepdims=True)
        ds2 += jnp.sum(g, axis=0, keepdims=True)
        dh3 = norm_rows_back(g, n, spread, row_of(gain_ref, 2))
        dy3 = dh3.astype(BF16)
        db6 += jnp.sum(dy3.astype(F32), axis=0, keepdims=True)
        dy_scr[rows] = dy3
        y_scr[rows] = dh3
    out.send()

    parts = width // 128

    def contract(c, carry):
        cols = pl.ds(pl.multiple_of(c * width, width), width)
        total = jnp.zeros((1, width), F32)
        dus = []
        for r in range(0, length, RT):
            rows = slice(r, r + RT)
            du = (gp[c, rows] * dot(dy_scr[rows], w2_ref[cols, :], NT)).astype(BF16)
            total += jnp.sum(du.astype(F32), axis=0, keepdims=True)
            y_scr[rows] += dot(du, w1_ref[:, cols], NT)
            dus.append(du)
        deb.ref[0:1, cols] = total
        du = jnp.concatenate(dus, axis=0)
        g1 = dot(a2t[...], du)
        for j in range(parts):
            put_block(
                keep.ref, send.ref, c ^ shard, slice(inner + j * width, inner + (j + 1) * width),
                g1[:, j * 128 : (j + 1) * 128].astype(BF16),
            )
        g2 = dot(act[c], dy_scr[...], TN)
        at = pl.ds(pl.multiple_of(c * width, width), width)
        for b in range(4):
            put_block(
                keep.ref, send.ref, shard ^ b, at, g2[:, b * 128 : (b + 1) * 128].astype(BF16)
            )
        return carry

    lax.fori_loop(0, chunks, contract, 0)
    for r in range(0, length, RT):
        rows = slice(r, r + RT)
        up = y_scr[rows]
        n = n1[rows]
        dg1 += jnp.sum(up * n, axis=0, keepdims=True)
        ds1 += jnp.sum(up, axis=0, keepdims=True)
        dh2 = norm_rows_back(up, n, r1[rows, 0:1], row_of(gain_ref, 1))
        dh.ref[rows] = dh2
        dy2 = dh2.astype(BF16)
        dy_scr[rows] = dy2
        db5 += jnp.sum(dy2.astype(F32), axis=0, keepdims=True)
        do.ref[rows] = dot(dy2, wout_ref[...], NT).astype(BF16)
    dh.send()
    do.send()
    g3 = dot(o.ref[...], dy_scr[...], TN)
    for b in range(4):
        put_block(
            keep.ref, send.ref, shard ^ b, slice(2 * inner, 2 * inner + width),
            g3[:, b * 128 : (b + 1) * 128].astype(BF16),
        )
    for i, value in enumerate((db5, db6, dg1, dg2, ds1, ds2)):
        small.ref[i : i + 1, :] = value
    small.ref[6:8, :] = jnp.zeros((2, width), F32)


def cross_forward(rng, parts, fq, fk, q, a1, cot, wkv, wout, w1, w2, eb, pb, gain, shift):
    length, width = q.shape
    full, inner = len(parts) * length, w1.shape[1]
    return call(
        cross_body,
        rng,
        [wkv, pb, *parts, q, fq, fk, wout, a1, gain, shift, w1, w2, eb, cot],
        [
            ((full, width), BF16), ((full, width), BF16), ((length, width), BF16),
            ((width // 128, length, 128), F32), ((length, width), BF16), ((length, width), BF16),
            ((length, width), F32), ((2, 2 * inner + width, 128), BF16),
            ((2, 2 * inner + width, 128), BF16), ((1, inner), F32),
            ((8, width), F32),
        ],
        attend_scratch(length, full)
        + [
            ((length, width), F32), ((length, 128), F32), ((length, width), F32), ((width, length), BF16),
            ((inner // width, length, width), BF16), ((inner // width, length, width), F32),
            ((length, width), F32), ((length, width), BF16),
        ],
        flops=30 * 10**9,
        vmem=60,
    )


def back_body(rng, held, results, qh, doh, qm, dom, dq_scr, w_scr, c_scr, *, causal, pack):
    q, fq, lse, do, o, fk, k, v, xq, x0, x1, x2, x3 = held[:13]
    dq_out, dkv, w, small = results[:4]
    length = q.ref.shape[0]
    shard = rng[SHARD]
    dkv.ref[...] = jnp.zeros_like(dkv.ref)
    dq = attend_back(
        rng, q.get()[...], fq.get()[...], lse.get()[0], do.get()[...], o.get()[...], k.get(), v.get(),
        fk.get(), dkv.ref, qh, doh, qm, dom, dq_scr, causal,
    ).astype(BF16)
    dkv.send()
    dq_out.ref[...] = dq
    dq_out.send()
    w.ref[0] = dot(xq.get()[...], dq, TN).astype(BF16)
    w_scr[...] = jnp.zeros_like(w_scr)
    c_scr[...] = jnp.zeros_like(c_scr)
    for m, x in enumerate((x0, x1, x2, x3)):
        x_ref = x.get()

        def more(m=m, x_ref=x_ref):
            part = dkv.ref[m * length : (m + 1) * length, :]
            w_scr[...] += dot(x_ref[...], part, TN)
            c_scr[...] += jnp.sum(part[:, 128:].astype(F32), axis=0, keepdims=True)

        if causal and m:
            pl.when((shard ^ m) < shard)(more)
        else:
            more()
    w.ref[1] = w_scr[:, :128].astype(BF16)
    w.ref[2] = w_scr[:, 128:].astype(BF16)
    small.ref[0:1, :] = jnp.sum(dq.astype(F32), axis=0, keepdims=True)
    small.ref[1:2, :] = c_scr[0:1]
    small.ref[2:8, :] = jnp.zeros((6, 128), F32)
    if pack is not None:
        pack(shard, [x.get() for x in held[13:]], w.ref, small.ref, results[4].ref, results[5].ref)


def pack_early(shard, others, w, small, keep, send):
    w0, w1 = others
    width = w.shape[1]
    for b, columns in enumerate(((w0[0], w1[0]), (w0[1], w1[1]), (w[1], w0[2]), (w1[2], w[2]))):
        for at, value in enumerate(columns):
            put_block(keep, send, shard ^ b, slice(at * width, (at + 1) * width), value)


def pack_late(shard, others, w, small, keep, send):
    w2, a0, a1, a2, b0, b1, b2, b3, s0_ref, s2_ref, deb_ref = others
    width = w.shape[1]
    own, other = (a0, a1, a2, small), (b0, b1, b2, b3)
    for b, value in enumerate((w2[0], w[0], w[1], w[2])):
        put_block(keep, send, shard ^ b, slice(0, width), value)
    pad = keep.shape[1] - width
    for b in range(4):
        cols = slice(b * 128, (b + 1) * 128)
        rows = [deb_ref[0:1, b * width + j * 128 : b * width + (j + 1) * 128] for j in range(width // 128)]
        rows += [own[b][0:1], own[b][1:2], s0_ref[0:1, cols], other[b][0:1], other[b][1:2]]
        rows += [s2_ref[0:1, cols], s2_ref[1:2, cols]]
        rows += [s0_ref[1:2, cols], s2_ref[2:3, cols], s2_ref[3:4, cols]]
        rows += [s0_ref[2:3, cols], s2_ref[4:5, cols], s2_ref[5:6, cols]]
        rows.append(jnp.zeros((pad - len(rows), 128), F32))
        put_block(
            keep, send, shard ^ b, slice(width, width + pad), jnp.concatenate(rows, axis=0).astype(BF16)
        )


def attend_backward(rng, p, q, fq, lse, do, o, fk, k, v, xq, parts, causal, pack=None, extra=(), rows=0):
    length, width = q.shape
    full = k.shape[0]
    cut = pl.ds(p * 128, 128)
    outs = [((length, 128), BF16), ((full, 256), BF16), ((3, width, 128), BF16), ((8, 128), F32)]
    if pack is not None:
        outs += [((2, rows, 128), BF16)] * 2
    return call(
        functools.partial(back_body, causal=causal, pack=pack),
        rng,
        [(q, cut), fq, lse[p : p + 1], (do, cut), (o, cut), fk, (k, cut), (v, cut), xq, *parts, *extra],
        outs,
        [((2, length, 128), BF16)] * 4 + [((128, length), F32), ((width, 256), F32), ((8, 128), F32)],
        flops=9 * 10**9,
    )


def middle_body(rng, held, results, dy_scr):
    dq0, dq1, dq2, dq3, wq, dh2, n0, r0, gain, wout, o, u0, u1, u2, u3 = held
    dh, do, keep, send, small = results
    length, width = dh2.ref.shape
    pairs = width // 128
    shard = rng[SHARD]
    zero = jnp.zeros((1, width), F32)
    db2, dg0, ds0 = zero, zero, zero
    dq_refs = [x.get() for x in (dq0, dq1, dq2, dq3)]
    wq_ref, dh2_ref, n_ref, r_ref, gain_ref, wout_ref = (x.get() for x in (wq, dh2, n0, r0, gain, wout))
    for r in range(0, length, RT):
        rows = slice(r, r + RT)
        up = dh2_ref[rows] + dot(jnp.concatenate([d[rows] for d in dq_refs], axis=1), wq_ref[...], NT)
        n = n_ref[rows]
        dg0 += jnp.sum(up * n, axis=0, keepdims=True)
        ds0 += jnp.sum(up, axis=0, keepdims=True)
        new = norm_rows_back(up, n, r_ref[rows, 0:1], row_of(gain_ref, 0))
        dh.ref[rows] = new
        dy = new.astype(BF16)
        dy_scr[rows] = dy
        db2 += jnp.sum(dy.astype(F32), axis=0, keepdims=True)
        do.ref[rows] = dot(dy, wout_ref[...], NT).astype(BF16)
    dh.send()
    do.send()
    g = dot(o.get()[...], dy_scr[...], TN)
    for b in range(4):
        put_block(keep.ref, send.ref, shard ^ b, slice(0, width), g[:, b * 128 : (b + 1) * 128].astype(BF16))
    units = [x.get() for x in (u0, u1, u2, u3)]
    for b in range(4):
        put_block(keep.ref, send.ref, shard ^ b, slice(width, 2 * width), units[b][0])
    for i in range(2 * pairs):
        b, at = i // 2, 2 + i % 2
        put_block(
            keep.ref, send.ref, shard ^ b, slice(at * width, (at + 1) * width), units[i % pairs][1 + i // pairs]
        )
    for i, value in enumerate((db2, dg0, ds0)):
        small.ref[i : i + 1, :] = value
    small.ref[3:8, :] = jnp.zeros((5, width), F32)


def middle(rng, dqs, units, dh2, n, r, o, wq, wout, gain):
    length, width = dh2.shape
    return call(
        middle_body,
        rng,
        [*dqs, wq, dh2, n, r, gain, wout, o, *units],
        [
            ((length, width), F32), ((length, width), BF16), ((2, 4 * width, 128), BF16),
            ((2, 4 * width, 128), BF16), ((8, width), F32),
        ],
        [((length, width), BF16)],
        flops=3 * 10**9,
    )


def spread_body(rng, held, results, *, causal, offset):
    keep, send = results
    length, width = keep.ref.shape[1:]
    shard = rng[SHARD]
    refs = [x.get() for x in held]
    w_ref, parts = refs[0], refs[1:]
    for m in (1, 3, 0, 2):
        ref = (keep.ref, send.ref)[m % 2]

        def fill(m=m, ref=ref):
            for r in range(0, length, RT):
                rows = slice(m * length + r, m * length + r + RT)
                dk = jnp.concatenate([d[rows, :128] for d in parts], axis=1)
                dv = jnp.concatenate([d[rows, 128:] for d in parts], axis=1)
                total = dot(dk, w_ref[:, offset : offset + width], NT)
                total += dot(dv, w_ref[:, offset + width : offset + 2 * width], NT)
                ref[m // 2, r : r + RT] = total.astype(BF16)

        def clear(m=m, ref=ref):
            ref[m // 2] = jnp.zeros((length, width), BF16)

        if causal and m:
            pl.when((shard ^ m) < shard)(fill)
            pl.when((shard ^ m) > shard)(clear)
        else:
            fill()
        if m == 3:
            send.send()


def spread_keys(rng, dkvs, w, length, causal, offset):
    width = w.shape[0]
    return call(
        functools.partial(spread_body, causal=causal, offset=offset),
        rng,
        [w, *dkvs],
        [((2, length, width), BF16), ((2, length, width), BF16)],
        [],
        flops=2 * 10**9,
    )


def partner(x, axis, mask):
    n = lax.axis_size(axis)
    return lax.ppermute(x, axis, [(i, i ^ mask) for i in range(n)])


def add(a, b):
    return (a.astype(F32) + b.astype(F32)).astype(BF16)


def after(x, *deps):
    return lax.optimization_barrier((x, *deps))[0]


def half_of(x, bit):
    half = x.shape[0] // 2
    return lax.dynamic_slice_in_dim(x, bit * half, half, 0)


def dp_bit(j):
    return (lax.axis_index("dp") >> j) & 1


class Flow:
    def __init__(self, keep, send):
        bits = lax.axis_size("dp").bit_length() - 1
        self.steps = [("core", 0), ("chip", 0)]
        self.steps += [("fold", j) for j in range(bits)]
        self.steps += [("join", j) for j in reversed(range(bits))]
        self.keep, self.out, self.cur, self.got = keep, send, None, None

    def done(self):
        return not self.steps

    def begin(self):
        if self.done():
            return
        kind, j = self.steps[0]
        if kind == "core":
            self.got = partner(self.out, "seq", 1)
        elif kind == "chip":
            self.got = partner(self.out, "seq", 2)
        elif kind == "fold":
            self.got = partner(half_of(self.cur, 1 - dp_bit(j)), "dp", 1 << j)
        else:
            self.got = partner(self.cur, "dp", 1 << j)

    def end(self, *deps):
        if self.done():
            return
        kind, j = self.steps.pop(0)
        got = after(self.got, *deps) if deps else self.got
        if kind == "core":
            self.out = add(self.keep[1], got[1])
            self.cur = add(self.keep[0], got[0])
        elif kind == "chip":
            self.cur = add(self.cur, got)
        elif kind == "fold":
            self.cur = add(half_of(self.cur, dp_bit(j)), got)
        else:
            low = dp_bit(j) == 0
            self.cur = jnp.where(low, jnp.concatenate([self.cur, got]), jnp.concatenate([got, self.cur]))

    def state(self):
        return self.out if self.steps and self.steps[0][0] == "chip" else self.cur


def local(
    target, memory, cotangent, target_segments, source_segments, target_lengths, source_lengths,
    self_inproj, self_outproj, cross_query, cross_keyval, cross_outproj, ffn_expand, ffn_reduce,
    expand_bias, proj_bias, norm_gain, norm_shift,
):
    target, memory, cotangent = target[0], memory[0], cotangent[0]
    length, width = target.shape
    pairs = width // 128
    shard = lax.axis_index("seq").astype(jnp.int32)
    unit = 16 * lax.axis_size("dp")

    t2 = partner(target, "seq", 2)
    t1 = partner(target, "seq", 1)
    m1 = partner(memory, "seq", 1)
    self_rng, cross_rng, fq, self_fk, cross_fk = prepare(
        shard, target_lengths, source_lengths, target_segments, source_segments, length
    )
    t2 = after(t2, self_rng)
    t3 = partner(t2, "seq", 1)
    m2 = partner(after(memory, t2), "seq", 2)
    target_parts = [target, t1, t2, t3]

    q1, k1, v1, o1, lse1, a1, n0, r0, q2 = self_forward(
        self_rng, target_parts, fq, self_fk, self_inproj, self_outproj, cross_query, proj_bias,
        norm_gain, norm_shift,
    )
    m2 = after(m2, q2)
    memory_parts = [memory, m1, m2, partner(m2, "seq", 1)]
    a1_low = a1.astype(BF16)
    k2, v2, o2, lse2, layer_out, do2, dh2, keep_a, send_a, deb, small2 = cross_forward(
        cross_rng, memory_parts, fq, cross_fk, q2, a1, cotangent, cross_keyval, cross_outproj,
        ffn_expand, ffn_reduce, expand_bias, proj_bias, norm_gain, norm_shift,
    )
    flow_a = Flow(keep_a, send_a)
    flow_a.begin()

    def cross_back(p, *deps):
        rng = after(cross_rng, *deps) if deps else cross_rng
        return attend_backward(
            rng, p, q2, fq, lse2, do2, o2, cross_fk, k2, v2, a1_low, memory_parts, False
        )

    def self_back(p, *deps, **pack):
        rng = after(self_rng, *deps) if deps else self_rng
        return attend_backward(
            rng, p, q1, fq, lse1, do1, o1, self_fk, k1, v1, target, target_parts, True, **pack
        )

    c0 = cross_back(0)
    flow_a.end(c0[0])
    flow_a.begin()
    c1 = cross_back(1, flow_a.state(), c0[0])
    c2 = cross_back(2, c1[0])
    flow_a.end(c2[0])
    flow_a.begin()
    c3 = cross_back(3, flow_a.state(), c2[0])
    cross = (c0, c1, c2, c3)
    dh1, do1, keep_b, send_b, small0 = middle(
        self_rng, [c[0] for c in cross], [c[2] for c in cross], dh2, n0, r0, o1, cross_query,
        self_outproj, norm_gain,
    )
    flow_a.end(do1)
    flow_a.begin()
    flow_b = Flow(keep_b, send_b)
    flow_b.begin()
    mem_keep, mem_send = spread_keys(
        after(cross_rng, flow_a.state(), do1), [c[1] for c in cross], cross_keyval, length, False, 0
    )
    mem_got = partner(mem_send, "seq", 1)
    flow_b.end(mem_keep)
    flow_b.begin()
    s0 = self_back(0, flow_b.state(), mem_keep)
    flow_a.end(s0[0])
    flow_b.end(s0[0])
    mem_got = after(mem_got, s0[0])
    mem_far = add(mem_keep[1], mem_got[1])
    mem_get = partner(mem_far, "seq", 2)
    flow_a.begin()
    flow_b.begin()
    s1 = self_back(1, flow_a.state(), flow_b.state(), mem_far, s0[0])
    flow_a.end(s1[0])
    flow_b.end(s1[0])
    flow_a.begin()
    flow_b.begin()
    s2 = self_back(2, flow_a.state(), flow_b.state(), s1[0], pack=pack_early, extra=(s0[2], s1[2]), rows=2 * width)
    flow_c = Flow(s2[4], s2[5])
    flow_c.begin()
    flow_a.end(s2[0])
    flow_b.end(s2[0])
    mem_get = after(mem_get, s2[0])
    memory_grad = (
        mem_keep[0].astype(F32) + mem_got[0].astype(F32) + mem_get.astype(F32)
    )
    flow_a.begin()
    flow_b.begin()
    s3 = self_back(
        3, flow_a.state(), flow_b.state(), s2[0], pack=pack_late,
        extra=(s2[2], s0[3], s1[3], s2[3], c0[3], c1[3], c2[3], c3[3], small0, small2, deb),
        rows=width + unit,
    )
    selfs = (s0, s1, s2, s3)
    flow_d = Flow(s3[4], s3[5])
    flow_d.begin()
    flow_c.end(s3[0])
    flow_c.begin()
    tgt_keep, tgt_send = spread_keys(
        after(self_rng, flow_c.state(), s3[0]), [s[1] for s in selfs], self_inproj, length, True, width
    )
    flow_d.end(tgt_keep)
    flow_d.begin()
    flow_c.end(tgt_keep)
    flow_c.begin()
    tgt_got = partner(tgt_send, "seq", 1)
    flow_a.end(tgt_keep)
    flow_b.end(tgt_keep)
    flow_a.begin()
    flow_b.begin()
    tgt_far = add(tgt_keep[1], tgt_got[1])
    dq1 = jnp.concatenate([s[0] for s in selfs], axis=1)
    query_part = dh1 + dot(dq1, self_inproj[:, :width], NT) + tgt_keep[0].astype(F32) + tgt_got[0].astype(F32)
    flow_d.end()
    flow_d.begin()
    tgt_get = partner(after(tgt_far, flow_d.cur), "seq", 2)
    flows = (flow_d, flow_c, flow_a, flow_b)
    while not all(f.done() for f in flows):
        for f in flows[1:] + flows[:1]:
            f.end()
            f.begin()
    target_grad = query_part + tgt_get.astype(F32)

    def take(x, at, rows, cols):
        n = cols // 128
        x = x[at : at + n * rows].reshape(n, rows, 128).transpose(1, 0, 2)
        return x.reshape(rows, cols).astype(F32)

    inner = ffn_expand.shape[1]
    tail = flow_d.cur[width:].astype(F32)
    early, late = flow_c.cur.reshape(2, width, 128), flow_d.cur[:width]
    columns = [
        jnp.where(shard == 1, late, early[0]),
        jnp.where(shard == 1, early[0], jnp.where(shard == 2, late, early[1])),
        jnp.where((shard == 1) | (shard == 2), early[1], late),
    ]
    return (
        layer_out[None],
        target_grad[None],
        memory_grad[None],
        jnp.concatenate(columns, axis=1).astype(F32),
        take(flow_b.cur, 0, width, 128),
        take(flow_b.cur, width, width, 128),
        take(flow_b.cur, 2 * width, width, 256),
        take(flow_a.cur, 2 * inner, width, 128),
        take(flow_a.cur, inner, width, 512),
        take(flow_a.cur, 0, inner, 128),
        tail[0:4].reshape(1, 512),
        tail[4:11],
        tail[11:14],
        tail[14:17],
    )


def solution(mesh):
    rows, shard = P("dp", "seq", None), P(None, "seq")
    in_specs = (rows, rows, rows, P("dp", None), P("dp", None), P("dp"), P("dp")) + (P(),) * 11
    out_specs = (rows, rows, rows) + (shard,) * 11
    return jax.shard_map(local, mesh=mesh, in_specs=in_specs, out_specs=out_specs, check_vma=False)
```

```python
import functools
import jax
import jax.numpy as jnp
from jax import lax
from jax.experimental import pallas as pl
from jax.experimental.pallas import tpu as pltpu
from jax.sharding import PartitionSpec as P

BF16 = jnp.bfloat16
F32 = jnp.float32
EPSILON = 1e-05
BK = 256
RT = 256
NT = (((1,), (1,)), ((), ()))
NN = (((1,), (0,)), ((), ()))
TN = (((0,), (0,)), ((), ()))


def dot(a, b, dims=NN):
    return lax.dot_general(a, b, dims, preferred_element_type=F32)


class Held:
    def __init__(self, copy, ref):
        self.copy, self.ref, self.waited = copy, ref, False

    def get(self):
        if not self.waited:
            self.copy.wait()
            self.waited = True
        return self.ref


class Result:
    def __init__(self, copy, ref):
        self.copy, self.ref, self.started = copy, ref, False

    def send(self):
        self.copy.start()
        self.started = True


def call(body, rng, ins, outs, scratch, flops=10**9, vmem=24):
    arrays, columns = [], []
    for x in ins:
        x, cut = x if isinstance(x, tuple) else (x, None)
        arrays.append(x)
        columns.append(cut)
    shapes = []
    for x, cut in zip(arrays, columns):
        shapes.append(x.shape if cut is None else x.shape[:-1] + (cut.size,))
    n_in, n_out, n_scr = len(ins), len(outs), len(scratch)

    def kernel(rng_ref, *refs):
        hbm_in, refs = refs[:n_in], refs[n_in:]
        hbm_out, refs = refs[:n_out], refs[n_out:]
        vm_in, refs = refs[:n_in], refs[n_in:]
        vm_out, refs = refs[:n_out], refs[n_out:]
        scr, refs = refs[:n_scr], refs[n_scr:]
        sem_in, sem_out = refs
        held = []
        for i, (src, dst, cut) in enumerate(zip(hbm_in, vm_in, columns)):
            if cut is not None:
                src = src.at[(slice(None),) * (len(src.shape) - 1) + (cut,)]
            copy = pltpu.make_async_copy(src, dst, sem_in.at[i])
            copy.start()
            held.append(Held(copy, dst))
        results = [
            Result(pltpu.make_async_copy(src, dst, sem_out.at[i]), src)
            for i, (src, dst) in enumerate(zip(vm_out, hbm_out))
        ]
        body(rng_ref, held, results, *scr)
        for x in held:
            x.get()
        for x in results:
            if not x.started:
                x.send()
        for x in results:
            x.copy.wait()

    hbm = pl.BlockSpec(memory_space=pltpu.HBM)
    return pl.pallas_call(
        kernel,
        out_shape=tuple(pltpu.HBM(s, d) for s, d in outs),
        in_specs=[pl.BlockSpec(memory_space=pltpu.SMEM)] + [hbm] * n_in,
        out_specs=(hbm,) * n_out,
        scratch_shapes=[pltpu.VMEM(s, x.dtype) for s, x in zip(shapes, arrays)]
        + [pltpu.VMEM(s, d) for s, d in outs]
        + [pltpu.VMEM(s, d) for s, d in scratch]
        + [pltpu.SemaphoreType.DMA((n_in,)), pltpu.SemaphoreType.DMA((n_out,))],
        compiler_params=pltpu.CompilerParams(vmem_limit_bytes=vmem * 2**20),
        cost_estimate=pl.CostEstimate(flops=flops, bytes_accessed=2**20, transcendentals=0),
    )(rng, *[pltpu.with_memory_space_constraint(x, pltpu.HBM) for x in arrays])


LO0, HI0, LO1, HI1, SHARD, VALID = range(6)


def prepare_body(
    info, lengths, t_smem, t_ref, s_ref, self_rng, cross_rng, fq_ref, self_fk, cross_fk, self_fkt, cross_fkt
):
    length = fq_ref.shape[0]
    shard = info[0]
    valid, count = lengths[0], lengths[1]
    full = t_ref.shape[1]
    t_row, s_row = t_ref[...], s_ref[...]

    def number(mask):
        return jnp.sum(jnp.where(mask, 1.0, 0.0)).astype(jnp.int32)

    for half in range(2):
        first = t_smem[0, shard * length + half * RT]
        last = t_smem[0, shard * length + half * RT + RT - 1]
        self_rng[LO0 + 2 * half] = lax.div(number(t_row < first), BK)
        self_rng[HI0 + 2 * half] = 0
        cross_rng[LO0 + 2 * half] = lax.div(number(s_row < first), BK)
        end = jnp.minimum(number(s_row <= last), count)
        cross_rng[HI0 + 2 * half] = lax.div(end + BK - 1, BK)
    for ref in (self_rng, cross_rng):
        ref[SHARD] = shard
        ref[VALID] = valid
        ref[6] = 0
        ref[7] = 0
    f = lax.broadcasted_iota(jnp.int32, (128, 128), 1) % 64

    def column(ref, at):
        return jnp.broadcast_to(ref[0:1, pl.ds(pl.multiple_of(at, 128), 128)], (128, 128)).T

    row = lax.broadcasted_iota(jnp.int32, (128, 128), 0)
    for m in range(full // length):
        for t in range(0, length, 128):
            at = (shard ^ m) * length + t
            for ref, total, out, out_t in ((t_ref, valid, self_fk, self_fkt), (s_ref, count, cross_fk, cross_fkt)):
                seg = column(ref, at)
                seen = (seg == f) & (row + at < total)
                feature = jnp.where(
                    f < 8, jnp.where(seen, 0.0, -1e30), jnp.where(f < 11, 1.0, 0.0)
                )
                out[m * length + t : m * length + t + 128] = feature.astype(BF16)
                out_t[:, m * length + t : m * length + t + 128] = feature.astype(BF16).T[0:64]
                if m == 0 and out is self_fk:
                    fq_ref[t : t + 128] = jnp.where(seg == f, 1.0, 0.0).astype(BF16)


def prepare(shard, target_length, source_length, target_segments, source_segments, length):
    full = target_segments.shape[1]
    sd = jax.ShapeDtypeStruct
    smem, vm = pl.BlockSpec(memory_space=pltpu.SMEM), pl.BlockSpec(memory_space=pltpu.VMEM)
    return pl.pallas_call(
        prepare_body,
        out_shape=(
            sd((8,), jnp.int32), sd((8,), jnp.int32), sd((length, 128), BF16), sd((full, 128), BF16),
            sd((full, 128), BF16), sd((64, full), BF16), sd((64, full), BF16),
        ),
        in_specs=[smem, smem, smem, vm, vm],
        out_specs=(smem, smem, vm, vm, vm, vm, vm),
    )(
        shard.reshape(1), jnp.concatenate([target_length, source_length]), target_segments,
        target_segments, source_segments,
    )


def half_masks():
    lane = lax.broadcasted_iota(jnp.int32, (1, 128), 1)
    return (lane < 64, lane >= 64), lane % 64


def relative_offset(block, shard, per_shard):
    owner = lax.div(block, per_shard)
    return pl.multiple_of(((owner ^ shard) * per_shard + lax.rem(block, per_shard)) * BK, BK)


def triangle(transposed):
    a = lax.broadcasted_iota(jnp.int32, (BK, BK), 0)
    b = lax.broadcasted_iota(jnp.int32, (BK, BK), 1)
    return a <= b if transposed else b <= a


def attend(rng, q_ref, fq_ref, kt, v_ref, fkt_ref, o_ref, lse_ref, qh, s_even, s_odd, mx_even, mx_odd, acc, causal):
    length, width = q_ref.shape
    per = length // BK
    pairs = width // 128
    shard = rng[SHARD]
    conds, _ = half_masks()
    lo0, hi0, lo1, hi1 = rng[LO0], rng[HI0], rng[LO1], rng[HI1]
    both, upper, lower = slice(0, length), slice(0, RT), slice(RT, length)
    s_bank, mx_bank = (s_even, s_odd), (mx_even, mx_odd)

    def scores(g, off, slot, rows, diagonal):
        s_scr, mx = s_bank[g % 2], mx_bank[g % 2]
        mask = fkt_ref[0:64, pl.ds(off, BK)]
        for h in range(2):
            at = g * 128 + 64 * h
            mine = kt[at : at + 64, pl.ds(off, BK)]
            w = jnp.concatenate([mine, mask] if h == 0 else [mask, mine], axis=0)
            s = dot(qh[h, rows], w)
            if diagonal:
                n = rows.stop - rows.start
                a = lax.broadcasted_iota(jnp.int32, (n, BK), 0)
                b = lax.broadcasted_iota(jnp.int32, (n, BK), 1)
                s = jnp.where(b <= a, s, -1e30)
            s_scr[h, slot, rows] = s
            m = mx[h, rows]
            for t in range(0, BK, 128):
                m = jnp.maximum(m, s[:, t : t + 128])
            mx[h, rows] = m

    def values(g, off, slot, rows):
        s_scr, mx = s_bank[g % 2], mx_bank[g % 2]
        for h in range(2):
            vp = v_ref[pl.ds(off, BK), g * 128 : g * 128 + 128]
            vh = jnp.where(conds[h], vp, jnp.ones_like(vp))
            m = mx[h, rows]
            p = jnp.concatenate(
                [
                    jnp.exp(s_scr[h, slot, rows, t : t + 128] - m).astype(BF16)
                    for t in range(0, BK, 128)
                ],
                axis=1,
            )
            acc[h, rows] += dot(p, vh)

    def sweep(f):
        def span(lo, hi, rows):
            def step(kb, carry):
                f(relative_offset(kb, shard, per), kb, rows, False)
                return carry

            lax.fori_loop(lo, hi, step, 0)

        if causal:
            own = shard * per
            span(lo0, jnp.minimum(lo1, own), upper)
            span(lo1, own, both)
            f(0, own, both, True)
            f(BK, own + 1, lower, True)
        else:
            span(lo0, jnp.minimum(lo1, hi0), upper)
            span(lo1, hi0, both)
            span(jnp.maximum(hi0, lo1), hi1, lower)

    def start(g):
        mx = mx_bank[g % 2]
        cols = slice(g * 128, g * 128 + 128)
        for h in range(2):
            qh[h] = jnp.where(conds[h], q_ref[:, cols], fq_ref[...])
            mx[h] = jnp.full((length, 128), -3e38, F32)

    def turn(g):
        mx = mx_bank[g % 2]
        for h in range(2):
            for r in range(0, length, 128):
                rows = slice(r, r + 128)
                top = jnp.max(mx[h, rows], axis=-1, keepdims=True)
                mx[h, rows] = jnp.broadcast_to(top, (128, 128))
                acc[h, rows] = jnp.zeros((128, 128), F32)

    def finish(g):
        mx = mx_bank[g % 2]
        cols = slice(g * 128, g * 128 + 128)
        for r in range(0, length, 128):
            rows = slice(r, r + 128)
            a0, a1 = acc[0, rows], acc[1, rows]
            num = jnp.where(conds[0], a0, a1)
            den = jnp.where(conds[0], a1, a0)
            o_ref[rows, cols] = (num / pltpu.roll(den, 64, 1)).astype(BF16)
            lse_ref[g, rows] = jnp.where(conds[0], mx[1, rows], mx[0, rows]) + jnp.log(den)

    start(0)
    sweep(lambda off, slot, rows, edge: scores(0, off, slot, rows, edge))

    for g in range(1, pairs):
        turn(g - 1)
        start(g)

        def pair(off, slot, rows, edge, g=g):
            scores(g, off, slot, rows, edge)
            values(g - 1, off, slot, rows)

        sweep(pair)
        finish(g - 1)
    turn(pairs - 1)
    sweep(lambda off, slot, rows, edge: values(pairs - 1, off, slot, rows))
    finish(pairs - 1)


def attend_scratch(length, full):
    return [
        ((2, length, 128), BF16),
        ((2, full // BK, length, BK), F32),
        ((2, full // BK, length, BK), F32),
        ((2, length, 128), F32),
        ((2, length, 128), F32),
        ((2, length, 128), F32),
    ]


def attend_back(rng, q, fq, logsum, do, o, k_ref, v_ref, fk_ref, dkv_ref, qh, doh, qm, dom, dq_scr, causal):
    length = q.shape[0]
    per = length // BK
    shard = rng[SHARD]
    conds, l64 = half_masks()

    def negated_parts(x):
        high = x.astype(BF16).astype(F32)
        rest = x - high
        mid = rest.astype(BF16).astype(F32)
        low = rest - mid
        return -jnp.where(
            l64 == 8, high, jnp.where(l64 == 9, mid, jnp.where(l64 == 10, low, 0.0))
        )

    for r in range(0, length, 128):
        rows = slice(r, r + 128)
        q_r, do_r = q[rows], do[rows]
        prod = do_r.astype(F32) * o[rows].astype(F32)
        delta = jnp.where(
            conds[0],
            jnp.sum(jnp.where(conds[1], prod, 0.0), axis=-1, keepdims=True),
            jnp.sum(jnp.where(conds[0], prod, 0.0), axis=-1, keepdims=True),
        )
        fl = (negated_parts(logsum[rows]) + fq[rows].astype(F32)).astype(BF16)
        fd = negated_parts(delta).astype(BF16)
        zero = jnp.zeros_like(q_r)
        for h in range(2):
            qh[h, :, rows] = jnp.where(conds[h], q_r, fl).T
            doh[h, :, rows] = jnp.where(conds[h], do_r, fd).T
            qm[h, rows] = jnp.where(conds[h], q_r, zero)
            dom[h, rows] = jnp.where(conds[h], do_r, zero)
    dq_scr[...] = jnp.zeros_like(dq_scr)
    ones = jnp.where((l64 >= 8) & (l64 <= 10), 1.0, 0.0).astype(BF16)

    def block(off, halves, diagonal=None, size=BK):
        kp = k_ref[pl.ds(off, size), :]
        vp = v_ref[pl.ds(off, size), :]
        fk = fk_ref[pl.ds(off, size), :]
        ones_block = jnp.broadcast_to(ones, vp.shape)
        kt = kp.T
        dk = jnp.zeros((size, 128), F32)
        dv = jnp.zeros((size, 128), F32)
        for h in range(2):
            kh = jnp.where(conds[h], kp, fk)
            vh = jnp.where(conds[h], vp, ones_block)
            rows = slice(64 * h, 64 * h + 64)
            for half in halves:
                r = half * RT
                s = dot(kh, qh[h, :, r : r + RT])
                if diagonal == half:
                    s = jnp.where(triangle(True), s, -1e30)
                p = jnp.exp(s)
                dp = dot(vh, doh[h, :, r : r + RT])
                ds = (p * dp).astype(BF16)
                dv += dot(p.astype(BF16), dom[h, r : r + RT])
                dk += dot(ds, qm[h, r : r + RT])
                dq_scr[rows, r : r + RT] += dot(kt[rows], ds)
        dkv_ref[pl.ds(off, size), 0:128] = dk.astype(BF16)
        dkv_ref[pl.ds(off, size), 128:256] = dv.astype(BF16)

    def sweep(lo, hi, halves):
        def step(kb, carry):
            block(relative_offset(kb, shard, per), halves)
            return carry

        lax.fori_loop(lo, hi, step, 0)

    def sweep_two(lo, hi, halves):
        first = lax.div(lo + 1, 2)
        last = lax.div(hi, 2)

        def step(kb, carry):
            block(relative_offset(2 * kb, shard, per), halves, size=2 * BK)
            return carry

        lax.fori_loop(first, last, step, 0)
        sweep(lo, jnp.minimum(2 * first, hi), halves)
        sweep(jnp.maximum(2 * last, 2 * first), hi, halves)

    lo0, lo1 = rng[LO0], rng[LO1]
    common = sweep_two
    if causal:
        own = shard * per
        sweep(lo0, jnp.minimum(lo1, own), (0,))
        common(lo1, own, (0, 1))
        block(0, (0, 1), 0)
        block(BK, (1,), 1)
    else:
        hi0, hi1 = rng[HI0], rng[HI1]
        sweep(lo0, jnp.minimum(lo1, hi0), (0,))
        common(lo1, hi0, (0, 1))
        sweep(jnp.maximum(hi0, lo1), hi1, (1,))
    return dq_scr[...].T * 0.125


def norm_rows(hidden):
    center = hidden - jnp.mean(hidden, axis=-1, keepdims=True)
    spread = lax.rsqrt(jnp.mean(center * center, axis=-1, keepdims=True) + EPSILON)
    return center * spread, spread


def norm_rows_back(upstream, normed, spread, gain):
    scaled = upstream * gain
    return spread * (
        scaled
        - jnp.mean(scaled, axis=-1, keepdims=True)
        - normed * jnp.mean(scaled * normed, axis=-1, keepdims=True)
    )


def put_block(keep_ref, send_ref, m, rows, value):
    def keep():
        keep_ref[m // 2, rows] = value

    def send():
        send_ref[m // 2, rows] = value

    pl.when(m % 2 == 0)(keep)
    pl.when(m % 2 == 1)(send)


def put_far(keep_ref, send_ref, m, rows, value):
    def keep():
        keep_ref[m % 2, rows] = value

    def send():
        send_ref[m % 2, rows] = value

    pl.when(m // 2 == 0)(keep)
    pl.when(m // 2 == 1)(send)


def row_of(ref, i):
    return ref[i : i + 1, :].astype(F32)


def self_body(rng, held, results, qh, s_even, s_odd, mx_even, mx_odd, acc, kt):
    x0, win, pb, x1, x2, x3, fq, fkt, wout, wq, gain, shift = held
    q, k, v, o, lse, a, n_out, r_out, q2_out, xt, at_out = results
    length, width = x0.ref.shape
    shard = rng[SHARD]
    eighth = jnp.asarray(0.125, BF16)
    x_ref, win_ref, pb_ref = x0.get(), win.get(), pb.get()
    for r in range(0, length, RT):
        rows = slice(r, r + RT)
        q.ref[rows] = (dot(x_ref[rows], win_ref[:, :width]) + row_of(pb_ref, 0)).astype(BF16) * eighth
    q.send()
    for m, x in enumerate((x0, x1, x2, x3)):
        x_m = x.get()

        def fill(m=m, x_m=x_m):
            for r in range(0, length, RT):
                x = x_m[r : r + RT]
                rows = slice(m * length + r, m * length + r + RT)
                k_new = dot(x, win_ref[:, width : 2 * width]).astype(BF16)
                k.ref[rows] = k_new
                kt[:, rows] = k_new.T
                v.ref[rows] = (dot(x, win_ref[:, 2 * width :]) + row_of(pb_ref, 1)).astype(BF16)
                xt.ref[:, rows] = x.T

        if m == 0:
            fill()
        else:
            pl.when((shard ^ m) < shard)(fill)
    k.send()
    v.send()
    xt.send()
    attend(rng, q.ref, fq.get(), kt, v.ref, fkt.get(), o.ref, lse.ref, qh, s_even, s_odd, mx_even, mx_odd, acc, True)
    o.send()
    lse.send()
    wout_ref, wq_ref, gain_ref, shift_ref = wout.get(), wq.get(), gain.get(), shift.get()
    for r in range(0, length, RT):
        rows = slice(r, r + RT)
        h = x_ref[rows].astype(F32) + dot(o.ref[rows], wout_ref[...]) + row_of(pb_ref, 2)
        n, spread = norm_rows(h)
        a_new = n * row_of(gain_ref, 0) + row_of(shift_ref, 0)
        n_out.ref[rows] = n
        r_out.ref[rows] = jnp.broadcast_to(spread, (RT, 128))
        a.ref[rows] = a_new
        a_low = a_new.astype(BF16)
        at_out.ref[:, rows] = a_low.T
        q2 = dot(a_low, wq_ref[...]) + row_of(pb_ref, 3)
        q2_out.ref[rows] = q2.astype(BF16) * eighth


def self_forward(rng, parts, fq, fkt, win, wout, wq, pb, gain, shift):
    length, width = parts[0].shape
    full = len(parts) * length
    return call(
        self_body,
        rng,
        [parts[0], win, pb, *parts[1:], fq, fkt, wout, wq, gain, shift],
        [
            ((length, width), BF16), ((full, width), BF16), ((full, width), BF16),
            ((length, width), BF16), ((width // 128, length, 128), F32), ((length, width), F32),
            ((length, width), F32), ((length, 128), F32), ((length, width), BF16), ((width, full), BF16),
            ((width, length), BF16),
        ],
        attend_scratch(length, full) + [((width, full), BF16)],
        flops=14 * 10**9,
        vmem=40,
    )


GELU_A = 0.7978845608028654
GELU_B = 0.044715


def cross_body(rng, held, results, qh, s_even, s_odd, mx_even, mx_odd, acc, kt, n1, r1, a2, a2t, act, gp, y_scr, dy_scr):
    wkv, pb, y0, y1, y2, y3, q, fq, fkt, wout, a1, gain, shift, w1, w2, eb, cot = held
    k, v, o, lse, out, do, dh, keep, send, deb, small, yt = results
    length, width = q.ref.shape
    shard = rng[SHARD]
    wkv_ref, pb_ref = wkv.get(), pb.get()
    for m, y in enumerate((y0, y1, y2, y3)):
        y_ref = y.get()
        for r in range(0, length, RT):
            x = y_ref[r : r + RT]
            rows = slice(m * length + r, m * length + r + RT)
            k_new = dot(x, wkv_ref[:, :width]).astype(BF16)
            k.ref[rows] = k_new
            kt[:, rows] = k_new.T
            yt.ref[:, rows] = x.T
            v.ref[rows] = (dot(x, wkv_ref[:, width:]) + row_of(pb_ref, 4)).astype(BF16)
    k.send()
    v.send()
    yt.send()
    attend(rng, q.get(), fq.get(), kt, v.ref, fkt.get(), o.ref, lse.ref, qh, s_even, s_odd, mx_even, mx_odd, acc, False)
    o.send()
    lse.send()
    wout_ref, a1_ref, gain_ref, shift_ref = wout.get(), a1.get(), gain.get(), shift.get()
    for r in range(0, length, RT):
        rows = slice(r, r + RT)
        n, spread = norm_rows(a1_ref[rows] + dot(o.ref[rows], wout_ref[...]) + row_of(pb_ref, 5))
        n1[rows] = n
        r1[rows] = jnp.broadcast_to(spread, (RT, 128))
        a2[rows] = n * row_of(gain_ref, 1) + row_of(shift_ref, 1)
        y_scr[rows] = jnp.zeros((RT, width), F32)
    a2t[...] = a2[...].astype(BF16).T
    w1_ref, w2_ref, eb_ref, cot_ref = w1.get(), w2.get(), eb.get(), cot.get()
    inner = w1_ref.shape[1]
    chunks = inner // width

    def expand(c, carry):
        cols = pl.ds(pl.multiple_of(c * width, width), width)
        for r in range(0, length, RT):
            rows = slice(r, r + RT)
            u = dot(a2[rows].astype(BF16), w1_ref[:, cols]) + eb_ref[0:1, cols].astype(F32)
            square = u * u
            t = jnp.tanh(GELU_A * (u + GELU_B * u * square))
            half = 0.5 * (1.0 + t)
            act_low = (u * half).astype(BF16)
            act[c, rows] = act_low
            gp[c, rows] = half + 0.5 * u * (1.0 - t * t) * (GELU_A + 3.0 * GELU_A * GELU_B * square)
            y_scr[rows] += dot(act_low, w2_ref[cols, :])
        return carry

    lax.fori_loop(0, chunks, expand, 0)
    zero = jnp.zeros((1, width), F32)
    db5, db6, dg1, ds1, dg2, ds2 = (zero,) * 6
    for r in range(0, length, RT):
        rows = slice(r, r + RT)
        n, spread = norm_rows(a2[rows] + y_scr[rows] + row_of(pb_ref, 6))
        out.ref[rows] = (n * row_of(gain_ref, 2) + row_of(shift_ref, 2)).astype(BF16)
        position = shard * length + r + lax.broadcasted_iota(jnp.int32, (RT, 1), 0)
        g = jnp.where(position < rng[VALID], cot_ref[rows].astype(F32), 0.0)
        dg2 += jnp.sum(g * n, axis=0, keepdims=True)
        ds2 += jnp.sum(g, axis=0, keepdims=True)
        dh3 = norm_rows_back(g, n, spread, row_of(gain_ref, 2))
        dy3 = dh3.astype(BF16)
        db6 += jnp.sum(dy3.astype(F32), axis=0, keepdims=True)
        dy_scr[rows] = dy3
        y_scr[rows] = dh3
    out.send()

    parts = width // 128

    def contract(c, carry):
        cols = pl.ds(pl.multiple_of(c * width, width), width)
        total = jnp.zeros((1, width), F32)
        dus = []
        for r in range(0, length, RT):
            rows = slice(r, r + RT)
            du = (gp[c, rows] * dot(dy_scr[rows], w2_ref[cols, :], NT)).astype(BF16)
            total += jnp.sum(du.astype(F32), axis=0, keepdims=True)
            y_scr[rows] += dot(du, w1_ref[:, cols], NT)
            dus.append(du)
        deb.ref[0:1, cols] = total
        du = jnp.concatenate(dus, axis=0)
        g1 = dot(a2t[...], du)
        for j in range(parts):
            put_block(
                keep.ref, send.ref, c ^ shard, slice(inner + j * width, inner + (j + 1) * width),
                g1[:, j * 128 : (j + 1) * 128].astype(BF16),
            )
        g2 = dot(act[c], dy_scr[...], TN)
        at = pl.ds(pl.multiple_of(c * width, width), width)
        for b in range(4):
            put_block(
                keep.ref, send.ref, shard ^ b, at, g2[:, b * 128 : (b + 1) * 128].astype(BF16)
            )
        return carry

    lax.fori_loop(0, chunks, contract, 0)
    for r in range(0, length, RT):
        rows = slice(r, r + RT)
        up = y_scr[rows]
        n = n1[rows]
        dg1 += jnp.sum(up * n, axis=0, keepdims=True)
        ds1 += jnp.sum(up, axis=0, keepdims=True)
        dh2 = norm_rows_back(up, n, r1[rows, 0:1], row_of(gain_ref, 1))
        dh.ref[rows] = dh2
        dy2 = dh2.astype(BF16)
        dy_scr[rows] = dy2
        db5 += jnp.sum(dy2.astype(F32), axis=0, keepdims=True)
        do.ref[rows] = dot(dy2, wout_ref[...], NT).astype(BF16)
    dh.send()
    do.send()
    g3 = dot(o.ref[...], dy_scr[...], TN)
    for b in range(4):
        put_block(
            keep.ref, send.ref, shard ^ b, slice(2 * inner, 2 * inner + width),
            g3[:, b * 128 : (b + 1) * 128].astype(BF16),
        )
    for i, value in enumerate((db5, db6, dg1, dg2, ds1, ds2)):
        small.ref[i : i + 1, :] = value
    small.ref[6:8, :] = jnp.zeros((2, width), F32)


def cross_forward(rng, parts, fq, fkt, q, a1, cot, wkv, wout, w1, w2, eb, pb, gain, shift):
    length, width = q.shape
    full, inner = len(parts) * length, w1.shape[1]
    return call(
        cross_body,
        rng,
        [wkv, pb, *parts, q, fq, fkt, wout, a1, gain, shift, w1, w2, eb, cot],
        [
            ((full, width), BF16), ((full, width), BF16), ((length, width), BF16),
            ((width // 128, length, 128), F32), ((length, width), BF16), ((length, width), BF16),
            ((length, width), F32), ((2, 2 * inner + width, 128), BF16),
            ((2, 2 * inner + width, 128), BF16), ((1, inner), F32),
            ((8, width), F32), ((width, full), BF16),
        ],
        attend_scratch(length, full)
        + [
            ((width, full), BF16),
            ((length, width), F32), ((length, 128), F32), ((length, width), F32), ((width, length), BF16),
            ((inner // width, length, width), BF16), ((inner // width, length, width), F32),
            ((length, width), F32), ((length, width), BF16),
        ],
        flops=30 * 10**9,
        vmem=60,
    )


def back_body(rng, held, results, qh, doh, qm, dom, dq_scr, w_scr, c_scr, *, causal, pack):
    q, fq, lse, do, o, fk, k, v, xq, xt = held[:10]
    dq_out, dkv, w, small = results[:4]
    length = q.ref.shape[0]
    shard = rng[SHARD]
    dkv.ref[...] = jnp.zeros_like(dkv.ref)
    dq = attend_back(
        rng, q.get(), fq.get(), lse.get().at[0], do.get(), o.get(), k.get(), v.get(),
        fk.get(), dkv.ref, qh, doh, qm, dom, dq_scr, causal,
    ).astype(BF16)
    dkv.send()
    dq_out.ref[...] = dq
    dq_out.send()
    w.ref[0] = dot(xq.get()[...], dq).astype(BF16)
    w_scr[...] = jnp.zeros_like(w_scr)
    c_scr[...] = jnp.zeros_like(c_scr)
    xt_ref = xt.get()
    for m in range(xt_ref.shape[1] // length):

        def more(m=m):
            span = slice(m * length, (m + 1) * length)
            part = dkv.ref[span, :]
            w_scr[...] += dot(xt_ref[:, span], part)
            c_scr[...] += jnp.sum(part[:, 128:].astype(F32), axis=0, keepdims=True)

        if causal and m:
            pl.when((shard ^ m) < shard)(more)
        else:
            more()
    w.ref[1] = w_scr[:, :128].astype(BF16)
    w.ref[2] = w_scr[:, 128:].astype(BF16)
    small.ref[0:1, :] = jnp.sum(dq.astype(F32), axis=0, keepdims=True)
    small.ref[1:2, :] = c_scr[0:1]
    small.ref[2:8, :] = jnp.zeros((6, 128), F32)
    if pack is not None:
        pack(shard, [x.get() for x in held[10:]], w.ref, small.ref, results[4].ref, results[5].ref)


def pack_early(shard, others, w, small, keep, send):
    w0, w1 = others
    width = w.shape[1]
    for b, columns in enumerate(((w0[0], w1[0]), (w0[1], w1[1]), (w[1], w0[2]), (w1[2], w[2]))):
        for at, value in enumerate(columns):
            put_far(keep, send, shard ^ b, slice(at * width, (at + 1) * width), value)


def pack_late(shard, others, w, small, keep, send):
    w2, a0, a1, a2, b0, b1, b2, b3, s0_ref, s2_ref, deb_ref = others
    width = w.shape[1]
    own, other = (a0, a1, a2, small), (b0, b1, b2, b3)
    for b, value in enumerate((w2[0], w[0], w[1], w[2])):
        put_block(keep, send, shard ^ b, slice(0, width), value)
    pad = keep.shape[1] - width
    for b in range(4):
        cols = slice(b * 128, (b + 1) * 128)
        rows = [deb_ref[0:1, b * width + j * 128 : b * width + (j + 1) * 128] for j in range(width // 128)]
        rows += [own[b][0:1], own[b][1:2], s0_ref[0:1, cols], other[b][0:1], other[b][1:2]]
        rows += [s2_ref[0:1, cols], s2_ref[1:2, cols]]
        rows += [s0_ref[1:2, cols], s2_ref[2:3, cols], s2_ref[3:4, cols]]
        rows += [s0_ref[2:3, cols], s2_ref[4:5, cols], s2_ref[5:6, cols]]
        rows.append(jnp.zeros((pad - len(rows), 128), F32))
        put_block(
            keep, send, shard ^ b, slice(width, width + pad), jnp.concatenate(rows, axis=0).astype(BF16)
        )


def attend_backward(rng, p, q, fq, lse, do, o, fk, k, v, xq, xt, causal, pack=None, extra=(), rows=0):
    length, width = q.shape
    full = k.shape[0]
    cut = pl.ds(p * 128, 128)
    outs = [((length, 128), BF16), ((full, 256), BF16), ((3, width, 128), BF16), ((8, 128), F32)]
    if pack is not None:
        outs += [((2, rows, 128), BF16)] * 2
    return call(
        functools.partial(back_body, causal=causal, pack=pack),
        rng,
        [(q, cut), fq, lse[p : p + 1], (do, cut), (o, cut), fk, (k, cut), (v, cut), xq, xt, *extra],
        outs,
        [((2, 128, length), BF16)] * 2 + [((2, length, 128), BF16)] * 2 + [((128, length), F32), ((width, 256), F32), ((8, 128), F32)],
        flops=9 * 10**9,
    )


def middle_body(rng, held, results, dy_scr):
    dq0, dq1, dq2, dq3, wq, dh2, n0, r0, gain, wout, o, u0, u1, u2, u3 = held
    dh, do, keep, send, small = results
    length, width = dh2.ref.shape
    pairs = width // 128
    shard = rng[SHARD]
    zero = jnp.zeros((1, width), F32)
    db2, dg0, ds0 = zero, zero, zero
    dq_refs = [x.get() for x in (dq0, dq1, dq2, dq3)]
    wq_ref, dh2_ref, n_ref, r_ref, gain_ref, wout_ref = (x.get() for x in (wq, dh2, n0, r0, gain, wout))
    for r in range(0, length, RT):
        rows = slice(r, r + RT)
        up = dh2_ref[rows] + dot(jnp.concatenate([d[rows] for d in dq_refs], axis=1), wq_ref[...], NT)
        n = n_ref[rows]
        dg0 += jnp.sum(up * n, axis=0, keepdims=True)
        ds0 += jnp.sum(up, axis=0, keepdims=True)
        new = norm_rows_back(up, n, r_ref[rows, 0:1], row_of(gain_ref, 0))
        dh.ref[rows] = new
        dy = new.astype(BF16)
        dy_scr[rows] = dy
        db2 += jnp.sum(dy.astype(F32), axis=0, keepdims=True)
        do.ref[rows] = dot(dy, wout_ref[...], NT).astype(BF16)
    dh.send()
    do.send()
    g = dot(o.get()[...], dy_scr[...], TN)
    for b in range(4):
        put_block(keep.ref, send.ref, shard ^ b, slice(0, width), g[:, b * 128 : (b + 1) * 128].astype(BF16))
    units = [x.get() for x in (u0, u1, u2, u3)]
    for b in range(4):
        put_block(keep.ref, send.ref, shard ^ b, slice(width, 2 * width), units[b][0])
    for i in range(2 * pairs):
        b, at = i // 2, 2 + i % 2
        put_block(
            keep.ref, send.ref, shard ^ b, slice(at * width, (at + 1) * width), units[i % pairs][1 + i // pairs]
        )
    for i, value in enumerate((db2, dg0, ds0)):
        small.ref[i : i + 1, :] = value
    small.ref[3:8, :] = jnp.zeros((5, width), F32)


def middle(rng, dqs, units, dh2, n, r, o, wq, wout, gain):
    length, width = dh2.shape
    return call(
        middle_body,
        rng,
        [*dqs, wq, dh2, n, r, gain, wout, o, *units],
        [
            ((length, width), F32), ((length, width), BF16), ((2, 4 * width, 128), BF16),
            ((2, 4 * width, 128), BF16), ((8, width), F32),
        ],
        [((length, width), BF16)],
        flops=3 * 10**9,
    )


def spread_body(rng, held, results, *, causal, offset):
    keep, send = results
    length, width = keep.ref.shape[1:]
    shard = rng[SHARD]
    refs = [x.get() for x in held]
    w_ref, parts = refs[0], refs[1:]
    for m in (1, 3, 0, 2):
        ref = (keep.ref, send.ref)[m % 2]

        def fill(m=m, ref=ref):
            for r in range(0, length, RT):
                rows = slice(m * length + r, m * length + r + RT)
                dk = jnp.concatenate([d[rows, :128] for d in parts], axis=1)
                dv = jnp.concatenate([d[rows, 128:] for d in parts], axis=1)
                total = dot(dk, w_ref[:, offset : offset + width], NT)
                total += dot(dv, w_ref[:, offset + width : offset + 2 * width], NT)
                ref[m // 2, r : r + RT] = total.astype(BF16)

        def clear(m=m, ref=ref):
            ref[m // 2] = jnp.zeros((length, width), BF16)

        if causal and m:
            pl.when((shard ^ m) < shard)(fill)
            pl.when((shard ^ m) > shard)(clear)
        else:
            fill()
        if m == 3:
            send.send()


def spread_keys(rng, dkvs, w, length, causal, offset):
    width = w.shape[0]
    return call(
        functools.partial(spread_body, causal=causal, offset=offset),
        rng,
        [w, *dkvs],
        [((2, length, width), BF16), ((2, length, width), BF16)],
        [],
        flops=2 * 10**9,
    )


def partner(x, axis, mask):
    n = lax.axis_size(axis)
    return lax.ppermute(x, axis, [(i, i ^ mask) for i in range(n)])


def add(a, b):
    return (a.astype(F32) + b.astype(F32)).astype(BF16)


def after(x, *deps):
    return lax.optimization_barrier((x, *deps))[0]


def half_of(x, bit):
    half = x.shape[0] // 2
    return lax.dynamic_slice_in_dim(x, bit * half, half, 0)


def dp_bit(j):
    return (lax.axis_index("dp") >> j) & 1


class Flow:
    def __init__(self, keep, send):
        bits = lax.axis_size("dp").bit_length() - 1
        self.steps = [("core", 0), ("chip", 0)]
        self.steps += [("fold", j) for j in range(bits)]
        self.steps += [("join", j) for j in reversed(range(bits))]
        self.keep, self.out, self.cur, self.got = keep, send, None, None

    def done(self):
        return not self.steps

    def begin(self):
        if self.done():
            return
        kind, j = self.steps[0]
        if kind == "core":
            self.got = partner(self.out, "seq", 1)
        elif kind == "chip":
            self.got = partner(self.out, "seq", 2)
        elif kind == "fold":
            self.got = partner(half_of(self.cur, 1 - dp_bit(j)), "dp", 1 << j)
        else:
            self.got = partner(self.cur, "dp", 1 << j)

    def end(self, *deps):
        if self.done():
            return
        kind, j = self.steps.pop(0)
        got = after(self.got, *deps) if deps else self.got
        if kind == "core":
            self.out = add(self.keep[1], got[1])
            self.cur = add(self.keep[0], got[0])
        elif kind == "chip":
            self.cur = add(self.cur, got)
        elif kind == "fold":
            self.cur = add(half_of(self.cur, dp_bit(j)), got)
        else:
            low = dp_bit(j) == 0
            self.cur = jnp.where(low, jnp.concatenate([self.cur, got]), jnp.concatenate([got, self.cur]))

    def state(self):
        return self.out if self.steps and self.steps[0][0] == "chip" else self.cur


def local(
    target, memory, cotangent, target_segments, source_segments, target_lengths, source_lengths,
    self_inproj, self_outproj, cross_query, cross_keyval, cross_outproj, ffn_expand, ffn_reduce,
    expand_bias, proj_bias, norm_gain, norm_shift,
):
    target, memory, cotangent = target[0], memory[0], cotangent[0]
    length, width = target.shape
    pairs = width // 128
    shard = lax.axis_index("seq").astype(jnp.int32)
    unit = 16 * lax.axis_size("dp")

    t2 = partner(target, "seq", 2)
    t1 = partner(target, "seq", 1)
    m1 = partner(memory, "seq", 1)
    self_rng, cross_rng, fq, self_fk, cross_fk, self_fkt, cross_fkt = prepare(
        shard, target_lengths, source_lengths, target_segments, source_segments, length
    )
    t2 = after(t2, self_rng)
    t3 = partner(t2, "seq", 1)
    m2 = partner(after(memory, t2), "seq", 2)
    target_parts = [target, t1, t2, t3]

    q1, k1, v1, o1, lse1, a1, n0, r0, q2, target_t, a1_t = self_forward(
        self_rng, target_parts, fq, self_fkt, self_inproj, self_outproj, cross_query, proj_bias,
        norm_gain, norm_shift,
    )
    m2 = after(m2, q2)
    memory_parts = [memory, m1, m2, partner(m2, "seq", 1)]
    k2, v2, o2, lse2, layer_out, do2, dh2, keep_a, send_a, deb, small2, memory_t = cross_forward(
        cross_rng, memory_parts, fq, cross_fkt, q2, a1, cotangent, cross_keyval, cross_outproj,
        ffn_expand, ffn_reduce, expand_bias, proj_bias, norm_gain, norm_shift,
    )
    flow_a = Flow(keep_a, send_a)
    flow_a.begin()

    def cross_back(p, *deps):
        rng = after(cross_rng, *deps) if deps else cross_rng
        return attend_backward(
            rng, p, q2, fq, lse2, do2, o2, cross_fk, k2, v2, a1_t, memory_t, False
        )

    def self_back(p, *deps, **pack):
        rng = after(self_rng, *deps) if deps else self_rng
        return attend_backward(
            rng, p, q1, fq, lse1, do1, o1, self_fk, k1, v1, target_t[:, :length], target_t, True, **pack
        )

    c0 = cross_back(0)
    flow_a.end(c0[0])
    flow_a.begin()
    c1 = cross_back(1, flow_a.state(), c0[0])
    c2 = cross_back(2, c1[0])
    flow_a.end(c2[0])
    flow_a.begin()
    c3 = cross_back(3, flow_a.state(), c2[0])
    cross = (c0, c1, c2, c3)
    dh1, do1, keep_b, send_b, small0 = middle(
        self_rng, [c[0] for c in cross], [c[2] for c in cross], dh2, n0, r0, o1, cross_query,
        self_outproj, norm_gain,
    )
    flow_a.end(do1)
    flow_a.begin()
    flow_b = Flow(keep_b, send_b)
    flow_b.begin()
    mem_keep, mem_send = spread_keys(
        after(cross_rng, flow_a.state(), do1), [c[1] for c in cross], cross_keyval, length, False, 0
    )
    mem_got = partner(mem_send, "seq", 1)
    flow_b.end(mem_keep)
    flow_b.begin()
    s0 = self_back(0, flow_b.state(), mem_keep)
    flow_a.end(s0[0])
    flow_b.end(s0[0])
    mem_got = after(mem_got, s0[0])
    mem_far = add(mem_keep[1], mem_got[1])
    mem_get = partner(mem_far, "seq", 2)
    flow_a.begin()
    flow_b.begin()
    s1 = self_back(1, flow_a.state(), flow_b.state(), mem_far, s0[0])
    flow_a.end(s1[0])
    flow_b.end(s1[0])
    flow_a.begin()
    flow_b.begin()
    s2 = self_back(2, flow_a.state(), flow_b.state(), s1[0], pack=pack_early, extra=(s0[2], s1[2]), rows=2 * width)
    keep_c, send_c = s2[4], s2[5]
    got_c = partner(send_c, "seq", 2)
    flow_a.end(s2[0])
    flow_b.end(s2[0])
    mem_get = after(mem_get, s2[0])
    memory_grad = (
        mem_keep[0].astype(F32) + mem_got[0].astype(F32) + mem_get.astype(F32)
    )
    flow_a.begin()
    flow_b.begin()
    s3 = self_back(
        3, flow_a.state(), flow_b.state(), s2[0], pack=pack_late,
        extra=(s2[2], s0[3], s1[3], s2[3], c0[3], c1[3], c2[3], c3[3], small0, small2, deb),
        rows=width + unit,
    )
    selfs = (s0, s1, s2, s3)
    keep_d, send_d = s3[4], s3[5]
    got_d = partner(send_d, "seq", 1)
    two_c = add(keep_c, after(got_c, s3[0]))
    core_c = partner(two_c[1], "seq", 1)
    flow_a.end(s3[0])
    flow_b.end(s3[0])
    flow_a.begin()
    flow_b.begin()
    far_d, near_d = add(keep_d[1], got_d[1]), add(keep_d[0], got_d[0])
    get_d = partner(far_d, "seq", 2)
    tgt_keep, tgt_send = spread_keys(
        after(self_rng, far_d, two_c, flow_a.state(), flow_b.state()), [s[1] for s in selfs], self_inproj,
        length, True, width,
    )
    get_d, core_c = after(get_d, tgt_keep), after(core_c, tgt_keep)
    tgt_got = partner(tgt_send, "seq", 1)
    flow_b.end(tgt_keep)
    flow_b.begin()
    block = jnp.concatenate([add(two_c[0], core_c), add(near_d, get_d)])
    dq1 = jnp.concatenate([s[0] for s in selfs], axis=1)
    tgt_got = after(tgt_got, block)
    tgt_far = add(tgt_keep[1], tgt_got[1])
    tgt_get = partner(tgt_far, "seq", 2)
    block = after(block, tgt_far)
    devices = lax.axis_size("dp")
    parts = lax.all_to_all(block.reshape(devices, -1, 128), "dp", 0, 0, tiled=True)
    part = jnp.sum(parts.astype(F32), axis=0).astype(BF16)
    flow_b.end(part)
    flow_b.begin()
    part = after(part, flow_b.state())
    whole = lax.all_to_all(jnp.broadcast_to(part[None], parts.shape), "dp", 0, 0, tiled=True).reshape(-1, 128)
    flow_a.end()
    flow_b.end()
    for flow in (flow_a, flow_b):
        while not flow.done():
            flow.begin()
            flow.end()
    target_grad = (
        dh1 + dot(dq1, self_inproj[:, :width], NT)
        + (tgt_keep[0].astype(F32) + tgt_got[0].astype(F32) + tgt_get.astype(F32))
    )

    def take(x, at, rows, cols):
        n = cols // 128
        x = x[at : at + n * rows].reshape(n, rows, 128).transpose(1, 0, 2)
        return x.reshape(rows, cols).astype(F32)

    inner = ffn_expand.shape[1]
    tail = whole[3 * width :].astype(F32)
    early, late = whole[: 2 * width].reshape(2, width, 128), whole[2 * width : 3 * width]
    columns = [
        jnp.where(shard == 1, late, early[0]),
        jnp.where(shard == 1, early[0], jnp.where(shard == 2, late, early[1])),
        jnp.where((shard == 1) | (shard == 2), early[1], late),
    ]
    return (
        layer_out[None],
        target_grad[None],
        memory_grad[None],
        jnp.concatenate(columns, axis=1).astype(F32),
        take(flow_b.cur, 0, width, 128),
        take(flow_b.cur, width, width, 128),
        take(flow_b.cur, 2 * width, width, 256),
        take(flow_a.cur, 2 * inner, width, 128),
        take(flow_a.cur, inner, width, 512),
        take(flow_a.cur, 0, inner, 128),
        tail[0:4].reshape(1, 512),
        tail[4:11],
        tail[11:14],
        tail[14:17],
    )


def solution(mesh):
    rows, shard = P("dp", "seq", None), P(None, "seq")
    in_specs = (rows, rows, rows, P("dp", None), P("dp", None), P("dp"), P("dp")) + (P(),) * 11
    out_specs = (rows, rows, rows) + (shard,) * 11
    return jax.shard_map(local, mesh=mesh, in_specs=in_specs, out_specs=out_specs, check_vma=False)
```

```python
import functools
import jax
import jax.numpy as jnp
from jax import lax
from jax.experimental import pallas as pl
from jax.experimental.pallas import tpu as pltpu
from jax.sharding import PartitionSpec as P

BF16 = jnp.bfloat16
F32 = jnp.float32
EPSILON = 1e-05
BK = 256
RT = 256
NT = (((1,), (1,)), ((), ()))
NN = (((1,), (0,)), ((), ()))
TN = (((0,), (0,)), ((), ()))


def dot(a, b, dims=NN):
    return lax.dot_general(a, b, dims, preferred_element_type=F32)


class Held:
    def __init__(self, copy, ref):
        self.copy, self.ref, self.started, self.waited = copy, ref, False, False

    def start(self):
        if not self.started:
            self.copy.start()
            self.started = True

    def get(self):
        self.start()
        if not self.waited:
            self.copy.wait()
            self.waited = True
        return self.ref


class Result:
    def __init__(self, copy, ref):
        self.copy, self.ref, self.started = copy, ref, False

    def send(self):
        self.copy.start()
        self.started = True


def call(body, rng, ins, outs, scratch, flops=10**7, vmem=24, loose=(), early=None):
    arrays, columns = [], []
    for x in ins:
        x, cut = x if isinstance(x, tuple) else (x, None)
        arrays.append(x)
        columns.append(cut)
    shapes = []
    for x, cut in zip(arrays, columns):
        if cut is None:
            shapes.append(x.shape)
        else:
            shapes.append(x.shape[1:] if isinstance(cut, int) else x.shape[:-1] + (cut.size,))
    n_in, n_out, n_scr = len(ins), len(outs), len(scratch)

    def kernel(rng_ref, *refs):
        hbm_in, refs = refs[:n_in], refs[n_in:]
        hbm_out, refs = refs[:n_out], refs[n_out:]
        vm_in, refs = refs[:n_in], refs[n_in:]
        vm_out, refs = refs[:n_out], refs[n_out:]
        scr, refs = refs[:n_scr], refs[n_scr:]
        sem_in, sem_out = refs
        held = []
        for i, (src, dst, cut) in enumerate(zip(hbm_in, vm_in, columns)):
            if isinstance(cut, int):
                src = src.at[cut]
            elif cut is not None:
                src = src.at[(slice(None),) * (len(src.shape) - 1) + (cut,)]
            held.append(Held(pltpu.make_async_copy(src, dst, sem_in.at[i]), dst))
        for x in held[:early]:
            x.start()
        results = [
            Result(pltpu.make_async_copy(src, dst, sem_out.at[i]), src)
            for i, (src, dst) in enumerate(zip(vm_out, hbm_out))
        ]
        body(rng_ref, held, results, *scr)
        for x in held:
            x.get()
        for x in results:
            if not x.started:
                x.send()
        for x in results:
            x.copy.wait()

    hbm = pl.BlockSpec(memory_space=pltpu.HBM)
    return pl.pallas_call(
        kernel,
        out_shape=tuple(pltpu.HBM(s, d) for s, d in outs),
        in_specs=[pl.BlockSpec(memory_space=pltpu.SMEM)] + [hbm] * n_in,
        out_specs=(hbm,) * n_out,
        scratch_shapes=[pltpu.VMEM(s, x.dtype) for s, x in zip(shapes, arrays)]
        + [pltpu.VMEM(s, d) for s, d in outs]
        + [pltpu.VMEM(s, d) for s, d in scratch]
        + [pltpu.SemaphoreType.DMA((n_in,)), pltpu.SemaphoreType.DMA((n_out,))],
        compiler_params=pltpu.CompilerParams(vmem_limit_bytes=vmem * 2**20),
        cost_estimate=pl.CostEstimate(flops=flops, bytes_accessed=2**20, transcendentals=0),
    )(
        rng,
        *[
            x if any(x is y for y in loose) else pltpu.with_memory_space_constraint(x, pltpu.HBM)
            for x in arrays
        ],
    )


LO0, HI0, LO1, HI1, SHARD, VALID = range(6)


def prepare_body(
    info, lengths, t_smem, t_ref, s_ref, self_rng, cross_rng, fq_ref, self_fk, cross_fk, self_fkt, cross_fkt
):
    length = fq_ref.shape[0]
    shard = info[0]
    valid, count = lengths[0], lengths[1]
    full = t_ref.shape[1]
    t_row, s_row = t_ref[...], s_ref[...]

    def number(mask):
        return jnp.sum(jnp.where(mask, 1.0, 0.0)).astype(jnp.int32)

    for half in range(2):
        first = t_smem[0, shard * length + half * RT]
        last = t_smem[0, shard * length + half * RT + RT - 1]
        self_rng[LO0 + 2 * half] = lax.div(number(t_row < first), BK)
        self_rng[HI0 + 2 * half] = 0
        cross_rng[LO0 + 2 * half] = lax.div(number(s_row < first), BK)
        end = jnp.minimum(number(s_row <= last), count)
        cross_rng[HI0 + 2 * half] = lax.div(end + BK - 1, BK)
    for ref in (self_rng, cross_rng):
        ref[SHARD] = shard
        ref[VALID] = valid
        ref[6] = 0
        ref[7] = 0
    f = lax.broadcasted_iota(jnp.int32, (128, 128), 1) % 64

    def column(ref, at):
        return jnp.broadcast_to(ref[0:1, pl.ds(pl.multiple_of(at, 128), 128)], (128, 128)).T

    row = lax.broadcasted_iota(jnp.int32, (128, 128), 0)
    for m in range(full // length):
        for t in range(0, length, 128):
            at = (shard ^ m) * length + t
            for ref, total, out, out_t in ((t_ref, valid, self_fk, self_fkt), (s_ref, count, cross_fk, cross_fkt)):
                seg = column(ref, at)
                seen = (seg == f) & (row + at < total)
                feature = jnp.where(
                    f < 8, jnp.where(seen, 0.0, -1e30), jnp.where(f < 11, 1.0, 0.0)
                )
                out[m * length + t : m * length + t + 128] = feature.astype(BF16)
                out_t[:, m * length + t : m * length + t + 128] = feature.astype(BF16).T[0:64]
                if m == 0 and out is self_fk:
                    fq_ref[t : t + 128] = jnp.where(seg == f, 1.0, 0.0).astype(BF16)


def prepare(shard, target_length, source_length, target_segments, source_segments, length):
    full = target_segments.shape[1]
    sd = jax.ShapeDtypeStruct
    smem, vm = pl.BlockSpec(memory_space=pltpu.SMEM), pl.BlockSpec(memory_space=pltpu.VMEM)
    return pl.pallas_call(
        prepare_body,
        out_shape=(
            sd((8,), jnp.int32), sd((8,), jnp.int32), sd((length, 128), BF16), sd((full, 128), BF16),
            sd((full, 128), BF16), sd((64, full), BF16), sd((64, full), BF16),
        ),
        in_specs=[smem, smem, smem, vm, vm],
        out_specs=(smem, smem, vm, vm, vm, vm, vm),
    )(
        shard.reshape(1), jnp.concatenate([target_length, source_length]), target_segments,
        target_segments, source_segments,
    )


def start_all(held):
    for x in held:
        x.start()


def half_masks():
    lane = lax.broadcasted_iota(jnp.int32, (1, 128), 1)
    return (lane < 64, lane >= 64), lane % 64


def relative_offset(block, shard, per_shard):
    owner = lax.div(block, per_shard)
    return pl.multiple_of(((owner ^ shard) * per_shard + lax.rem(block, per_shard)) * BK, BK)


def triangle(transposed):
    a = lax.broadcasted_iota(jnp.int32, (BK, BK), 0)
    b = lax.broadcasted_iota(jnp.int32, (BK, BK), 1)
    return a <= b if transposed else b <= a


def attend(rng, q_ref, fq_ref, kt, v_ref, fkt_ref, o_ref, lse_ref, qh, s_even, s_odd, mx_even, mx_odd, acc, causal):
    length, width = q_ref.shape
    per = length // BK
    pairs = width // 128
    shard = rng[SHARD]
    conds, _ = half_masks()
    lo0, hi0, lo1, hi1 = rng[LO0], rng[HI0], rng[LO1], rng[HI1]
    both, upper, lower = slice(0, length), slice(0, RT), slice(RT, length)
    s_bank, mx_bank = (s_even, s_odd), (mx_even, mx_odd)

    def scores(g, off, slot, rows, diagonal):
        s_scr, mx = s_bank[g % 2], mx_bank[g % 2]
        mask = fkt_ref[0:64, pl.ds(off, BK)]
        for h in range(2):
            at = g * 128 + 64 * h
            mine = kt[at : at + 64, pl.ds(off, BK)]
            w = jnp.concatenate([mine, mask] if h == 0 else [mask, mine], axis=0)
            s = dot(qh[h, rows], w)
            if diagonal:
                n = rows.stop - rows.start
                a = lax.broadcasted_iota(jnp.int32, (n, BK), 0)
                b = lax.broadcasted_iota(jnp.int32, (n, BK), 1)
                s = jnp.where(b <= a, s, -1e30)
            s_scr[h, slot, rows] = s
            m = mx[h, rows]
            for t in range(0, BK, 128):
                m = jnp.maximum(m, s[:, t : t + 128])
            mx[h, rows] = m

    def values(g, off, slot, rows):
        s_scr, mx = s_bank[g % 2], mx_bank[g % 2]
        for h in range(2):
            vp = v_ref[pl.ds(off, BK), g * 128 : g * 128 + 128]
            vh = jnp.where(conds[h], vp, jnp.ones_like(vp))
            m = mx[h, rows]
            p = jnp.concatenate(
                [
                    jnp.exp(s_scr[h, slot, rows, t : t + 128] - m).astype(BF16)
                    for t in range(0, BK, 128)
                ],
                axis=1,
            )
            acc[h, rows] += dot(p, vh)

    def sweep(f):
        def span(lo, hi, rows):
            def step(kb, carry):
                f(relative_offset(kb, shard, per), kb, rows, False)
                return carry

            lax.fori_loop(lo, hi, step, 0)

        if causal:
            own = shard * per
            span(lo0, jnp.minimum(lo1, own), upper)
            span(lo1, own, both)
            f(0, own, both, True)
            f(BK, own + 1, lower, True)
        else:
            span(lo0, jnp.minimum(lo1, hi0), upper)
            span(lo1, hi0, both)
            span(jnp.maximum(hi0, lo1), hi1, lower)

    def start(g):
        mx = mx_bank[g % 2]
        cols = slice(g * 128, g * 128 + 128)
        for h in range(2):
            qh[h] = jnp.where(conds[h], q_ref[:, cols], fq_ref[...])
            mx[h] = jnp.full((length, 128), -3e38, F32)

    def turn(g):
        mx = mx_bank[g % 2]
        for h in range(2):
            for r in range(0, length, 128):
                rows = slice(r, r + 128)
                top = jnp.max(mx[h, rows], axis=-1, keepdims=True)
                mx[h, rows] = jnp.broadcast_to(top, (128, 128))
                acc[h, rows] = jnp.zeros((128, 128), F32)

    def finish(g):
        mx = mx_bank[g % 2]
        cols = slice(g * 128, g * 128 + 128)
        for r in range(0, length, 128):
            rows = slice(r, r + 128)
            a0, a1 = acc[0, rows], acc[1, rows]
            num = jnp.where(conds[0], a0, a1)
            den = jnp.where(conds[0], a1, a0)
            o_ref[rows, cols] = (num / pltpu.roll(den, 64, 1)).astype(BF16)
            lse_ref[g, rows] = jnp.where(conds[0], mx[1, rows], mx[0, rows]) + jnp.log(den)

    start(0)
    sweep(lambda off, slot, rows, edge: scores(0, off, slot, rows, edge))

    for g in range(1, pairs):
        turn(g - 1)
        start(g)

        def pair(off, slot, rows, edge, g=g):
            scores(g, off, slot, rows, edge)
            values(g - 1, off, slot, rows)

        sweep(pair)
        finish(g - 1)
    turn(pairs - 1)
    sweep(lambda off, slot, rows, edge: values(pairs - 1, off, slot, rows))
    finish(pairs - 1)


def attend_scratch(length, full):
    return [
        ((2, length, 128), BF16),
        ((2, full // BK, length, BK), F32),
        ((2, full // BK, length, BK), F32),
        ((2, length, 128), F32),
        ((2, length, 128), F32),
        ((2, length, 128), F32),
    ]


def attend_back(rng, q, fq, logsum, do, o, keys, dkv_ref, qh, doh, qm, dom, dq_scr, causal):
    length = q.shape[0]
    per = length // BK
    shard = rng[SHARD]
    conds, l64 = half_masks()

    def negated_parts(x):
        high = x.astype(BF16).astype(F32)
        rest = x - high
        mid = rest.astype(BF16).astype(F32)
        low = rest - mid
        return -jnp.where(
            l64 == 8, high, jnp.where(l64 == 9, mid, jnp.where(l64 == 10, low, 0.0))
        )

    for r in range(0, length, 128):
        rows = slice(r, r + 128)
        q_r, do_r = q[rows], do[rows]
        prod = do_r.astype(F32) * o[rows].astype(F32)
        delta = jnp.where(
            conds[0],
            jnp.sum(jnp.where(conds[1], prod, 0.0), axis=-1, keepdims=True),
            jnp.sum(jnp.where(conds[0], prod, 0.0), axis=-1, keepdims=True),
        )
        fl = (negated_parts(logsum[rows]) + fq[rows].astype(F32)).astype(BF16)
        fd = negated_parts(delta).astype(BF16)
        zero = jnp.zeros_like(q_r)
        for h in range(2):
            qh[h, :, rows] = jnp.where(conds[h], q_r, fl).T
            doh[h, :, rows] = jnp.where(conds[h], do_r, fd).T
            qm[h, rows] = jnp.where(conds[h], q_r, zero)
            dom[h, rows] = jnp.where(conds[h], do_r, zero)
    dq_scr[...] = jnp.zeros_like(dq_scr)
    ones = jnp.where((l64 >= 8) & (l64 <= 10), 1.0, 0.0).astype(BF16)
    k_ref, v_ref, fk_ref = (x.get() for x in keys)

    def block(off, halves, diagonal=None, size=BK):
        kp = k_ref[pl.ds(off, size), :]
        vp = v_ref[pl.ds(off, size), :]
        fk = fk_ref[pl.ds(off, size), :]
        ones_block = jnp.broadcast_to(ones, vp.shape)
        kt = kp.T
        dk = jnp.zeros((size, 128), F32)
        dv = jnp.zeros((size, 128), F32)
        for h in range(2):
            kh = jnp.where(conds[h], kp, fk)
            vh = jnp.where(conds[h], vp, ones_block)
            rows = slice(64 * h, 64 * h + 64)
            for half in halves:
                r = half * RT
                s = dot(kh, qh[h, :, r : r + RT])
                if diagonal == half:
                    s = jnp.where(triangle(True), s, -1e30)
                p = jnp.exp(s)
                dp = dot(vh, doh[h, :, r : r + RT])
                ds = (p * dp).astype(BF16)
                dv += dot(p.astype(BF16), dom[h, r : r + RT])
                dk += dot(ds, qm[h, r : r + RT])
                dq_scr[rows, r : r + RT] += dot(kt[rows], ds)
        dkv_ref[pl.ds(off, size), 0:128] = dk.astype(BF16)
        dkv_ref[pl.ds(off, size), 128:256] = dv.astype(BF16)

    def sweep(lo, hi, halves):
        def step(kb, carry):
            block(relative_offset(kb, shard, per), halves)
            return carry

        lax.fori_loop(lo, hi, step, 0)

    def sweep_two(lo, hi, halves):
        first = lax.div(lo + 1, 2)
        last = lax.div(hi, 2)

        def step(kb, carry):
            block(relative_offset(2 * kb, shard, per), halves, size=2 * BK)
            return carry

        lax.fori_loop(first, last, step, 0)
        sweep(lo, jnp.minimum(2 * first, hi), halves)
        sweep(jnp.maximum(2 * last, 2 * first), hi, halves)

    lo0, lo1 = rng[LO0], rng[LO1]
    common = sweep_two
    if causal:
        own = shard * per
        sweep(lo0, jnp.minimum(lo1, own), (0,))
        common(lo1, own, (0, 1))
        block(0, (0, 1), 0)
        block(BK, (1,), 1)
    else:
        hi0, hi1 = rng[HI0], rng[HI1]
        sweep(lo0, jnp.minimum(lo1, hi0), (0,))
        common(lo1, hi0, (0, 1))
        sweep(jnp.maximum(hi0, lo1), hi1, (1,))
    return dq_scr[...].T * 0.125


def norm_rows(hidden):
    center = hidden - jnp.mean(hidden, axis=-1, keepdims=True)
    spread = lax.rsqrt(jnp.mean(center * center, axis=-1, keepdims=True) + EPSILON)
    return center * spread, spread


def norm_rows_back(upstream, normed, spread, gain):
    scaled = upstream * gain
    return spread * (
        scaled
        - jnp.mean(scaled, axis=-1, keepdims=True)
        - normed * jnp.mean(scaled * normed, axis=-1, keepdims=True)
    )


def put_block(keep_ref, send_ref, m, rows, value):
    def keep():
        keep_ref[m // 2, rows] = value

    def send():
        send_ref[m // 2, rows] = value

    pl.when(m % 2 == 0)(keep)
    pl.when(m % 2 == 1)(send)


def put_far(keep_ref, send_ref, m, rows, value):
    def keep():
        keep_ref[m % 2, rows] = value

    def send():
        send_ref[m % 2, rows] = value

    pl.when(m // 2 == 0)(keep)
    pl.when(m // 2 == 1)(send)


def row_of(ref, i):
    return ref[i : i + 1, :].astype(F32)


def self_body(rng, held, results, qh, s_even, s_odd, mx_even, mx_odd, acc, kt):
    x0, win, pb, x1, x2, x3, fq, fkt, wout, wq, gain, shift = held
    q, k, v, o, lse, a, n_out, r_out, q2_out, xt, at_out = results
    length, width = x0.ref.shape
    shard = rng[SHARD]
    eighth = jnp.asarray(0.125, BF16)
    x_ref, win_ref, pb_ref = x0.get(), win.get(), pb.get()
    start_all(held)
    q.ref[...] = (dot(x_ref[...], win_ref[:, :width]) + row_of(pb_ref, 0)).astype(BF16) * eighth
    q.send()
    for m, x in enumerate((x0, x1, x2, x3)):
        x_m = x.get()

        def fill(m=m, x_m=x_m):
            x = x_m[...]
            rows = slice(m * length, (m + 1) * length)
            for c in range(0, width, 256):
                cols = slice(c, c + 256)
                k_new = dot(x, win_ref[:, width + c : width + c + 256]).astype(BF16)
                k.ref[rows, cols] = k_new
                kt[cols, rows] = k_new.T
                v_new = dot(x, win_ref[:, 2 * width + c : 2 * width + c + 256])
                v.ref[rows, cols] = (v_new + pb_ref[1:2, cols].astype(F32)).astype(BF16)
            xt.ref[:, rows] = x.T

        if m == 0:
            fill()
        else:
            pl.when((shard ^ m) < shard)(fill)
    k.send()
    v.send()
    xt.send()
    attend(rng, q.ref, fq.get(), kt, v.ref, fkt.get(), o.ref, lse.ref, qh, s_even, s_odd, mx_even, mx_odd, acc, True)
    o.send()
    lse.send()
    wout_ref, wq_ref, gain_ref, shift_ref = wout.get(), wq.get(), gain.get(), shift.get()
    for r in range(0, length, RT):
        rows = slice(r, r + RT)
        h = x_ref[rows].astype(F32) + dot(o.ref[rows], wout_ref[...]) + row_of(pb_ref, 2)
        n, spread = norm_rows(h)
        a_new = n * row_of(gain_ref, 0) + row_of(shift_ref, 0)
        n_out.ref[rows] = n
        r_out.ref[rows] = jnp.broadcast_to(spread, (RT, 128))
        a.ref[rows] = a_new
        a_low = a_new.astype(BF16)
        at_out.ref[:, rows] = a_low.T
        q2 = dot(a_low, wq_ref[...]) + row_of(pb_ref, 3)
        q2_out.ref[rows] = q2.astype(BF16) * eighth


def self_forward(rng, parts, fq, fkt, win, wout, wq, pb, gain, shift):
    length, width = parts[0].shape
    full = len(parts) * length
    return call(
        self_body,
        rng,
        [parts[0], win, pb, *parts[1:], fq, fkt, wout, wq, gain, shift],
        [
            ((length, width), BF16), ((full, width), BF16), ((full, width), BF16),
            ((length, width), BF16), ((width // 128, length, 128), F32), ((length, width), F32),
            ((length, width), F32), ((length, 128), F32), ((length, width), BF16), ((width, full), BF16),
            ((width, length), BF16),
        ],
        attend_scratch(length, full) + [((width, full), BF16)],
        flops=10**7,
        vmem=40,
        loose=parts[1:],
        early=6,
    )


GELU_A = 0.7978845608028654
GELU_B = 0.044715


def cross_body(rng, held, results, qh, s_even, s_odd, mx_even, mx_odd, acc, kt, n1, r1, a2, a2_low, a2t, act, gp, y_scr, dy_scr):
    wkv, pb, y0, y1, y2, y3, q, fq, fkt, wout, a1, gain, shift, w1, w2, eb, cot = held
    k, v, o, lse, out, do, dh, keep, send, deb, small, yt = results
    length, width = q.ref.shape
    shard = rng[SHARD]
    wkv_ref, pb_ref = wkv.get(), pb.get()
    for m, y in enumerate((y0, y1, y2, y3)):
        y_ref = y.get()
        if m == 1:
            start_all(held)
        x = y_ref[...]
        rows = slice(m * length, (m + 1) * length)
        for c in range(0, width, 256):
            cols = slice(c, c + 256)
            k_new = dot(x, wkv_ref[:, cols]).astype(BF16)
            k.ref[rows, cols] = k_new
            kt[cols, rows] = k_new.T
            v_new = dot(x, wkv_ref[:, width + c : width + c + 256])
            v.ref[rows, cols] = (v_new + pb_ref[4:5, cols].astype(F32)).astype(BF16)
        yt.ref[:, rows] = x.T
    k.send()
    v.send()
    yt.send()
    attend(rng, q.get(), fq.get(), kt, v.ref, fkt.get(), o.ref, lse.ref, qh, s_even, s_odd, mx_even, mx_odd, acc, False)
    o.send()
    lse.send()
    wout_ref, a1_ref, gain_ref, shift_ref = wout.get(), a1.get(), gain.get(), shift.get()
    for r in range(0, length, RT):
        rows = slice(r, r + RT)
        n, spread = norm_rows(a1_ref[rows] + dot(o.ref[rows], wout_ref[...]) + row_of(pb_ref, 5))
        n1[rows] = n
        r1[rows] = jnp.broadcast_to(spread, (RT, 128))
        a2[rows] = n * row_of(gain_ref, 1) + row_of(shift_ref, 1)
        y_scr[rows] = jnp.zeros((RT, width), F32)
    a2_low[...] = a2[...].astype(BF16)
    a2t[...] = a2_low[...].T
    w1_ref, w2_ref, eb_ref, cot_ref = w1.get(), w2.get(), eb.get(), cot.get()
    inner = w1_ref.shape[1]
    chunks = inner // width

    def expand(c, carry):
        cols = pl.ds(pl.multiple_of(c * width, width), width)
        for t in range(0, width, 256):
            half_cols = pl.ds(pl.multiple_of(c * width + t, 256), 256)
            u = dot(a2_low[...], w1_ref[:, half_cols]) + eb_ref[0:1, half_cols].astype(F32)
            square = u * u
            th = jnp.tanh(u * (GELU_A + (GELU_A * GELU_B) * square))
            half = 0.5 * th + 0.5
            act[c, :, t : t + 256] = (u * half).astype(BF16)
            slope = (u - u * (th * th)) * (0.5 * GELU_A + (1.5 * GELU_A * GELU_B) * square)
            gp[c, :, t : t + 256] = half + slope
        y_scr[...] += dot(act[c], w2_ref[cols, :])
        return carry

    lax.fori_loop(0, chunks, expand, 0)
    zero = jnp.zeros((1, width), F32)
    db5, db6, dg1, ds1, dg2, ds2 = (zero,) * 6
    for r in range(0, length, RT):
        rows = slice(r, r + RT)
        n, spread = norm_rows(a2[rows] + y_scr[rows] + row_of(pb_ref, 6))
        out.ref[rows] = (n * row_of(gain_ref, 2) + row_of(shift_ref, 2)).astype(BF16)
        position = shard * length + r + lax.broadcasted_iota(jnp.int32, (RT, 1), 0)
        g = jnp.where(position < rng[VALID], cot_ref[rows].astype(F32), 0.0)
        dg2 += jnp.sum(g * n, axis=0, keepdims=True)
        ds2 += jnp.sum(g, axis=0, keepdims=True)
        dh3 = norm_rows_back(g, n, spread, row_of(gain_ref, 2))
        dy3 = dh3.astype(BF16)
        db6 += jnp.sum(dy3.astype(F32), axis=0, keepdims=True)
        dy_scr[rows] = dy3
        y_scr[rows] = dh3
    out.send()

    parts = width // 128

    def contract(c, carry):
        cols = pl.ds(pl.multiple_of(c * width, width), width)
        dus = []
        for t in range(0, width, 256):
            half_cols = pl.ds(pl.multiple_of(c * width + t, 256), 256)
            du = (gp[c, :, t : t + 256] * dot(dy_scr[...], w2_ref[half_cols, :], NT)).astype(BF16)
            deb.ref[0:1, half_cols] = jnp.sum(du.astype(F32), axis=0, keepdims=True)
            dus.append(du)
        du = jnp.concatenate(dus, axis=1)
        y_scr[...] += dot(du, w1_ref[:, cols], NT)
        g1 = dot(a2t[...], du)
        for j in range(parts):
            put_block(
                keep.ref, send.ref, c ^ shard, slice(inner + j * width, inner + (j + 1) * width),
                g1[:, j * 128 : (j + 1) * 128].astype(BF16),
            )
        g2 = dot(act[c], dy_scr[...], TN)
        at = pl.ds(pl.multiple_of(c * width, width), width)
        for b in range(4):
            put_block(
                keep.ref, send.ref, shard ^ b, at, g2[:, b * 128 : (b + 1) * 128].astype(BF16)
            )
        return carry

    lax.fori_loop(0, chunks, contract, 0)
    for r in range(0, length, RT):
        rows = slice(r, r + RT)
        up = y_scr[rows]
        n = n1[rows]
        dg1 += jnp.sum(up * n, axis=0, keepdims=True)
        ds1 += jnp.sum(up, axis=0, keepdims=True)
        dh2 = norm_rows_back(up, n, r1[rows, 0:1], row_of(gain_ref, 1))
        dh.ref[rows] = dh2
        dy2 = dh2.astype(BF16)
        dy_scr[rows] = dy2
        db5 += jnp.sum(dy2.astype(F32), axis=0, keepdims=True)
        do.ref[rows] = dot(dy2, wout_ref[...], NT).astype(BF16)
    dh.send()
    do.send()
    g3 = dot(o.ref[...], dy_scr[...], TN)
    for b in range(4):
        put_block(
            keep.ref, send.ref, shard ^ b, slice(2 * inner, 2 * inner + width),
            g3[:, b * 128 : (b + 1) * 128].astype(BF16),
        )
    for i, value in enumerate((db5, db6, dg1, dg2, ds1, ds2)):
        small.ref[i : i + 1, :] = value
    small.ref[6:8, :] = jnp.zeros((2, width), F32)


def cross_forward(rng, parts, fq, fkt, q, a1, cot, wkv, wout, w1, w2, eb, pb, gain, shift):
    length, width = q.shape
    full, inner = len(parts) * length, w1.shape[1]
    return call(
        cross_body,
        rng,
        [wkv, pb, *parts, q, fq, fkt, wout, a1, gain, shift, w1, w2, eb, cot],
        [
            ((full, width), BF16), ((full, width), BF16), ((length, width), BF16),
            ((width // 128, length, 128), F32), ((length, width), BF16), ((length, width), BF16),
            ((length, width), F32), ((2, 2 * inner + width, 128), BF16),
            ((2, 2 * inner + width, 128), BF16), ((1, inner), F32),
            ((8, width), F32), ((width, full), BF16),
        ],
        attend_scratch(length, full)
        + [
            ((width, full), BF16),
            ((length, width), F32), ((length, 128), F32), ((length, width), F32), ((length, width), BF16),
            ((width, length), BF16), ((inner // width, length, width), BF16), ((inner // width, length, width), F32),
            ((length, width), F32), ((length, width), BF16),
        ],
        flops=10**7,
        vmem=60,
        loose=parts[1:],
        early=6,
    )


def back_body(rng, held, results, qh, doh, qm, dom, dq_scr, w_scr, c_scr, *, causal, pack, pairs):
    first, second, shared = held[:8], held[8 : 6 * pairs + 2], held[6 * pairs + 2 :]
    xq, xt = shared[:2]
    fq, fk = held[1], held[7]
    shard = rng[SHARD]
    groups = [(held[0], held[2], held[3], held[4], held[5], held[6])]
    if pairs == 2:
        groups.append(tuple(second))
    for i, (q, lse, do, o, k, v) in enumerate(groups):
        dq_out, dkv, w, small = results[4 * i : 4 * i + 4]
        length = q.ref.shape[0]
        dkv.ref[...] = jnp.zeros_like(dkv.ref)
        own = [x.get() for x in (q, fq, lse, do, o)]
        start_all(held)
        dq = attend_back(rng, *own, (k, v, fk), dkv.ref, qh, doh, qm, dom, dq_scr, causal).astype(BF16)
        dkv.send()
        dq_out.ref[...] = dq
        dq_out.send()
        w.ref[0] = dot(xq.get()[...], dq).astype(BF16)
        w_scr[...] = jnp.zeros_like(w_scr)
        c_scr[...] = jnp.zeros_like(c_scr)
        xt_ref = xt.get()
        for m in range(xt_ref.shape[1] // length):

            def more(m=m):
                span = slice(m * length, (m + 1) * length)
                part = dkv.ref[span, :]
                w_scr[...] += dot(xt_ref[:, span], part)
                c_scr[...] += jnp.sum(part[:, 128:].astype(F32), axis=0, keepdims=True)

            if causal and m:
                pl.when((shard ^ m) < shard)(more)
            else:
                more()
        w.ref[1] = w_scr[:, :128].astype(BF16)
        w.ref[2] = w_scr[:, 128:].astype(BF16)
        small.ref[0:1, :] = jnp.sum(dq.astype(F32), axis=0, keepdims=True)
        small.ref[1:2, :] = c_scr[0:1]
        small.ref[2:8, :] = jnp.zeros((6, 128), F32)
        w.send()
    if pack is not None:
        dkvs = [results[4 * i + 1].ref for i in range(pairs)]
        pack(shard, [x.get() for x in shared[2:]], w.ref, small.ref, dkvs, results[-2].ref, results[-1].ref)


def pack_memory(shard, others, w, small, dkv, keep, send):
    for m in (1, 3, 0, 2):
        spread_block([*others[1:], *dkv], others[0], 0, m, (keep, send)[m % 2])


def pack_early(shard, others, w, small, dkv, keep, send):
    w0, w1 = others
    width = w.shape[1]
    for b, columns in enumerate(((w0[0], w1[0]), (w0[1], w1[1]), (w[1], w0[2]), (w1[2], w[2]))):
        for at, value in enumerate(columns):
            put_far(keep, send, shard ^ b, slice(at * width, (at + 1) * width), value)


def pack_late(shard, others, w, small, dkv, keep, send):
    w2, a0, a1, a2, b0, b1, b2, b3, s0_ref, s2_ref, deb_ref = others
    width = w.shape[1]
    own, other = (a0, a1, a2, small), (b0, b1, b2, b3)
    for b, value in enumerate((w2[0], w[0], w[1], w[2])):
        put_block(keep, send, shard ^ b, slice(0, width), value)
    pad = keep.shape[1] - width
    for b in range(4):
        cols = slice(b * 128, (b + 1) * 128)
        rows = [deb_ref[0:1, b * width + j * 128 : b * width + (j + 1) * 128] for j in range(width // 128)]
        rows += [own[b][0:1], own[b][1:2], s0_ref[0:1, cols], other[b][0:1], other[b][1:2]]
        rows += [s2_ref[0:1, cols], s2_ref[1:2, cols]]
        rows += [s0_ref[1:2, cols], s2_ref[2:3, cols], s2_ref[3:4, cols]]
        rows += [s0_ref[2:3, cols], s2_ref[4:5, cols], s2_ref[5:6, cols]]
        rows.append(jnp.zeros((pad - len(rows), 128), F32))
        put_block(
            keep, send, shard ^ b, slice(width, width + pad), jnp.concatenate(rows, axis=0).astype(BF16)
        )


def attend_backward(rng, pairs, q, fq, lse, do, o, fk, k, v, xq, xt, causal, pack=None, extra=(), packed=None):
    length, width = q.shape
    full = k.shape[0]
    ins, outs = [], []
    for i, p in enumerate(pairs):
        cut = pl.ds(p * 128, 128)
        if i == 0:
            ins += [(q, cut), fq, (lse, p), (do, cut), (o, cut), (k, cut), (v, cut), fk]
        else:
            ins += [(q, cut), (lse, p), (do, cut), (o, cut), (k, cut), (v, cut)]
        outs += [((length, 128), BF16), ((full, 256), BF16), ((3, width, 128), BF16), ((8, 128), F32)]
    if pack is not None:
        outs += [(packed, BF16)] * 2
    out = call(
        functools.partial(back_body, causal=causal, pack=pack, pairs=len(pairs)),
        rng,
        [*ins, (xq, pl.ds(0, length)), xt, *extra],
        outs,
        [((2, 128, length), BF16)] * 2
        + [((2, length, 128), BF16)] * 2
        + [((128, length), F32), ((width, 256), F32), ((8, 128), F32)],
        flops=10**7,
        vmem=40,
        early=8,
    )
    return [out[4 * i : 4 * i + 4] for i in range(len(pairs))] + [out[4 * len(pairs) :]]


def middle_body(rng, held, results, dy_scr):
    dq0, dq1, dq2, dq3, wq, dh2, n0, r0, gain, wout, o, u0, u1, u2, u3 = held
    dh, do, keep, send, small = results
    length, width = dh2.ref.shape
    pairs = width // 128
    shard = rng[SHARD]
    zero = jnp.zeros((1, width), F32)
    db2, dg0, ds0 = zero, zero, zero
    dq_refs = [x.get() for x in (dq0, dq1, dq2, dq3)]
    wq_ref, dh2_ref, n_ref, r_ref, gain_ref, wout_ref = (x.get() for x in (wq, dh2, n0, r0, gain, wout))
    start_all(held)
    for r in range(0, length, RT):
        rows = slice(r, r + RT)
        up = dh2_ref[rows] + dot(jnp.concatenate([d[rows] for d in dq_refs], axis=1), wq_ref[...], NT)
        n = n_ref[rows]
        dg0 += jnp.sum(up * n, axis=0, keepdims=True)
        ds0 += jnp.sum(up, axis=0, keepdims=True)
        new = norm_rows_back(up, n, r_ref[rows, 0:1], row_of(gain_ref, 0))
        dh.ref[rows] = new
        dy = new.astype(BF16)
        dy_scr[rows] = dy
        db2 += jnp.sum(dy.astype(F32), axis=0, keepdims=True)
        do.ref[rows] = dot(dy, wout_ref[...], NT).astype(BF16)
    dh.send()
    do.send()
    start_all(held)
    g = dot(o.get()[...], dy_scr[...], TN)
    for b in range(4):
        put_block(keep.ref, send.ref, shard ^ b, slice(0, width), g[:, b * 128 : (b + 1) * 128].astype(BF16))
    units = [x.get() for x in (u0, u1, u2, u3)]
    for b in range(4):
        put_block(keep.ref, send.ref, shard ^ b, slice(width, 2 * width), units[b][0])
    for i in range(2 * pairs):
        b, at = i // 2, 2 + i % 2
        put_block(
            keep.ref, send.ref, shard ^ b, slice(at * width, (at + 1) * width), units[i % pairs][1 + i // pairs]
        )
    for i, value in enumerate((db2, dg0, ds0)):
        small.ref[i : i + 1, :] = value
    small.ref[3:8, :] = jnp.zeros((5, width), F32)


def middle(rng, dqs, units, dh2, n, r, o, wq, wout, gain):
    length, width = dh2.shape
    return call(
        middle_body,
        rng,
        [*dqs, wq, dh2, n, r, gain, wout, o, *units],
        [
            ((length, width), F32), ((length, width), BF16), ((2, 4 * width, 128), BF16),
            ((2, 4 * width, 128), BF16), ((8, width), F32),
        ],
        [((length, width), BF16)],
        flops=10**7,
        early=10,
    )


def spread_block(parts, w_ref, offset, m, ref):
    length, width = ref.shape[1:]
    rows = slice(m * length, (m + 1) * length)
    dk = jnp.concatenate([d[rows, :128] for d in parts], axis=1)
    dv = jnp.concatenate([d[rows, 128:] for d in parts], axis=1)
    for c in range(0, width, 256):
        cols = slice(c, c + 256)
        total = dot(dk, w_ref[cols, offset : offset + width], NT)
        total += dot(dv, w_ref[cols, offset + width : offset + 2 * width], NT)
        ref[m // 2, :, cols] = total.astype(BF16)


def spread_body(rng, held, results, *, causal, offset):
    keep, send = results
    shard = rng[SHARD]
    refs = [x.get() for x in held]
    w_ref, parts = refs[0], refs[1:]
    for m in (1, 3, 0, 2):
        ref = (keep.ref, send.ref)[m % 2]

        def fill(m=m, ref=ref):
            spread_block(parts, w_ref, offset, m, ref)

        def clear(m=m, ref=ref):
            ref[m // 2] = jnp.zeros_like(ref[m // 2])

        if causal and m:
            pl.when((shard ^ m) < shard)(fill)
            pl.when((shard ^ m) > shard)(clear)
        else:
            fill()
        if m == 3:
            send.send()


def spread_keys(rng, dkvs, w, length, causal, offset):
    width = w.shape[0]
    return call(
        functools.partial(spread_body, causal=causal, offset=offset),
        rng,
        [w, *dkvs],
        [((2, length, width), BF16), ((2, length, width), BF16)],
        [],
        flops=10**7,
    )


def partial_body(rng, held, results):
    wq, dq0, dq1, dq2, dq3, dh, near, got = held
    total = results[0].ref
    width = total.shape[1]
    dq = jnp.concatenate([x.get()[...] for x in (dq0, dq1, dq2, dq3)], axis=1)
    wq_ref, dh_ref, near_ref, got_ref = (x.get() for x in (wq, dh, near, got))
    for c in range(0, width, 256):
        cols = slice(c, c + 256)
        total[:, cols] = (
            dh_ref[:, cols]
            + dot(dq, wq_ref[cols, :], NT)
            + (near_ref[:, cols].astype(F32) + got_ref[:, cols].astype(F32))
        )


def target_partial(rng, win, dqs, dh, near, got):
    length, width = dh.shape
    return call(
        partial_body,
        rng,
        [(win, pl.ds(0, width)), *dqs, dh, (near, 0), (got, 0)],
        [((length, width), F32)],
        [],
        flops=20 * 10**9,
        loose=[got],
    )[0]


def outputs_body(rng, held, results):
    part, far_t, near, got, far_m, sums = held
    target_grad, memory_grad, expand, reduce, outproj = results
    part_ref, far_ref = part.get(), far_t.get()
    target_grad.ref[...] = part_ref[...] + far_ref[...].astype(F32)
    target_grad.send()
    near_ref, got_ref, far_ref = near.get(), got.get(), far_m.get()
    memory_grad.ref[...] = near_ref[...].astype(F32) + got_ref[...].astype(F32) + far_ref[...].astype(F32)
    memory_grad.send()
    sums_ref = sums.get()
    inner = reduce.ref.shape[0]
    width = expand.ref.shape[0]
    reduce.ref[...] = sums_ref[0:inner].astype(F32)
    reduce.send()
    for j in range(expand.ref.shape[1] // 128):
        rows = slice(inner + j * width, inner + (j + 1) * width)
        expand.ref[:, j * 128 : (j + 1) * 128] = sums_ref[rows].astype(F32)
    expand.send()
    outproj.ref[...] = sums_ref[2 * inner : 2 * inner + width].astype(F32)


def first_outputs(rng, part, far_t, near, got, far_m, sums, inner, shards):
    length, width = part.shape
    return call(
        outputs_body,
        rng,
        [part, far_t, (near, 0), (got, 0), far_m, sums],
        [
            ((length, width), F32), ((length, width), F32), ((width, inner // shards), F32), ((inner, 128), F32),
            ((width, 128), F32),
        ],
        [],
        flops=20 * 10**9,
        loose=[far_t, got, far_m, sums],
    )


def finish_body(rng, held, results):
    sums = held[1].get()
    w, outproj, query, keyval, eb, pb, gain, shift = (r.ref for r in results)
    width = w.shape[0]
    shard = rng[SHARD]
    outproj[...] = sums[0:width].astype(F32)
    query[...] = sums[width : 2 * width].astype(F32)
    for j in range(keyval.shape[1] // 128):
        keyval[:, j * 128 : (j + 1) * 128] = sums[(2 + j) * width : (3 + j) * width].astype(F32)
    for x in results[1:4]:
        x.send()
    total = held[0].get()
    second = jnp.where(shard == 1, 0, jnp.where(shard == 2, 2, 1))
    third = jnp.where((shard == 1) | (shard == 2), 1, 2)
    for j, at in enumerate((jnp.where(shard == 1, 2, 0), second, third)):
        rows = pl.ds(pl.multiple_of(at * width, width), width)
        w[:, j * 128 : (j + 1) * 128] = total[rows].astype(F32)
    results[0].send()
    rest = total[3 * width : 3 * width + 32].astype(F32)
    for j in range(width // 128):
        eb[0:1, j * 128 : (j + 1) * 128] = rest[j : j + 1]
    pb[...] = rest[4:11]
    gain[...] = rest[11:14]
    shift[...] = rest[14:17]


def finish(rng, total, sums, width):
    return call(
        finish_body,
        rng,
        [total, sums],
        [
            ((width, 384), F32), ((width, 128), F32), ((width, 128), F32), ((width, 256), F32), ((1, width), F32),
            ((7, 128), F32), ((3, 128), F32), ((3, 128), F32),
        ],
        [],
        loose=[total, sums],
    )


def partner(x, axis, mask):
    n = lax.axis_size(axis)
    return lax.ppermute(x, axis, [(i, i ^ mask) for i in range(n)])


def add(a, b):
    return (a.astype(F32) + b.astype(F32)).astype(BF16)


def after(x, *deps):
    return lax.optimization_barrier((x, *deps))[0]


def half_of(x, bit):
    half = x.shape[0] // 2
    return lax.dynamic_slice_in_dim(x, bit * half, half, 0)


def dp_bit(j):
    return (lax.axis_index("dp") >> j) & 1


class Flow:
    def __init__(self, keep, send):
        bits = lax.axis_size("dp").bit_length() - 1
        self.steps = [("core", 0), ("chip", 0)]
        self.steps += [("fold", j) for j in range(bits)]
        self.steps += [("join", j) for j in reversed(range(bits))]
        self.keep, self.out, self.cur, self.got = keep, send, None, None

    def done(self):
        return not self.steps

    def begin(self):
        if self.done():
            return
        kind, j = self.steps[0]
        if kind == "core":
            self.got = partner(self.out, "seq", 1)
        elif kind == "chip":
            self.got = partner(self.out, "seq", 2)
        elif kind == "fold":
            self.got = partner(half_of(self.cur, 1 - dp_bit(j)), "dp", 1 << j)
        else:
            self.got = partner(self.cur, "dp", 1 << j)

    def end(self, *deps):
        if self.done():
            return
        kind, j = self.steps.pop(0)
        got = after(self.got, *deps) if deps else self.got
        if kind == "core":
            self.out = add(self.keep[1], got[1])
            self.cur = add(self.keep[0], got[0])
        elif kind == "chip":
            self.cur = add(self.cur, got)
        elif kind == "fold":
            self.cur = add(half_of(self.cur, dp_bit(j)), got)
        else:
            low = dp_bit(j) == 0
            self.cur = jnp.where(low, jnp.concatenate([self.cur, got]), jnp.concatenate([got, self.cur]))

    def state(self):
        return self.out if self.steps and self.steps[0][0] == "chip" else self.cur


class SplitFlow:
    def __init__(self, keep, got):
        half = keep.shape[1] // 2
        low, high = keep[:, :half], keep[:, half:]
        got_low, got_high = got[:, :half], got[:, half:]
        self.near, self.far = add(low[0], got_low[0]), add(low[1], got_low[1])
        self.two = add(high, got_high)
        bits = lax.axis_size("dp").bit_length() - 1
        self.steps = ["cross", "back"] + [("fold", j) for j in range(1, bits)]
        self.steps += [("join", j) for j in reversed(range(1, bits))] + ["last"]
        self.cur = self.got = None

    def done(self):
        return not self.steps

    def begin(self):
        if self.done():
            return
        step = self.steps[0]
        if step == "cross":
            rows = self.two.shape[1] // 2
            bit = dp_bit(0)
            self.mine = lax.dynamic_slice_in_dim(self.two, bit * rows, rows, 1)
            self.other = lax.dynamic_slice_in_dim(self.two, (1 - bit) * rows, rows, 1)
            self.got = (partner(self.far, "seq", 2), partner(self.other, "dp", 1))
        elif step == "back":
            self.got = (partner(half_of(self.low, 1 - dp_bit(0)), "dp", 1), partner(self.high[1], "seq", 2))
        elif step == "last":
            self.got = partner(self.cur, "dp", 1)
        elif step[0] == "fold":
            self.got = partner(half_of(self.cur, 1 - dp_bit(step[1])), "dp", 1 << step[1])
        else:
            self.got = partner(self.cur, "dp", 1 << step[1])

    def end(self, *deps):
        if self.done():
            return
        step = self.steps.pop(0)
        if step in ("cross", "back"):
            one, two = after(self.got[0], *deps), after(self.got[1], *deps)
        else:
            got = after(self.got, *deps)
        if step == "cross":
            self.low = add(self.near, one)
            self.high = add(self.mine, two)
        elif step == "back":
            self.cur = jnp.concatenate([add(half_of(self.low, dp_bit(0)), one), add(self.high[0], two)])
        elif step == "last":
            low = dp_bit(0) == 0
            a, b = jnp.where(low, self.cur, got), jnp.where(low, got, self.cur)
            half = a.shape[0] // 2
            self.cur = jnp.concatenate([a[:half], b[:half], a[half:], b[half:]])
        elif step[0] == "fold":
            self.cur = add(half_of(self.cur, dp_bit(step[1])), got)
        else:
            low = dp_bit(step[1]) == 0
            self.cur = jnp.where(low, jnp.concatenate([self.cur, got]), jnp.concatenate([got, self.cur]))

    def state(self):
        if self.cur is not None:
            return (self.cur,)
        return (self.far, self.other) if self.steps[0] == "cross" else (self.low, self.high)


def local(
    target, memory, cotangent, target_segments, source_segments, target_lengths, source_lengths,
    self_inproj, self_outproj, cross_query, cross_keyval, cross_outproj, ffn_expand, ffn_reduce,
    expand_bias, proj_bias, norm_gain, norm_shift,
):
    target, memory, cotangent = target[0], memory[0], cotangent[0]
    length, width = target.shape
    shards = lax.axis_size("seq")
    shard = lax.axis_index("seq").astype(jnp.int32)
    unit = 16 * lax.axis_size("dp")

    t2 = partner(target, "seq", 2)
    t1 = partner(target, "seq", 1)
    m1 = partner(memory, "seq", 1)
    self_rng, cross_rng, fq, self_fk, cross_fk, self_fkt, cross_fkt = prepare(
        shard, target_lengths, source_lengths, target_segments, source_segments, length
    )
    t2 = after(t2, self_rng)
    t3 = partner(t2, "seq", 1)
    m2 = partner(after(memory, t2), "seq", 2)
    target_parts = [target, t1, t2, t3]

    q1, k1, v1, o1, lse1, a1, n0, r0, q2, target_t, a1_t = self_forward(
        self_rng, target_parts, fq, self_fkt, self_inproj, self_outproj, cross_query, proj_bias,
        norm_gain, norm_shift,
    )
    m2 = after(m2, q2)
    memory_parts = [memory, m1, m2, partner(m2, "seq", 1)]
    k2, v2, o2, lse2, layer_out, do2, dh2, keep_a, send_a, deb, small2, memory_t = cross_forward(
        cross_rng, memory_parts, fq, cross_fkt, q2, a1, cotangent, cross_keyval, cross_outproj,
        ffn_expand, ffn_reduce, expand_bias, proj_bias, norm_gain, norm_shift,
    )
    got_a = partner(send_a, "seq", 1)

    def cross_back(pairs, *deps, **pack):
        rng = after(cross_rng, *deps) if deps else cross_rng
        return attend_backward(
            rng, pairs, q2, fq, lse2, do2, o2, cross_fk, k2, v2, a1_t, memory_t, False, **pack
        )

    def self_back(p, *deps, **pack):
        rng = after(self_rng, *deps) if deps else self_rng
        return attend_backward(
            rng, [p], q1, fq, lse1, do1, o1, self_fk, k1, v1, target_t, target_t, True, **pack
        )

    c0, c1, _ = cross_back([0, 1])
    got_a = after(got_a, c1[0])
    flow_a = SplitFlow(keep_a, got_a)
    flow_a.begin()
    c2, c3, (mem_keep, mem_send) = cross_back(
        [2, 3], c1[0], *flow_a.state(), pack=pack_memory, extra=(cross_keyval, c0[1], c1[1]),
        packed=(2, length, width),
    )
    cross = (c0, c1, c2, c3)
    mem_got = partner(mem_send, "seq", 1)
    flow_a.end(c3[0])
    flow_a.begin()
    dh1, do1, keep_b, send_b, small0 = middle(
        after(self_rng, *flow_a.state(), c3[0]), [c[0] for c in cross], [c[2] for c in cross], dh2, n0, r0, o1,
        cross_query, self_outproj, norm_gain,
    )
    mem_far = add(mem_keep[1], after(mem_got, do1)[1])
    mem_get = partner(mem_far, "seq", 2)
    flow_b = Flow(keep_b, send_b)
    flow_b.begin()
    s0 = self_back(0, do1, mem_far)[0]
    flow_a.end(s0[0])
    flow_b.end(s0[0])
    flow_a.begin()
    flow_b.begin()
    s1 = self_back(1, *flow_a.state(), flow_b.state(), s0[0])[0]
    flow_a.end(s1[0])
    flow_b.end(s1[0])
    flow_a.begin()
    flow_b.begin()
    s2, (keep_c, send_c) = self_back(
        2, *flow_a.state(), flow_b.state(), s1[0], pack=pack_early, extra=(s0[2], s1[2]), packed=(2, 2 * width, 128)
    )
    got_c = partner(send_c, "seq", 2)
    flow_a.end(s2[0])
    flow_b.end(s2[0])
    flow_a.begin()
    flow_b.begin()
    s3, (keep_d, send_d) = self_back(
        3, *flow_a.state(), flow_b.state(), s2[0], pack=pack_late,
        extra=(s2[2], s0[3], s1[3], s2[3], c0[3], c1[3], c2[3], c3[3], small0, small2, deb),
        packed=(2, width + unit, 128),
    )
    selfs = (s0, s1, s2, s3)
    got_d = partner(send_d, "seq", 1)
    two_c = add(keep_c, after(got_c, s3[0]))
    core_c = partner(two_c[1], "seq", 1)
    flow_a.end(s3[0])
    flow_b.end(s3[0])
    flow_a.begin()
    flow_b.begin()
    far_d, near_d = add(keep_d[1], got_d[1]), add(keep_d[0], got_d[0])
    get_d = partner(far_d, "seq", 2)
    tgt_keep, tgt_send = spread_keys(
        after(self_rng, far_d, two_c, *flow_a.state(), flow_b.state()), [s[1] for s in selfs], self_inproj,
        length, True, width,
    )
    get_d, core_c = after(get_d, tgt_keep), after(core_c, tgt_keep)
    tgt_got = partner(tgt_send, "seq", 1)
    flow_a.end(tgt_keep)
    flow_b.end(tgt_keep)
    flow_a.begin()
    flow_b.begin()
    block = jnp.concatenate([add(two_c[0], core_c), add(near_d, get_d)])
    tgt_got = after(tgt_got, block)
    tgt_far = add(tgt_keep[1], tgt_got[1])
    tgt_get = partner(tgt_far, "seq", 2)
    block = after(block, tgt_far, *flow_a.state(), flow_b.state())
    devices = lax.axis_size("dp")
    parts = lax.all_to_all(block.reshape(devices, -1, 128), "dp", 0, 0, tiled=True)
    partial = target_partial(
        after(self_rng, block), self_inproj, [s[0] for s in selfs], dh1, tgt_keep, tgt_got
    )
    flow_b.end(partial)
    flow_b.begin()
    parts = after(parts, partial, flow_b.state(), tgt_get)
    part = jnp.sum(parts.astype(F32), axis=0).astype(BF16)
    flow_b.end(part)
    flow_b.begin()
    spread_part = after(jnp.broadcast_to(part[None], parts.shape), flow_b.state())
    whole = lax.all_to_all(spread_part, "dp", 0, 0, tiled=True).reshape(-1, 128)
    flow_a.end(part)
    while not flow_a.done():
        flow_a.begin()
        flow_a.end()
    target_grad, memory_grad, expand_grad, reduce_grad, outproj_grad = first_outputs(
        after(self_rng, spread_part), partial, tgt_get, mem_keep, mem_got, mem_get, flow_a.cur,
        ffn_expand.shape[1], shards,
    )
    flow_b.end(target_grad)
    while not flow_b.done():
        flow_b.begin()
        flow_b.end()
    self_in, self_out_grad, query_grad, keyval_grad, eb_grad, pb_grad, gain_grad, shift_grad = finish(
        self_rng, after(whole, target_grad), flow_b.cur, width
    )
    return (
        layer_out[None],
        target_grad[None],
        memory_grad[None],
        self_in,
        self_out_grad,
        query_grad,
        keyval_grad,
        outproj_grad,
        expand_grad,
        reduce_grad,
        eb_grad,
        pb_grad,
        gain_grad,
        shift_grad,
    )


def solution(mesh):
    rows, shard = P("dp", "seq", None), P(None, "seq")
    in_specs = (rows, rows, rows, P("dp", None), P("dp", None), P("dp"), P("dp")) + (P(),) * 11
    out_specs = (rows, rows, rows) + (shard,) * 11
    return jax.shard_map(local, mesh=mesh, in_specs=in_specs, out_specs=out_specs, check_vma=False)
```

```python
import functools
import jax
import jax.numpy as jnp
from jax import lax
from jax.experimental import pallas as pl
from jax.experimental.pallas import tpu as pltpu
from jax.sharding import PartitionSpec as P

BF16 = jnp.bfloat16
F32 = jnp.float32
EPSILON = 1e-05
BK = 256
RT = 256
NT = (((1,), (1,)), ((), ()))
NN = (((1,), (0,)), ((), ()))
TN = (((0,), (0,)), ((), ()))


def dot(a, b, dims=NN):
    return lax.dot_general(a, b, dims, preferred_element_type=F32)


class Held:
    def __init__(self, copy, ref):
        self.copy, self.ref, self.started, self.waited = copy, ref, False, False

    def start(self):
        if not self.started:
            self.copy.start()
            self.started = True

    def get(self):
        self.start()
        if not self.waited:
            self.copy.wait()
            self.waited = True
        return self.ref


class Result:
    def __init__(self, copy, ref, both=None):
        self.copy, self.ref, self.both, self.started = copy, ref, both, False

    def send(self):
        self.copy.start()
        self.started = True


def call(body, rng, ins, outs, scratch, flops=10**7, vmem=24, loose=(), early=None):
    arrays, columns = [], []
    for x in ins:
        x, cut = x if isinstance(x, tuple) else (x, None)
        arrays.append(x)
        columns.append(cut)
    shapes = []
    for x, cut in zip(arrays, columns):
        if cut is None:
            shapes.append(x.shape)
        else:
            shapes.append(x.shape[1:] if isinstance(cut, int) else x.shape[:-1] + (cut.size,))
    pairs = [len(out) == 3 for out in outs]
    buffers = [((2, *out[0]) if pair else out[0], out[1]) for out, pair in zip(outs, pairs)]
    outs = [out[:2] for out, pair in zip(outs, pairs) for _ in range(1 + pair)]
    n_in, n_out, n_buf, n_scr = len(ins), len(outs), len(buffers), len(scratch)

    def kernel(rng_ref, *refs):
        hbm_in, refs = refs[:n_in], refs[n_in:]
        hbm_out, refs = refs[:n_out], refs[n_out:]
        vm_in, refs = refs[:n_in], refs[n_in:]
        vm_buf, refs = refs[:n_buf], refs[n_buf:]
        scr, refs = refs[:n_scr], refs[n_scr:]
        sem_in, sem_out = refs
        held = []
        for i, (src, dst, cut) in enumerate(zip(hbm_in, vm_in, columns)):
            if isinstance(cut, int):
                src = src.at[cut]
            elif cut is not None:
                src = src.at[(slice(None),) * (len(src.shape) - 1) + (cut,)]
            held.append(Held(pltpu.make_async_copy(src, dst, sem_in.at[i]), dst))
        for x in held[:early]:
            x.start()
        parts = []
        for ref, pair in zip(vm_buf, pairs):
            parts += [(ref.at[0], ref), (ref.at[1], ref)] if pair else [(ref, None)]
        results = [
            Result(pltpu.make_async_copy(src, dst, sem_out.at[i]), src, both)
            for i, ((src, both), dst) in enumerate(zip(parts, hbm_out))
        ]
        body(rng_ref, held, results, *scr)
        for x in held:
            x.get()
        for x in results:
            if not x.started:
                x.send()
        for x in results:
            x.copy.wait()

    hbm = pl.BlockSpec(memory_space=pltpu.HBM)
    return pl.pallas_call(
        kernel,
        out_shape=tuple(pltpu.HBM(s, d) for s, d in outs),
        in_specs=[pl.BlockSpec(memory_space=pltpu.SMEM)] + [hbm] * n_in,
        out_specs=(hbm,) * n_out,
        scratch_shapes=[pltpu.VMEM(s, x.dtype) for s, x in zip(shapes, arrays)]
        + [pltpu.VMEM(s, d) for s, d in buffers]
        + [pltpu.VMEM(s, d) for s, d in scratch]
        + [pltpu.SemaphoreType.DMA((n_in,)), pltpu.SemaphoreType.DMA((n_out,))],
        compiler_params=pltpu.CompilerParams(vmem_limit_bytes=vmem * 2**20),
        cost_estimate=pl.CostEstimate(flops=flops, bytes_accessed=2**20, transcendentals=0),
    )(
        rng,
        *[
            x if any(x is y for y in loose) else pltpu.with_memory_space_constraint(x, pltpu.HBM)
            for x in arrays
        ],
    )


LO0, HI0, LO1, HI1, SHARD, VALID = range(6)


def prepare_body(
    info, lengths, t_smem, t_ref, s_ref, self_rng, cross_rng, fq_ref, self_fk, cross_fk, self_fkt, cross_fkt
):
    length = fq_ref.shape[0]
    shard = info[0]
    valid, count = lengths[0], lengths[1]
    full = t_ref.shape[1]
    t_row, s_row = t_ref[...], s_ref[...]

    def number(mask):
        return jnp.sum(jnp.where(mask, 1.0, 0.0)).astype(jnp.int32)

    for half in range(2):
        first = t_smem[0, shard * length + half * RT]
        last = t_smem[0, shard * length + half * RT + RT - 1]
        self_rng[LO0 + 2 * half] = lax.div(number(t_row < first), BK)
        self_rng[HI0 + 2 * half] = 0
        cross_rng[LO0 + 2 * half] = lax.div(number(s_row < first), BK)
        end = jnp.minimum(number(s_row <= last), count)
        cross_rng[HI0 + 2 * half] = lax.div(end + BK - 1, BK)
    for ref in (self_rng, cross_rng):
        ref[SHARD] = shard
        ref[VALID] = valid
        ref[6] = 0
        ref[7] = 0
    f = lax.broadcasted_iota(jnp.int32, (128, 128), 1) % 64

    def column(ref, at):
        return jnp.broadcast_to(ref[0:1, pl.ds(pl.multiple_of(at, 128), 128)], (128, 128)).T

    row = lax.broadcasted_iota(jnp.int32, (128, 128), 0)
    for m in range(full // length):
        for t in range(0, length, 128):
            at = (shard ^ m) * length + t
            for ref, total, out, out_t in ((t_ref, valid, self_fk, self_fkt), (s_ref, count, cross_fk, cross_fkt)):
                seg = column(ref, at)
                seen = (seg == f) & (row + at < total)
                feature = jnp.where(
                    f < 8, jnp.where(seen, 0.0, -1e30), jnp.where(f < 11, 1.0, 0.0)
                )
                out[m * length + t : m * length + t + 128] = feature.astype(BF16)
                out_t[:, m * length + t : m * length + t + 128] = feature.astype(BF16).T[0:64]
                if m == 0 and out is self_fk:
                    fq_ref[t : t + 128] = jnp.where(seg == f, 1.0, 0.0).astype(BF16)


def prepare(shard, target_length, source_length, target_segments, source_segments, length):
    full = target_segments.shape[1]
    sd = jax.ShapeDtypeStruct
    smem, vm = pl.BlockSpec(memory_space=pltpu.SMEM), pl.BlockSpec(memory_space=pltpu.VMEM)
    return pl.pallas_call(
        prepare_body,
        out_shape=(
            sd((8,), jnp.int32), sd((8,), jnp.int32), sd((length, 128), BF16), sd((full, 128), BF16),
            sd((full, 128), BF16), sd((64, full), BF16), sd((64, full), BF16),
        ),
        in_specs=[smem, smem, smem, vm, vm],
        out_specs=(smem, smem, vm, vm, vm, vm, vm),
    )(
        shard.reshape(1), jnp.concatenate([target_length, source_length]), target_segments,
        target_segments, source_segments,
    )


def start_all(held):
    for x in held:
        x.start()


def half_masks():
    lane = lax.broadcasted_iota(jnp.int32, (1, 128), 1)
    return (lane < 64, lane >= 64), lane % 64


def relative_offset(block, shard, per_shard):
    owner = lax.div(block, per_shard)
    return pl.multiple_of(((owner ^ shard) * per_shard + lax.rem(block, per_shard)) * BK, BK)


def triangle(transposed):
    a = lax.broadcasted_iota(jnp.int32, (BK, BK), 0)
    b = lax.broadcasted_iota(jnp.int32, (BK, BK), 1)
    return a <= b if transposed else b <= a


def attend(rng, q_ref, fq_ref, kt, v_ref, fkt_ref, o_ref, lse_ref, qh, s_even, s_odd, mx_even, mx_odd, acc, causal):
    length, width = q_ref.shape
    per = length // BK
    pairs = width // 128
    shard = rng[SHARD]
    conds, _ = half_masks()
    lo0, hi0, lo1, hi1 = rng[LO0], rng[HI0], rng[LO1], rng[HI1]
    both, upper, lower = slice(0, length), slice(0, RT), slice(RT, length)
    s_bank, mx_bank = (s_even, s_odd), (mx_even, mx_odd)

    def scores(g, off, slot, rows, diagonal):
        s_scr, mx = s_bank[g % 2], mx_bank[g % 2]
        mask = fkt_ref[0:64, pl.ds(off, BK)]
        for h in range(2):
            at = g * 128 + 64 * h
            mine = kt[at : at + 64, pl.ds(off, BK)]
            w = jnp.concatenate([mine, mask] if h == 0 else [mask, mine], axis=0)
            s = dot(qh[h, rows], w)
            if diagonal:
                n = rows.stop - rows.start
                a = lax.broadcasted_iota(jnp.int32, (n, BK), 0)
                b = lax.broadcasted_iota(jnp.int32, (n, BK), 1)
                s = jnp.where(b <= a, s, -1e30)
            s_scr[h, slot, rows] = s
            m = mx[h, rows]
            for t in range(0, BK, 128):
                m = jnp.maximum(m, s[:, t : t + 128])
            mx[h, rows] = m

    def values(g, off, slot, rows):
        s_scr, mx = s_bank[g % 2], mx_bank[g % 2]
        for h in range(2):
            vp = v_ref[pl.ds(off, BK), g * 128 : g * 128 + 128]
            vh = jnp.where(conds[h], vp, jnp.ones_like(vp))
            m = mx[h, rows]
            p = jnp.concatenate(
                [
                    jnp.exp(s_scr[h, slot, rows, t : t + 128] - m).astype(BF16)
                    for t in range(0, BK, 128)
                ],
                axis=1,
            )
            acc[h, rows] += dot(p, vh)

    def sweep(f):
        def span(lo, hi, rows, unroll=1):
            def step(kb, carry):
                f(relative_offset(kb, shard, per), kb, rows, False)
                return carry

            def steps(i, carry):
                for j in range(unroll):
                    step(lo + unroll * i + j, carry)
                return carry

            if unroll > 1:
                turns = lax.div(jnp.maximum(hi - lo, 0), unroll)
                lax.fori_loop(0, turns, steps, 0)
                lo = lo + unroll * turns
            lax.fori_loop(lo, hi, step, 0)

        if causal:
            own = shard * per
            span(lo0, jnp.minimum(lo1, own), upper, 2)
            span(lo1, own, both, 2)
            f(0, own, both, True)
            f(BK, own + 1, lower, True)
        else:
            span(lo0, jnp.minimum(lo1, hi0), upper)
            span(lo1, hi0, both, 2)
            span(jnp.maximum(hi0, lo1), hi1, lower)

    def start(g):
        mx = mx_bank[g % 2]
        cols = slice(g * 128, g * 128 + 128)
        for h in range(2):
            qh[h] = jnp.where(conds[h], q_ref[:, cols], fq_ref[...])
            mx[h] = jnp.full((length, 128), -3e38, F32)

    def turn(g):
        mx = mx_bank[g % 2]
        for h in range(2):
            for r in range(0, length, 128):
                rows = slice(r, r + 128)
                top = jnp.max(mx[h, rows], axis=-1, keepdims=True)
                mx[h, rows] = jnp.broadcast_to(top, (128, 128))
                acc[h, rows] = jnp.zeros((128, 128), F32)

    def finish(g):
        mx = mx_bank[g % 2]
        cols = slice(g * 128, g * 128 + 128)
        for r in range(0, length, 128):
            rows = slice(r, r + 128)
            a0, a1 = acc[0, rows], acc[1, rows]
            num = jnp.where(conds[0], a0, a1)
            den = jnp.where(conds[0], a1, a0)
            o_ref[rows, cols] = (num / pltpu.roll(den, 64, 1)).astype(BF16)
            lse_ref[g, rows] = jnp.where(conds[0], mx[1, rows], mx[0, rows]) + jnp.log(den)

    start(0)
    sweep(lambda off, slot, rows, edge: scores(0, off, slot, rows, edge))

    for g in range(1, pairs):
        turn(g - 1)
        start(g)

        def pair(off, slot, rows, edge, g=g):
            scores(g, off, slot, rows, edge)
            values(g - 1, off, slot, rows)

        sweep(pair)
        finish(g - 1)
    turn(pairs - 1)
    sweep(lambda off, slot, rows, edge: values(pairs - 1, off, slot, rows))
    finish(pairs - 1)


def attend_scratch(length, full):
    return [
        ((2, length, 128), BF16),
        ((2, full // BK, length, BK), F32),
        ((2, full // BK, length, BK), F32),
        ((2, length, 128), F32),
        ((2, length, 128), F32),
        ((2, length, 128), F32),
    ]


def attend_back(rng, q, fq, logsum, do, o, keys, dkv_ref, qh, doh, qm, dom, dq_scr, causal):
    length = q.shape[0]
    per = length // BK
    shard = rng[SHARD]
    conds, l64 = half_masks()

    def negated_parts(x):
        high = x.astype(BF16).astype(F32)
        rest = x - high
        mid = rest.astype(BF16).astype(F32)
        low = rest - mid
        return -jnp.where(
            l64 == 8, high, jnp.where(l64 == 9, mid, jnp.where(l64 == 10, low, 0.0))
        )

    for r in range(0, length, 128):
        rows = slice(r, r + 128)
        q_r, do_r = q[rows], do[rows]
        prod = do_r.astype(F32) * o[rows].astype(F32)
        delta = jnp.where(
            conds[0],
            jnp.sum(jnp.where(conds[1], prod, 0.0), axis=-1, keepdims=True),
            jnp.sum(jnp.where(conds[0], prod, 0.0), axis=-1, keepdims=True),
        )
        fl = (negated_parts(logsum[rows]) + fq[rows].astype(F32)).astype(BF16)
        fd = negated_parts(delta).astype(BF16)
        zero = jnp.zeros_like(q_r)
        for h in range(2):
            qh[h, :, rows] = jnp.where(conds[h], q_r, fl).T
            doh[h, :, rows] = jnp.where(conds[h], do_r, fd).T
            qm[h, rows] = jnp.where(conds[h], q_r, zero)
            dom[h, rows] = jnp.where(conds[h], do_r, zero)
    dq_scr[...] = jnp.zeros_like(dq_scr)
    ones = jnp.where((l64 >= 8) & (l64 <= 10), 1.0, 0.0).astype(BF16)
    k_ref, v_ref, fk_ref = (x.get() for x in keys)

    def block(off, halves, diagonal=None, size=BK):
        kp = k_ref[pl.ds(off, size), :]
        vp = v_ref[pl.ds(off, size), :]
        fk = fk_ref[pl.ds(off, size), :]
        ones_block = jnp.broadcast_to(ones, vp.shape)
        kt = kp.T
        dk = jnp.zeros((size, 128), F32)
        dv = jnp.zeros((size, 128), F32)
        for h in range(2):
            kh = jnp.where(conds[h], kp, fk)
            vh = jnp.where(conds[h], vp, ones_block)
            rows = slice(64 * h, 64 * h + 64)
            for half in halves:
                r = half * RT
                s = dot(kh, qh[h, :, r : r + RT])
                if diagonal == half:
                    s = jnp.where(triangle(True), s, -1e30)
                p = jnp.exp(s)
                dp = dot(vh, doh[h, :, r : r + RT])
                ds = (p * dp).astype(BF16)
                dv += dot(p.astype(BF16), dom[h, r : r + RT])
                dk += dot(ds, qm[h, r : r + RT])
                dq_scr[rows, r : r + RT] += dot(kt[rows], ds)
        dkv_ref[pl.ds(off, size), 0:128] = dk.astype(BF16)
        dkv_ref[pl.ds(off, size), 128:256] = dv.astype(BF16)

    def sweep(lo, hi, halves):
        def step(kb, carry):
            block(relative_offset(kb, shard, per), halves)
            return carry

        lax.fori_loop(lo, hi, step, 0)

    def sweep_two(lo, hi, halves):
        first = lax.div(lo + 1, 2)
        last = lax.div(hi, 2)

        def step(kb, carry):
            block(relative_offset(2 * kb, shard, per), halves, size=2 * BK)
            return carry

        lax.fori_loop(first, last, step, 0)
        sweep(lo, jnp.minimum(2 * first, hi), halves)
        sweep(jnp.maximum(2 * last, 2 * first), hi, halves)

    lo0, lo1 = rng[LO0], rng[LO1]
    common = sweep_two
    if causal:
        own = shard * per
        sweep_two(lo0, jnp.minimum(lo1, own), (0,))
        common(lo1, own, (0, 1))
        block(0, (0, 1), 0)
        block(BK, (1,), 1)
    else:
        hi0, hi1 = rng[HI0], rng[HI1]
        sweep(lo0, jnp.minimum(lo1, hi0), (0,))
        common(lo1, hi0, (0, 1))
        sweep(jnp.maximum(hi0, lo1), hi1, (1,))
    return dq_scr[...].T * 0.125


def norm_rows(hidden):
    center = hidden - jnp.mean(hidden, axis=-1, keepdims=True)
    spread = lax.rsqrt(jnp.mean(center * center, axis=-1, keepdims=True) + EPSILON)
    return center * spread, spread


def norm_rows_back(upstream, normed, spread, gain):
    scaled = upstream * gain
    return spread * (
        scaled
        - jnp.mean(scaled, axis=-1, keepdims=True)
        - normed * jnp.mean(scaled * normed, axis=-1, keepdims=True)
    )


def put_block(both, m, rows, value):
    both[m % 2, m // 2, rows] = value


def put_far(both, m, rows, value):
    both[m // 2, m % 2, rows] = value


def row_of(ref, i):
    return ref[i : i + 1, :].astype(F32)


def self_body(rng, held, results, qh, s_even, s_odd, mx_even, mx_odd, acc, kt, a_low):
    x0, win, pb, x1, x2, x3, fq, fkt, wout, wq, gain, shift = held
    q, k, v, o, lse, a, n_out, r_out, q2_out, xt, at_out = results
    length, width = x0.ref.shape
    shard = rng[SHARD]
    eighth = jnp.asarray(0.125, BF16)
    x_ref, win_ref, pb_ref = x0.get(), win.get(), pb.get()
    start_all(held)
    q.ref[...] = (dot(x_ref[...], win_ref[:, :width]) + row_of(pb_ref, 0)).astype(BF16) * eighth
    q.send()
    for m, x in enumerate((x0, x1, x2, x3)):
        x_m = x.get()

        def fill(m=m, x_m=x_m):
            x = x_m[...]
            rows = slice(m * length, (m + 1) * length)
            for c in range(0, width, 256):
                cols = slice(c, c + 256)
                k_new = dot(x, win_ref[:, width + c : width + c + 256]).astype(BF16)
                k.ref[rows, cols] = k_new
                kt[cols, rows] = k_new.T
                v_new = dot(x, win_ref[:, 2 * width + c : 2 * width + c + 256])
                v.ref[rows, cols] = (v_new + pb_ref[1:2, cols].astype(F32)).astype(BF16)
            xt.ref[:, rows] = x.T

        if m == 0:
            fill()
        else:
            pl.when((shard ^ m) < shard)(fill)
    k.send()
    v.send()
    xt.send()
    attend(rng, q.ref, fq.get(), kt, v.ref, fkt.get(), o.ref, lse.ref, qh, s_even, s_odd, mx_even, mx_odd, acc, True)
    o.send()
    lse.send()
    wout_ref, wq_ref, gain_ref, shift_ref = wout.get(), wq.get(), gain.get(), shift.get()
    for c in range(0, width, 256):
        cols = slice(c, c + 256)
        h = x_ref[:, cols].astype(F32) + dot(o.ref[...], wout_ref[:, cols])
        n_out.ref[:, cols] = h + pb_ref[2:3, cols].astype(F32)
    for r in range(0, length, 128):
        rows = slice(r, r + 128)
        n, spread = norm_rows(n_out.ref[rows])
        a_new = n * row_of(gain_ref, 0) + row_of(shift_ref, 0)
        n_out.ref[rows] = n
        r_out.ref[rows] = jnp.broadcast_to(spread, (128, 128))
        a.ref[rows] = a_new
        a_low[rows] = a_new.astype(BF16)
    n_out.send()
    a.send()
    at_out.ref[...] = a_low[...].T
    for c in range(0, width, 256):
        cols = slice(c, c + 256)
        q2 = dot(a_low[...], wq_ref[:, cols]) + pb_ref[3:4, cols].astype(F32)
        q2_out.ref[:, cols] = q2.astype(BF16) * eighth


def self_forward(rng, parts, fq, fkt, win, wout, wq, pb, gain, shift):
    length, width = parts[0].shape
    full = len(parts) * length
    return call(
        self_body,
        rng,
        [parts[0], win, pb, *parts[1:], fq, fkt, wout, wq, gain, shift],
        [
            ((length, width), BF16), ((full, width), BF16), ((full, width), BF16),
            ((length, width), BF16), ((width // 128, length, 128), F32), ((length, width), F32),
            ((length, width), F32), ((length, 128), F32), ((length, width), BF16), ((width, full), BF16),
            ((width, length), BF16),
        ],
        attend_scratch(length, full) + [((width, full), BF16), ((length, width), BF16)],
        flops=10**7,
        vmem=40,
        loose=parts[1:],
        early=6,
    )


GELU_A = 0.7978845608028654
GELU_B = 0.044715


def cross_body(rng, held, results, qh, s_even, s_odd, mx_even, mx_odd, acc, kt, n1, r1, a2, a2_low, act, y_scr, dy_scr):
    wkv, pb, y0, y1, y2, y3, q, fq, fkt, wout, a1, gain, shift, w1, w2, eb, cot = held
    k, v, o, lse, out, do, dh, keep, send, deb, small, yt = results
    length, width = q.ref.shape
    shard = rng[SHARD]
    wkv_ref, pb_ref = wkv.get(), pb.get()
    for m, y in enumerate((y0, y1, y2, y3)):
        y_ref = y.get()
        if m == 1:
            start_all(held)
        x = y_ref[...]
        rows = slice(m * length, (m + 1) * length)
        for c in range(0, width, 256):
            cols = slice(c, c + 256)
            k_new = dot(x, wkv_ref[:, cols]).astype(BF16)
            k.ref[rows, cols] = k_new
            kt[cols, rows] = k_new.T
            v_new = dot(x, wkv_ref[:, width + c : width + c + 256])
            v.ref[rows, cols] = (v_new + pb_ref[4:5, cols].astype(F32)).astype(BF16)
        yt.ref[:, rows] = x.T
    k.send()
    v.send()
    yt.send()
    attend(rng, q.get(), fq.get(), kt, v.ref, fkt.get(), o.ref, lse.ref, qh, s_even, s_odd, mx_even, mx_odd, acc, False)
    o.send()
    lse.send()
    wout_ref, a1_ref, gain_ref, shift_ref = wout.get(), a1.get(), gain.get(), shift.get()
    for c in range(0, width, 256):
        cols = slice(c, c + 256)
        y_scr[:, cols] = a1_ref[:, cols] + (dot(o.ref[...], wout_ref[:, cols]) + pb_ref[5:6, cols].astype(F32))
    for r in range(0, length, 128):
        rows = slice(r, r + 128)
        n, spread = norm_rows(y_scr[rows])
        n1[rows] = n
        r1[rows] = jnp.broadcast_to(spread, (128, 128))
        a2[rows] = n * row_of(gain_ref, 1) + row_of(shift_ref, 1)
    y_scr[...] = jnp.zeros_like(y_scr)
    a2_low[...] = a2[...].astype(BF16)
    kt[:, 0:length] = a2_low[...].T
    w1_ref, w2_ref, eb_ref, cot_ref = w1.get(), w2.get(), eb.get(), cot.get()
    inner = w1_ref.shape[1]
    chunks = inner // width

    def expand(c):
        cols = slice(c * width, (c + 1) * width)
        for t in range(0, width, 256):
            half_cols = slice(c * width + t, c * width + t + 256)
            u = dot(a2_low[...], w1_ref[:, half_cols]) + eb_ref[0:1, half_cols].astype(F32)
            square = u * u
            th = jnp.tanh(u * (GELU_A + (GELU_A * GELU_B) * square))
            half = 0.5 * th + 0.5
            act[c, :, t : t + 256] = (u * half).astype(BF16)
            slope = (u - u * (th * th)) * (0.5 * GELU_A + (1.5 * GELU_A * GELU_B) * square)
            s_even[t // 256, c] = half + slope
        y_scr[...] += dot(act[c], w2_ref[cols, :])

    for c in range(chunks):
        expand(c)
    zero = jnp.zeros((1, width), F32)
    db5, db6, dg1, ds1, dg2, ds2 = (zero,) * 6
    for r in range(0, length, 128):
        rows = slice(r, r + 128)
        n, spread = norm_rows(a2[rows] + y_scr[rows] + row_of(pb_ref, 6))
        out.ref[rows] = (n * row_of(gain_ref, 2) + row_of(shift_ref, 2)).astype(BF16)
        position = shard * length + r + lax.broadcasted_iota(jnp.int32, (128, 1), 0)
        g = jnp.where(position < rng[VALID], cot_ref[rows].astype(F32), 0.0)
        dg2 += jnp.sum(g * n, axis=0, keepdims=True)
        ds2 += jnp.sum(g, axis=0, keepdims=True)
        dh3 = norm_rows_back(g, n, spread, row_of(gain_ref, 2))
        dy3 = dh3.astype(BF16)
        db6 += jnp.sum(dy3.astype(F32), axis=0, keepdims=True)
        dy_scr[rows] = dy3
        y_scr[rows] = dh3
    out.send()

    parts = width // 128

    def contract(c):
        cols = slice(c * width, (c + 1) * width)
        dus = []
        for t in range(0, width, 256):
            half_cols = slice(c * width + t, c * width + t + 256)
            du = (s_even[t // 256, c] * dot(dy_scr[...], w2_ref[half_cols, :], NT)).astype(BF16)
            deb.ref[0:1, half_cols] = jnp.sum(du.astype(F32), axis=0, keepdims=True)
            dus.append(du)
        du = jnp.concatenate(dus, axis=1)
        y_scr[...] += dot(du, w1_ref[:, cols], NT)
        g1 = dot(kt[:, 0:length], du)
        for j in range(parts):
            put_block(
                keep.both, c ^ shard, slice(inner + j * width, inner + (j + 1) * width),
                g1[:, j * 128 : (j + 1) * 128].astype(BF16),
            )
        g2 = dot(act[c], dy_scr[...], TN)
        at = slice(c * width, (c + 1) * width)
        for b in range(4):
            put_block(keep.both, shard ^ b, at, g2[:, b * 128 : (b + 1) * 128].astype(BF16))

    for c in range(chunks):
        contract(c)
    for r in range(0, length, 128):
        rows = slice(r, r + 128)
        up = y_scr[rows]
        n = n1[rows]
        dg1 += jnp.sum(up * n, axis=0, keepdims=True)
        ds1 += jnp.sum(up, axis=0, keepdims=True)
        dh2 = norm_rows_back(up, n, r1[rows, 0:1], row_of(gain_ref, 1))
        dh.ref[rows] = dh2
        dy2 = dh2.astype(BF16)
        dy_scr[rows] = dy2
        db5 += jnp.sum(dy2.astype(F32), axis=0, keepdims=True)
    dh.send()
    for c in range(0, width, 256):
        cols = slice(c, c + 256)
        do.ref[:, cols] = dot(dy_scr[...], wout_ref[cols, :], NT).astype(BF16)
    do.send()
    g3 = dot(o.ref[...], dy_scr[...], TN)
    for b in range(4):
        put_block(
            keep.both, shard ^ b, slice(2 * inner, 2 * inner + width),
            g3[:, b * 128 : (b + 1) * 128].astype(BF16),
        )
    for i, value in enumerate((db5, db6, dg1, dg2, ds1, ds2)):
        small.ref[i : i + 1, :] = value
    small.ref[6:8, :] = jnp.zeros((2, width), F32)


def cross_forward(rng, parts, fq, fkt, q, a1, cot, wkv, wout, w1, w2, eb, pb, gain, shift):
    length, width = q.shape
    full, inner = len(parts) * length, w1.shape[1]
    return call(
        cross_body,
        rng,
        [wkv, pb, *parts, q, fq, fkt, wout, a1, gain, shift, w1, w2, eb, cot],
        [
            ((full, width), BF16), ((full, width), BF16), ((length, width), BF16),
            ((width // 128, length, 128), F32), ((length, width), BF16), ((length, width), BF16),
            ((length, width), F32), ((2, 2 * inner + width, 128), BF16, 2), ((1, inner), F32),
            ((8, width), F32), ((width, full), BF16),
        ],
        attend_scratch(length, full)
        + [
            ((width, full), BF16),
            ((length, width), F32), ((length, 128), F32), ((length, width), F32), ((length, width), BF16),
            ((inner // width, length, width), BF16),
            ((length, width), F32), ((length, width), BF16),
        ],
        flops=10**7,
        vmem=60,
        loose=parts[1:],
        early=6,
    )


def back_body(rng, held, results, qh, doh, qm, dom, dq_scr, w_scr, c_scr, *more_scr, causal, pack, pairs):
    first, second, shared = held[:8], held[8 : 6 * pairs + 2], held[6 * pairs + 2 :]
    xq, xt = shared[:2]
    fq, fk = held[1], held[7]
    shard = rng[SHARD]
    groups = [(held[0], held[2], held[3], held[4], held[5], held[6])]
    if pairs == 2:
        groups.append(tuple(second))
    for i, (q, lse, do, o, k, v) in enumerate(groups):
        dq_out, dkv, w, small = results[4 * i : 4 * i + 4]
        length = q.ref.shape[0]
        dkv.ref[...] = jnp.zeros_like(dkv.ref)
        own = [x.get() for x in (q, fq, lse, do, o)]
        start_all(held)
        dq = attend_back(rng, *own, (k, v, fk), dkv.ref, qh, doh, qm, dom, dq_scr, causal).astype(BF16)
        dkv.send()
        dq_out.ref[...] = dq
        dq_out.send()
        w.ref[0] = dot(xq.get()[...], dq).astype(BF16)
        w_scr[...] = jnp.zeros_like(w_scr)
        c_scr[...] = jnp.zeros_like(c_scr)
        xt_ref = xt.get()
        for m in range(xt_ref.shape[1] // length):

            def more(m=m):
                span = slice(m * length, (m + 1) * length)
                part = dkv.ref[span, :]
                w_scr[...] += dot(xt_ref[:, span], part)
                c_scr[...] += jnp.sum(part[:, 128:].astype(F32), axis=0, keepdims=True)

            if causal and m:
                pl.when((shard ^ m) < shard)(more)
            else:
                more()
        w.ref[1] = w_scr[:, :128].astype(BF16)
        w.ref[2] = w_scr[:, 128:].astype(BF16)
        small.ref[0:1, :] = jnp.sum(dq.astype(F32), axis=0, keepdims=True)
        small.ref[1:2, :] = c_scr[0:1]
        small.ref[2:8, :] = jnp.zeros((6, 128), F32)
        w.send()
    if pack is not None:
        own = [[x.ref for x in results[4 * i : 4 * i + 4]] for i in range(pairs)]
        pack(rng, shared[2:], own, results[4 * pairs :], *more_scr)


def pack_memory(rng, others, own, outs, dy_scr):
    wkv, dkv0, dkv1, dq0, dq1, u0, u1, wq, dh2, n0, r0, gain, wout, o = others
    mem_keep, mem_send, dh, do, keep, send, small = outs
    parts = [dkv0.get(), dkv1.get(), own[0][1], own[1][1]]
    shard = rng[SHARD]
    for m in (1, 3, 0, 2):
        spread_block(parts, wkv.get(), 0, m, (mem_keep, mem_send)[m % 2].ref)
    mem_keep.send()
    mem_send.send()
    length, width = dh2.ref.shape
    pairs = width // 128
    zero = jnp.zeros((1, width), F32)
    db2, dg0, ds0 = zero, zero, zero
    dq_refs = [dq0.get(), dq1.get(), own[0][0], own[1][0]]
    dq = jnp.concatenate([d[...] for d in dq_refs], axis=1)
    wq_ref, dh2_ref, n_ref, r_ref, gain_ref, wout_ref = (x.get() for x in (wq, dh2, n0, r0, gain, wout))
    for c in range(0, width, 256):
        cols = slice(c, c + 256)
        dh.ref[:, cols] = dh2_ref[:, cols] + dot(dq, wq_ref[cols, :], NT)
    for r in range(0, length, 128):
        rows = slice(r, r + 128)
        up = dh.ref[rows]
        n = n_ref[rows]
        dg0 += jnp.sum(up * n, axis=0, keepdims=True)
        ds0 += jnp.sum(up, axis=0, keepdims=True)
        new = norm_rows_back(up, n, r_ref[rows, 0:1], row_of(gain_ref, 0))
        dh.ref[rows] = new
        dy = new.astype(BF16)
        dy_scr[rows] = dy
        db2 += jnp.sum(dy.astype(F32), axis=0, keepdims=True)
    dh.send()
    for c in range(0, width, 256):
        cols = slice(c, c + 256)
        do.ref[:, cols] = dot(dy_scr[...], wout_ref[cols, :], NT).astype(BF16)
    do.send()
    g = dot(o.get()[...], dy_scr[...], TN)
    for b in range(4):
        put_block(keep.both, shard ^ b, slice(0, width), g[:, b * 128 : (b + 1) * 128].astype(BF16))
    units = [u0.get(), u1.get(), own[0][2], own[1][2]]
    for b in range(4):
        put_block(keep.both, shard ^ b, slice(width, 2 * width), units[b][0])
    for i in range(2 * pairs):
        b, at = i // 2, 2 + i % 2
        put_block(keep.both, shard ^ b, slice(at * width, (at + 1) * width), units[i % pairs][1 + i // pairs])
    for i, value in enumerate((db2, dg0, ds0)):
        small.ref[i : i + 1, :] = value
    small.ref[3:8, :] = jnp.zeros((5, width), F32)


def pack_early(rng, others, own, outs):
    w0, w1 = (x.get() for x in others)
    w = own[0][2]
    both = outs[0].both
    width = w.shape[1]
    for b, columns in enumerate(((w0[0], w1[0]), (w0[1], w1[1]), (w[1], w0[2]), (w1[2], w[2]))):
        for at, value in enumerate(columns):
            put_far(both, rng[SHARD] ^ b, slice(at * width, (at + 1) * width), value)


def pack_late(rng, others, own, outs):
    w2, a0, a1, a2, b0, b1, b2, b3, s0_ref, s2_ref, deb_ref = (x.get() for x in others)
    w, small = own[0][2:]
    both = outs[0].both
    width = w.shape[1]
    own_small, other = (a0, a1, a2, small), (b0, b1, b2, b3)
    for b, value in enumerate((w2[0], w[0], w[1], w[2])):
        put_block(both, rng[SHARD] ^ b, slice(0, width), value)
    pad = both.shape[2] - width
    for b in range(4):
        cols = slice(b * 128, (b + 1) * 128)
        rows = [deb_ref[0:1, b * width + j * 128 : b * width + (j + 1) * 128] for j in range(width // 128)]
        rows += [own_small[b][0:1], own_small[b][1:2], s0_ref[0:1, cols], other[b][0:1], other[b][1:2]]
        rows += [s2_ref[0:1, cols], s2_ref[1:2, cols]]
        rows += [s0_ref[1:2, cols], s2_ref[2:3, cols], s2_ref[3:4, cols]]
        rows += [s0_ref[2:3, cols], s2_ref[4:5, cols], s2_ref[5:6, cols]]
        rows.append(jnp.zeros((pad - len(rows), 128), F32))
        put_block(both, rng[SHARD] ^ b, slice(width, width + pad), jnp.concatenate(rows, axis=0).astype(BF16))


def attend_backward(rng, pairs, q, fq, lse, do, o, fk, k, v, xq, xt, causal, pack=None, extra=(), packed=(), more=(), vmem=22):
    length, width = q.shape
    full = k.shape[0]
    ins, outs = [], []
    for i, p in enumerate(pairs):
        cut = pl.ds(p * 128, 128)
        if i == 0:
            ins += [(q, cut), fq, (lse, p), (do, cut), (o, cut), (k, cut), (v, cut), fk]
        else:
            ins += [(q, cut), (lse, p), (do, cut), (o, cut), (k, cut), (v, cut)]
        outs += [((length, 128), BF16), ((full, 256), BF16), ((3, width, 128), BF16), ((8, 128), F32)]
    if pack is not None:
        outs += list(packed)
    out = call(
        functools.partial(back_body, causal=causal, pack=pack, pairs=len(pairs)),
        rng,
        [*ins, (xq, pl.ds(0, length)), xt, *extra],
        outs,
        [((2, 128, length), BF16)] * 2
        + [((2, length, 128), BF16)] * 2
        + [((128, length), F32), ((width, 256), F32), ((8, 128), F32), *more],
        flops=10**7,
        vmem=vmem,
        early=8,
    )
    return [out[4 * i : 4 * i + 4] for i in range(len(pairs))] + [out[4 * len(pairs) :]]


def spread_block(parts, w_ref, offset, m, ref):
    length, width = ref.shape[1:]
    rows = slice(m * length, (m + 1) * length)
    dk = jnp.concatenate([d[rows, :128] for d in parts], axis=1)
    dv = jnp.concatenate([d[rows, 128:] for d in parts], axis=1)
    for c in range(0, width, 256):
        cols = slice(c, c + 256)
        total = dot(dk, w_ref[cols, offset : offset + width], NT)
        total += dot(dv, w_ref[cols, offset + width : offset + 2 * width], NT)
        ref[m // 2, :, cols] = total.astype(BF16)


def spread_body(rng, held, results, *, causal, offset):
    keep, send = results
    shard = rng[SHARD]
    refs = [x.get() for x in held]
    w_ref, parts = refs[0], refs[1:]
    for m in (1, 3, 0, 2):
        ref = (keep.ref, send.ref)[m % 2]

        def fill(m=m, ref=ref):
            spread_block(parts, w_ref, offset, m, ref)

        def clear(m=m, ref=ref):
            ref[m // 2] = jnp.zeros_like(ref[m // 2])

        if causal and m:
            pl.when((shard ^ m) < shard)(fill)
            pl.when((shard ^ m) > shard)(clear)
        else:
            fill()
        if m == 3:
            send.send()


def spread_keys(rng, dkvs, w, length, causal, offset):
    width = w.shape[0]
    return call(
        functools.partial(spread_body, causal=causal, offset=offset),
        rng,
        [w, *dkvs],
        [((2, length, width), BF16), ((2, length, width), BF16)],
        [],
        flops=10**7,
    )


def partial_body(rng, held, results):
    wq, dq0, dq1, dq2, dq3, dh, near, got = held
    total = results[0].ref
    width = total.shape[1]
    dq = jnp.concatenate([x.get()[...] for x in (dq0, dq1, dq2, dq3)], axis=1)
    wq_ref, dh_ref, near_ref, got_ref = (x.get() for x in (wq, dh, near, got))
    for c in range(0, width, 256):
        cols = slice(c, c + 256)
        total[:, cols] = (
            dh_ref[:, cols]
            + dot(dq, wq_ref[cols, :], NT)
            + (near_ref[:, cols].astype(F32) + got_ref[:, cols].astype(F32))
        )


def target_partial(rng, win, dqs, dh, near, got):
    length, width = dh.shape
    return call(
        partial_body,
        rng,
        [(win, pl.ds(0, width)), *dqs, dh, (near, 0), (got, 0)],
        [((length, width), F32)],
        [],
        flops=20 * 10**9,
        loose=[got],
    )[0]


def outputs_body(rng, held, results):
    part, far_t, near, got, far_m, sums = held
    target_grad, memory_grad, expand, reduce, outproj = results
    part_ref, far_ref = part.get(), far_t.get()
    target_grad.ref[...] = part_ref[...] + far_ref[...].astype(F32)
    target_grad.send()
    near_ref, got_ref, far_ref = near.get(), got.get(), far_m.get()
    memory_grad.ref[...] = near_ref[...].astype(F32) + got_ref[...].astype(F32) + far_ref[...].astype(F32)
    memory_grad.send()
    sums_ref = sums.get()
    inner = reduce.ref.shape[0]
    width = expand.ref.shape[0]
    reduce.ref[...] = sums_ref[0:inner].astype(F32)
    reduce.send()
    for j in range(expand.ref.shape[1] // 128):
        rows = slice(inner + j * width, inner + (j + 1) * width)
        expand.ref[:, j * 128 : (j + 1) * 128] = sums_ref[rows].astype(F32)
    expand.send()
    outproj.ref[...] = sums_ref[2 * inner : 2 * inner + width].astype(F32)


def first_outputs(rng, part, far_t, near, got, far_m, sums, inner, shards):
    length, width = part.shape
    return call(
        outputs_body,
        rng,
        [part, far_t, (near, 0), (got, 0), far_m, sums],
        [
            ((length, width), F32), ((length, width), F32), ((width, inner // shards), F32), ((inner, 128), F32),
            ((width, 128), F32),
        ],
        [],
        flops=20 * 10**9,
        loose=[far_t, got, far_m, sums],
    )


def finish_body(rng, held, results):
    sums = held[1].get()
    w, outproj, query, keyval, eb, pb, gain, shift = (r.ref for r in results)
    width = w.shape[0]
    shard = rng[SHARD]
    outproj[...] = sums[0:width].astype(F32)
    query[...] = sums[width : 2 * width].astype(F32)
    for j in range(keyval.shape[1] // 128):
        keyval[:, j * 128 : (j + 1) * 128] = sums[(2 + j) * width : (3 + j) * width].astype(F32)
    for x in results[1:4]:
        x.send()
    total = held[0].get()
    second = jnp.where(shard == 1, 0, jnp.where(shard == 2, 2, 1))
    third = jnp.where((shard == 1) | (shard == 2), 1, 2)
    for j, at in enumerate((jnp.where(shard == 1, 2, 0), second, third)):
        rows = pl.ds(pl.multiple_of(at * width, width), width)
        w[:, j * 128 : (j + 1) * 128] = total[rows].astype(F32)
    results[0].send()
    rest = total[3 * width : 3 * width + 32].astype(F32)
    for j in range(width // 128):
        eb[0:1, j * 128 : (j + 1) * 128] = rest[j : j + 1]
    pb[...] = rest[4:11]
    gain[...] = rest[11:14]
    shift[...] = rest[14:17]


def finish(rng, total, sums, width):
    return call(
        finish_body,
        rng,
        [total, sums],
        [
            ((width, 384), F32), ((width, 128), F32), ((width, 128), F32), ((width, 256), F32), ((1, width), F32),
            ((7, 128), F32), ((3, 128), F32), ((3, 128), F32),
        ],
        [],
        loose=[total, sums],
    )


def partner(x, axis, mask):
    n = lax.axis_size(axis)
    return lax.ppermute(x, axis, [(i, i ^ mask) for i in range(n)])


def add(a, b):
    return (a.astype(F32) + b.astype(F32)).astype(BF16)


def after(x, *deps):
    return lax.optimization_barrier((x, *deps))[0]


def half_of(x, bit):
    half = x.shape[0] // 2
    return lax.dynamic_slice_in_dim(x, bit * half, half, 0)


def dp_bit(j):
    return (lax.axis_index("dp") >> j) & 1


class Flow:
    def __init__(self, keep, send):
        bits = lax.axis_size("dp").bit_length() - 1
        self.steps = [("core", 0), ("chip", 0)]
        self.steps += [("fold", j) for j in range(bits)]
        self.steps += [("join", j) for j in reversed(range(bits))]
        self.keep, self.out, self.cur, self.got = keep, send, None, None

    def done(self):
        return not self.steps

    def begin(self):
        if self.done():
            return
        kind, j = self.steps[0]
        if kind == "core":
            self.got = partner(self.out, "seq", 1)
        elif kind == "chip":
            self.got = partner(self.out, "seq", 2)
        elif kind == "fold":
            self.got = partner(half_of(self.cur, 1 - dp_bit(j)), "dp", 1 << j)
        else:
            self.got = partner(self.cur, "dp", 1 << j)

    def end(self, *deps):
        if self.done():
            return
        kind, j = self.steps.pop(0)
        got = after(self.got, *deps) if deps else self.got
        if kind == "core":
            self.out = add(self.keep[1], got[1])
            self.cur = add(self.keep[0], got[0])
        elif kind == "chip":
            self.cur = add(self.cur, got)
        elif kind == "fold":
            self.cur = add(half_of(self.cur, dp_bit(j)), got)
        else:
            low = dp_bit(j) == 0
            self.cur = jnp.where(low, jnp.concatenate([self.cur, got]), jnp.concatenate([got, self.cur]))

    def state(self):
        return self.out if self.steps and self.steps[0][0] == "chip" else self.cur


class SplitFlow:
    def __init__(self, keep, got):
        half = keep.shape[1] // 2
        self.keep, self.arrived, self.half = keep, got, half
        self.far = add(keep[1, :half], got[1, :half])
        rows = half // 2
        at = half + (1 - dp_bit(0)) * rows
        self.other = add(
            lax.dynamic_slice_in_dim(keep, at, rows, 1), lax.dynamic_slice_in_dim(got, at, rows, 1)
        )
        bits = lax.axis_size("dp").bit_length() - 1
        self.steps = ["cross", "back"] + [("fold", j) for j in range(1, bits)]
        self.steps += [("join", j) for j in reversed(range(1, bits))] + ["last"]
        self.cur = self.got = None

    def done(self):
        return not self.steps

    def begin(self):
        if self.done():
            return
        step = self.steps[0]
        if step == "cross":
            self.got = (partner(self.far, "seq", 2), partner(self.other, "dp", 1))
        elif step == "back":
            self.got = (partner(half_of(self.low, 1 - dp_bit(0)), "dp", 1), partner(self.high[1], "seq", 2))
        elif step == "last":
            self.got = partner(self.cur, "dp", 1)
        elif step[0] == "fold":
            self.got = partner(half_of(self.cur, 1 - dp_bit(step[1])), "dp", 1 << step[1])
        else:
            self.got = partner(self.cur, "dp", 1 << step[1])

    def end(self, *deps):
        if self.done():
            return
        step = self.steps.pop(0)
        if step in ("cross", "back"):
            one, two = after(self.got[0], *deps), after(self.got[1], *deps)
        else:
            got = after(self.got, *deps)
        if step == "cross":
            keep, got, half = after(self.keep, *deps), after(self.arrived, *deps), self.half
            self.low = add(keep[0, :half].astype(F32) + got[0, :half].astype(F32), one)
            at = half + dp_bit(0) * (half // 2)
            mine = [lax.dynamic_slice_in_dim(x, at, half // 2, 1).astype(F32) for x in (keep, got)]
            self.high = add(mine[0] + mine[1], two)
        elif step == "back":
            self.cur = jnp.concatenate([add(half_of(self.low, dp_bit(0)), one), add(self.high[0], two)])
        elif step == "last":
            low = dp_bit(0) == 0
            a, b = jnp.where(low, self.cur, got), jnp.where(low, got, self.cur)
            half = a.shape[0] // 2
            self.cur = jnp.concatenate([a[:half], b[:half], a[half:], b[half:]])
        elif step[0] == "fold":
            self.cur = add(half_of(self.cur, dp_bit(step[1])), got)
        else:
            low = dp_bit(step[1]) == 0
            self.cur = jnp.where(low, jnp.concatenate([self.cur, got]), jnp.concatenate([got, self.cur]))

    def state(self):
        if self.cur is not None:
            return (self.cur,)
        return (self.far, self.other) if self.steps[0] == "cross" else (self.low, self.high)


def local(
    target, memory, cotangent, target_segments, source_segments, target_lengths, source_lengths,
    self_inproj, self_outproj, cross_query, cross_keyval, cross_outproj, ffn_expand, ffn_reduce,
    expand_bias, proj_bias, norm_gain, norm_shift,
):
    target, memory, cotangent = target[0], memory[0], cotangent[0]
    length, width = target.shape
    shards = lax.axis_size("seq")
    shard = lax.axis_index("seq").astype(jnp.int32)
    unit = 16 * lax.axis_size("dp")

    t2 = partner(target, "seq", 2)
    t1 = partner(target, "seq", 1)
    m1 = partner(memory, "seq", 1)
    self_rng, cross_rng, fq, self_fk, cross_fk, self_fkt, cross_fkt = prepare(
        shard, target_lengths, source_lengths, target_segments, source_segments, length
    )
    t2 = after(t2, self_rng)
    t3 = partner(t2, "seq", 1)
    m2 = partner(after(memory, t2), "seq", 2)
    target_parts = [target, t1, t2, t3]

    q1, k1, v1, o1, lse1, a1, n0, r0, q2, target_t, a1_t = self_forward(
        self_rng, target_parts, fq, self_fkt, self_inproj, self_outproj, cross_query, proj_bias,
        norm_gain, norm_shift,
    )
    m2 = after(m2, q2)
    memory_parts = [memory, m1, m2, partner(m2, "seq", 1)]
    k2, v2, o2, lse2, layer_out, do2, dh2, keep_a, send_a, deb, small2, memory_t = cross_forward(
        cross_rng, memory_parts, fq, cross_fkt, q2, a1, cotangent, cross_keyval, cross_outproj,
        ffn_expand, ffn_reduce, expand_bias, proj_bias, norm_gain, norm_shift,
    )
    got_a = partner(send_a, "seq", 1)

    def cross_back(pairs, *deps, **pack):
        rng = after(cross_rng, *deps) if deps else cross_rng
        return attend_backward(
            rng, pairs, q2, fq, lse2, do2, o2, cross_fk, k2, v2, a1_t, memory_t, False, **pack
        )

    def self_back(p, *deps, **pack):
        rng = after(self_rng, *deps) if deps else self_rng
        return attend_backward(
            rng, [p], q1, fq, lse1, do1, o1, self_fk, k1, v1, target_t, target_t, True, **pack
        )

    c0, c1, _ = cross_back([0, 1])
    got_a = after(got_a, c1[0])
    flow_a = SplitFlow(keep_a, got_a)
    flow_a.begin()
    rows_b = ((2, 4 * width, 128), BF16, 2)
    half = ((2, length, width), BF16)
    c2, c3, (mem_keep, mem_send, dh1, do1, keep_b, send_b, small0) = cross_back(
        [2, 3], c1[0], *flow_a.state(), pack=pack_memory,
        extra=(
            cross_keyval, c0[1], c1[1], c0[0], c1[0], c0[2], c1[2], cross_query, dh2, n0, r0, norm_gain,
            self_outproj, o1,
        ),
        packed=(
            half, half, ((length, width), F32), ((length, width), BF16), rows_b, ((8, width), F32),
        ),
        more=[((length, width), BF16)],
        vmem=36,
    )
    cross = (c0, c1, c2, c3)
    mem_got = partner(mem_send, "seq", 1)
    flow_b = Flow(keep_b, send_b)
    flow_b.begin()
    flow_a.end(do1)
    flow_a.begin()
    s0 = self_back(0, *flow_a.state(), do1)[0]
    mem_far = add(mem_keep[1], after(mem_got, s0[0])[1])
    mem_get = partner(mem_far, "seq", 2)
    flow_a.end(s0[0])
    flow_b.end(s0[0])
    flow_a.begin()
    flow_b.begin()
    s1 = self_back(1, *flow_a.state(), flow_b.state(), mem_far, s0[0])[0]
    flow_a.end(s1[0])
    flow_b.end(s1[0])
    flow_a.begin()
    flow_b.begin()
    s2, (keep_c, send_c) = self_back(
        2, *flow_a.state(), flow_b.state(), s1[0], pack=pack_early, extra=(s0[2], s1[2]), packed=[((2, 2 * width, 128), BF16, 2)],
    )
    got_c = partner(send_c, "seq", 2)
    flow_a.end(s2[0])
    flow_b.end(s2[0])
    flow_a.begin()
    flow_b.begin()
    s3, (keep_d, send_d) = self_back(
        3, *flow_a.state(), flow_b.state(), s2[0], pack=pack_late,
        extra=(s2[2], s0[3], s1[3], s2[3], c0[3], c1[3], c2[3], c3[3], small0, small2, deb),
        packed=[((2, width + unit, 128), BF16, 2)],
    )
    selfs = (s0, s1, s2, s3)
    got_d = partner(send_d, "seq", 1)
    two_c = add(keep_c, after(got_c, s3[0]))
    core_c = partner(two_c[1], "seq", 1)
    flow_a.end(s3[0])
    flow_b.end(s3[0])
    flow_a.begin()
    flow_b.begin()
    far_d, near_d = add(keep_d[1], got_d[1]), add(keep_d[0], got_d[0])
    get_d = partner(far_d, "seq", 2)
    tgt_keep, tgt_send = spread_keys(
        after(self_rng, far_d, two_c, *flow_a.state(), flow_b.state()), [s[1] for s in selfs], self_inproj,
        length, True, width,
    )
    get_d, core_c = after(get_d, tgt_keep), after(core_c, tgt_keep)
    tgt_got = partner(tgt_send, "seq", 1)
    flow_a.end(tgt_keep)
    flow_b.end(tgt_keep)
    flow_a.begin()
    flow_b.begin()
    block = jnp.concatenate([add(two_c[0], core_c), add(near_d, get_d)])
    tgt_far = add(tgt_keep[1], tgt_got[1])
    tgt_get = partner(tgt_far, "seq", 2)
    block = after(block, tgt_far)
    devices = lax.axis_size("dp")
    parts = lax.all_to_all(block.reshape(devices, -1, 128), "dp", 0, 0, tiled=True)
    partial = target_partial(
        after(self_rng, block), self_inproj, [s[0] for s in selfs], dh1, tgt_keep, tgt_got
    )
    flow_b.end(partial)
    flow_b.begin()
    parts = after(parts, partial, flow_b.state(), tgt_get)
    part = jnp.sum(parts.astype(F32), axis=0).astype(BF16)
    flow_b.end(part)
    flow_b.begin()
    spread_part = after(jnp.broadcast_to(part[None], parts.shape), flow_b.state())
    whole = lax.all_to_all(spread_part, "dp", 0, 0, tiled=True).reshape(-1, 128)
    flow_a.end(part)
    while not flow_a.done():
        flow_a.begin()
        flow_a.end()
    target_grad, memory_grad, expand_grad, reduce_grad, outproj_grad = first_outputs(
        after(self_rng, spread_part), partial, tgt_get, mem_keep, mem_got, mem_get, flow_a.cur,
        ffn_expand.shape[1], shards,
    )
    flow_b.end(target_grad)
    while not flow_b.done():
        flow_b.begin()
        flow_b.end()
    self_in, self_out_grad, query_grad, keyval_grad, eb_grad, pb_grad, gain_grad, shift_grad = finish(
        self_rng, after(whole, target_grad), flow_b.cur, width
    )
    return (
        layer_out[None],
        target_grad[None],
        memory_grad[None],
        self_in,
        self_out_grad,
        query_grad,
        keyval_grad,
        outproj_grad,
        expand_grad,
        reduce_grad,
        eb_grad,
        pb_grad,
        gain_grad,
        shift_grad,
    )


def solution(mesh):
    rows, shard = P("dp", "seq", None), P(None, "seq")
    in_specs = (rows, rows, rows, P("dp", None), P("dp", None), P("dp"), P("dp")) + (P(),) * 11
    out_specs = (rows, rows, rows) + (shard,) * 11
    return jax.shard_map(local, mesh=mesh, in_specs=in_specs, out_specs=out_specs, check_vma=False)
```

```python
import functools
import jax
import jax.numpy as jnp
from jax import lax
from jax.experimental import pallas as pl
from jax.experimental.pallas import tpu as pltpu
from jax.sharding import PartitionSpec as P

BF16 = jnp.bfloat16
F32 = jnp.float32
EPSILON = 1e-05
BK = 256
RT = 256
NT = (((1,), (1,)), ((), ()))
NN = (((1,), (0,)), ((), ()))
TN = (((0,), (0,)), ((), ()))


def dot(a, b, dims=NN):
    return lax.dot_general(a, b, dims, preferred_element_type=F32)


class Held:
    def __init__(self, copy, ref):
        self.copy, self.ref, self.started, self.waited = copy, ref, False, False

    def start(self):
        if not self.started:
            self.copy.start()
            self.started = True

    def get(self):
        self.start()
        if not self.waited:
            self.copy.wait()
            self.waited = True
        return self.ref


class Result:
    def __init__(self, copy, ref, both=None):
        self.copy, self.ref, self.both, self.started = copy, ref, both, False

    def send(self):
        self.copy.start()
        self.started = True


def call(body, rng, ins, outs, scratch, flops=10**7, vmem=24, loose=(), early=None):
    arrays, columns = [], []
    shapes = []
    for x in ins:
        x, cut, *shape = x if isinstance(x, tuple) else (x, None)
        arrays.append(x)
        columns.append(cut)
        if shape:
            shapes.append(shape[0])
        elif cut is None:
            shapes.append(x.shape)
        else:
            shapes.append(x.shape[1:] if isinstance(cut, int) else x.shape[:-1] + (cut.size,))
    pairs = [len(out) == 3 for out in outs]
    buffers = [((2, *out[0]) if pair else out[0], out[1]) for out, pair in zip(outs, pairs)]
    outs = [out[:2] for out, pair in zip(outs, pairs) for _ in range(1 + pair)]
    n_in, n_out, n_buf, n_scr = len(ins), len(outs), len(buffers), len(scratch)

    def kernel(rng_ref, *refs):
        hbm_in, refs = refs[:n_in], refs[n_in:]
        hbm_out, refs = refs[:n_out], refs[n_out:]
        vm_in, refs = refs[:n_in], refs[n_in:]
        vm_buf, refs = refs[:n_buf], refs[n_buf:]
        scr, refs = refs[:n_scr], refs[n_scr:]
        sem_in, sem_out = refs
        held = []
        for i, (src, dst, cut) in enumerate(zip(hbm_in, vm_in, columns)):
            if callable(cut):
                src = cut(src)
            elif isinstance(cut, int):
                src = src.at[cut]
            elif cut is not None:
                src = src.at[(slice(None),) * (len(src.shape) - 1) + (cut,)]
            held.append(Held(pltpu.make_async_copy(src, dst, sem_in.at[i]), dst))
        for x in held[:early]:
            x.start()
        parts = []
        for ref, pair in zip(vm_buf, pairs):
            parts += [(ref.at[0], ref), (ref.at[1], ref)] if pair else [(ref, None)]
        results = [
            Result(pltpu.make_async_copy(src, dst, sem_out.at[i]), src, both)
            for i, ((src, both), dst) in enumerate(zip(parts, hbm_out))
        ]
        body(rng_ref, held, results, *scr)
        for x in held:
            x.get()
        for x in results:
            if not x.started:
                x.send()
        for x in results:
            x.copy.wait()

    hbm = pl.BlockSpec(memory_space=pltpu.HBM)
    return pl.pallas_call(
        kernel,
        out_shape=tuple(pltpu.HBM(s, d) for s, d in outs),
        in_specs=[pl.BlockSpec(memory_space=pltpu.SMEM)] + [hbm] * n_in,
        out_specs=(hbm,) * n_out,
        scratch_shapes=[pltpu.VMEM(s, x.dtype) for s, x in zip(shapes, arrays)]
        + [pltpu.VMEM(s, d) for s, d in buffers]
        + [pltpu.VMEM(s, d) for s, d in scratch]
        + [pltpu.SemaphoreType.DMA((n_in,)), pltpu.SemaphoreType.DMA((n_out,))],
        compiler_params=pltpu.CompilerParams(vmem_limit_bytes=vmem * 2**20),
        cost_estimate=pl.CostEstimate(flops=flops, bytes_accessed=2**20, transcendentals=0),
    )(
        rng,
        *[
            x if any(x is y for y in loose) else pltpu.with_memory_space_constraint(x, pltpu.HBM)
            for x in arrays
        ],
    )


LO0, HI0, LO1, HI1, SHARD, VALID = range(6)


def prepare_body(
    info, lengths, t_smem, t_ref, s_ref, self_rng, cross_rng, fq_ref, self_fk, cross_fk, self_fkt, cross_fkt
):
    length = fq_ref.shape[0]
    shard = info[0]
    valid, count = lengths[0], lengths[1]
    full = t_ref.shape[1]
    t_row, s_row = t_ref[...], s_ref[...]

    def number(mask):
        return jnp.sum(jnp.where(mask, 1.0, 0.0)).astype(jnp.int32)

    for half in range(2):
        first = t_smem[0, shard * length + half * RT]
        last = t_smem[0, shard * length + half * RT + RT - 1]
        self_rng[LO0 + 2 * half] = lax.div(number(t_row < first), BK)
        self_rng[HI0 + 2 * half] = 0
        cross_rng[LO0 + 2 * half] = lax.div(number(s_row < first), BK)
        end = jnp.minimum(number(s_row <= last), count)
        cross_rng[HI0 + 2 * half] = lax.div(end + BK - 1, BK)
    for ref in (self_rng, cross_rng):
        ref[SHARD] = shard
        ref[VALID] = valid
        ref[6] = info[1]
        ref[7] = 0
    f = lax.broadcasted_iota(jnp.int32, (128, 128), 1) % 64

    def column(ref, at):
        return jnp.broadcast_to(ref[0:1, pl.ds(pl.multiple_of(at, 128), 128)], (128, 128)).T

    row = lax.broadcasted_iota(jnp.int32, (128, 128), 0)
    for m in range(full // length):
        for t in range(0, length, 128):
            at = (shard ^ m) * length + t
            for ref, total, out, out_t in ((t_ref, valid, self_fk, self_fkt), (s_ref, count, cross_fk, cross_fkt)):
                seg = column(ref, at)
                seen = (seg == f) & (row + at < total)
                feature = jnp.where(
                    f < 8, jnp.where(seen, 0.0, -1e30), jnp.where(f < 11, 1.0, 0.0)
                )
                out[m * length + t : m * length + t + 128] = feature.astype(BF16)
                out_t[:, m * length + t : m * length + t + 128] = feature.astype(BF16).T[0:64]
                if m == 0 and out is self_fk:
                    fq_ref[t : t + 128] = jnp.where(seg == f, 1.0, 0.0).astype(BF16)


def prepare(shard, target_length, source_length, target_segments, source_segments, length):
    full = target_segments.shape[1]
    sd = jax.ShapeDtypeStruct
    smem, vm = pl.BlockSpec(memory_space=pltpu.SMEM), pl.BlockSpec(memory_space=pltpu.VMEM)
    return pl.pallas_call(
        prepare_body,
        out_shape=(
            sd((8,), jnp.int32), sd((8,), jnp.int32), sd((length, 128), BF16), sd((full, 128), BF16),
            sd((full, 128), BF16), sd((64, full), BF16), sd((64, full), BF16),
        ),
        in_specs=[smem, smem, smem, vm, vm],
        out_specs=(smem, smem, vm, vm, vm, vm, vm),
    )(
        jnp.stack([shard, lax.axis_index("dp").astype(jnp.int32) & 1]),
        jnp.concatenate([target_length, source_length]), target_segments,
        target_segments, source_segments,
    )


def start_all(held):
    for x in held:
        x.start()


def half_masks():
    lane = lax.broadcasted_iota(jnp.int32, (1, 128), 1)
    return (lane < 64, lane >= 64), lane % 64


def relative_offset(block, shard, per_shard):
    owner = lax.div(block, per_shard)
    return pl.multiple_of(((owner ^ shard) * per_shard + lax.rem(block, per_shard)) * BK, BK)


def triangle(transposed):
    a = lax.broadcasted_iota(jnp.int32, (BK, BK), 0)
    b = lax.broadcasted_iota(jnp.int32, (BK, BK), 1)
    return a <= b if transposed else b <= a


def attend(rng, q_ref, fq_ref, kt, v_ref, fkt_ref, o_ref, lse_ref, qh, s_even, s_odd, mx_even, mx_odd, acc, causal):
    length, width = q_ref.shape
    per = length // BK
    pairs = width // 128
    shard = rng[SHARD]
    conds, _ = half_masks()
    lo0, hi0, lo1, hi1 = rng[LO0], rng[HI0], rng[LO1], rng[HI1]
    both, upper, lower = slice(0, length), slice(0, RT), slice(RT, length)
    s_bank, mx_bank = (s_even, s_odd), (mx_even, mx_odd)

    def scores(g, off, slot, rows, diagonal):
        s_scr, mx = s_bank[g % 2], mx_bank[g % 2]
        mask = fkt_ref[0:64, pl.ds(off, BK)]
        for h in range(2):
            at = g * 128 + 64 * h
            mine = kt[at : at + 64, pl.ds(off, BK)]
            w = jnp.concatenate([mine, mask] if h == 0 else [mask, mine], axis=0)
            s = dot(qh[h, rows], w)
            if diagonal:
                n = rows.stop - rows.start
                a = lax.broadcasted_iota(jnp.int32, (n, BK), 0)
                b = lax.broadcasted_iota(jnp.int32, (n, BK), 1)
                s = jnp.where(b <= a, s, -1e30)
            s_scr[h, slot, rows] = s
            m = mx[h, rows]
            for t in range(0, BK, 128):
                m = jnp.maximum(m, s[:, t : t + 128])
            mx[h, rows] = m

    def values(g, off, slot, rows):
        s_scr, mx = s_bank[g % 2], mx_bank[g % 2]
        for h in range(2):
            vp = v_ref[pl.ds(off, BK), g * 128 : g * 128 + 128]
            vh = jnp.where(conds[h], vp, jnp.ones_like(vp))
            m = mx[h, rows]
            p = jnp.concatenate(
                [
                    jnp.exp(s_scr[h, slot, rows, t : t + 128] - m).astype(BF16)
                    for t in range(0, BK, 128)
                ],
                axis=1,
            )
            acc[h, rows] += dot(p, vh)

    def sweep(f):
        def span(lo, hi, rows, unroll=1):
            def step(kb, carry):
                f(relative_offset(kb, shard, per), kb, rows, False)
                return carry

            def steps(i, carry):
                for j in range(unroll):
                    step(lo + unroll * i + j, carry)
                return carry

            if unroll > 1:
                turns = lax.div(jnp.maximum(hi - lo, 0), unroll)
                lax.fori_loop(0, turns, steps, 0)
                lo = lo + unroll * turns
            lax.fori_loop(lo, hi, step, 0)

        if causal:
            own = shard * per
            span(lo0, jnp.minimum(lo1, own), upper, 2)
            span(lo1, own, both, 2)
            f(0, own, both, True)
            f(BK, own + 1, lower, True)
        else:
            span(lo0, jnp.minimum(lo1, hi0), upper)
            span(lo1, hi0, both, 2)
            span(jnp.maximum(hi0, lo1), hi1, lower)

    def start(g):
        mx = mx_bank[g % 2]
        cols = slice(g * 128, g * 128 + 128)
        for h in range(2):
            qh[h] = jnp.where(conds[h], q_ref[:, cols], fq_ref[...])
            mx[h] = jnp.full((length, 128), -3e38, F32)

    def turn(g):
        mx = mx_bank[g % 2]
        for h in range(2):
            for r in range(0, length, 128):
                rows = slice(r, r + 128)
                top = jnp.max(mx[h, rows], axis=-1, keepdims=True)
                mx[h, rows] = jnp.broadcast_to(top, (128, 128))
                acc[h, rows] = jnp.zeros((128, 128), F32)

    def finish(g):
        mx = mx_bank[g % 2]
        cols = slice(g * 128, g * 128 + 128)
        for r in range(0, length, 128):
            rows = slice(r, r + 128)
            a0, a1 = acc[0, rows], acc[1, rows]
            num = jnp.where(conds[0], a0, a1)
            den = jnp.where(conds[0], a1, a0)
            o_ref[rows, cols] = (num / pltpu.roll(den, 64, 1)).astype(BF16)
            lse_ref[g, rows] = jnp.where(conds[0], mx[1, rows], mx[0, rows]) + jnp.log(den)

    start(0)
    sweep(lambda off, slot, rows, edge: scores(0, off, slot, rows, edge))

    for g in range(1, pairs):
        turn(g - 1)
        start(g)

        def pair(off, slot, rows, edge, g=g):
            scores(g, off, slot, rows, edge)
            values(g - 1, off, slot, rows)

        sweep(pair)
        finish(g - 1)
    turn(pairs - 1)
    sweep(lambda off, slot, rows, edge: values(pairs - 1, off, slot, rows))
    finish(pairs - 1)


def attend_scratch(length, full):
    return [
        ((2, length, 128), BF16),
        ((2, full // BK, length, BK), F32),
        ((2, full // BK, length, BK), F32),
        ((2, length, 128), F32),
        ((2, length, 128), F32),
        ((2, length, 128), F32),
    ]


def attend_back(rng, q, fq, logsum, do, o, keys, dkv_ref, qh, doh, qm, dom, dq_scr, causal):
    length = q.shape[0]
    per = length // BK
    shard = rng[SHARD]
    conds, l64 = half_masks()

    def negated_parts(x):
        high = x.astype(BF16).astype(F32)
        rest = x - high
        mid = rest.astype(BF16).astype(F32)
        low = rest - mid
        return -jnp.where(
            l64 == 8, high, jnp.where(l64 == 9, mid, jnp.where(l64 == 10, low, 0.0))
        )

    for r in range(0, length, 128):
        rows = slice(r, r + 128)
        q_r, do_r = q[rows], do[rows]
        prod = do_r.astype(F32) * o[rows].astype(F32)
        delta = jnp.where(
            conds[0],
            jnp.sum(jnp.where(conds[1], prod, 0.0), axis=-1, keepdims=True),
            jnp.sum(jnp.where(conds[0], prod, 0.0), axis=-1, keepdims=True),
        )
        fl = (negated_parts(logsum[rows]) + fq[rows].astype(F32)).astype(BF16)
        fd = negated_parts(delta).astype(BF16)
        zero = jnp.zeros_like(q_r)
        for h in range(2):
            qh[h, :, rows] = jnp.where(conds[h], q_r, fl).T
            doh[h, :, rows] = jnp.where(conds[h], do_r, fd).T
            qm[h, rows] = jnp.where(conds[h], q_r, zero)
            dom[h, rows] = jnp.where(conds[h], do_r, zero)
    dq_scr[...] = jnp.zeros_like(dq_scr)
    ones = jnp.where((l64 >= 8) & (l64 <= 10), 1.0, 0.0).astype(BF16)
    k_ref, v_ref, fk_ref = (x.get() for x in keys)

    def block(off, halves, diagonal=None, size=BK):
        kp = k_ref[pl.ds(off, size), :]
        vp = v_ref[pl.ds(off, size), :]
        fk = fk_ref[pl.ds(off, size), :]
        ones_block = jnp.broadcast_to(ones, vp.shape)
        kt = kp.T
        dk = jnp.zeros((size, 128), F32)
        dv = jnp.zeros((size, 128), F32)
        for h in range(2):
            kh = jnp.where(conds[h], kp, fk)
            vh = jnp.where(conds[h], vp, ones_block)
            rows = slice(64 * h, 64 * h + 64)
            for half in halves:
                r = half * RT
                s = dot(kh, qh[h, :, r : r + RT])
                if diagonal == half:
                    s = jnp.where(triangle(True), s, -1e30)
                p = jnp.exp(s)
                dp = dot(vh, doh[h, :, r : r + RT])
                ds = (p * dp).astype(BF16)
                dv += dot(p.astype(BF16), dom[h, r : r + RT])
                dk += dot(ds, qm[h, r : r + RT])
                dq_scr[rows, r : r + RT] += dot(kt[rows], ds)
        dkv_ref[pl.ds(off, size), 0:128] = dk.astype(BF16)
        dkv_ref[pl.ds(off, size), 128:256] = dv.astype(BF16)

    def sweep(lo, hi, halves):
        def step(kb, carry):
            block(relative_offset(kb, shard, per), halves)
            return carry

        lax.fori_loop(lo, hi, step, 0)

    def sweep_two(lo, hi, halves):
        first = lax.div(lo + 1, 2)
        last = lax.div(hi, 2)

        def step(kb, carry):
            block(relative_offset(2 * kb, shard, per), halves, size=2 * BK)
            return carry

        lax.fori_loop(first, last, step, 0)
        sweep(lo, jnp.minimum(2 * first, hi), halves)
        sweep(jnp.maximum(2 * last, 2 * first), hi, halves)

    lo0, lo1 = rng[LO0], rng[LO1]
    common = sweep_two
    if causal:
        own = shard * per
        sweep_two(lo0, jnp.minimum(lo1, own), (0,))
        common(lo1, own, (0, 1))
        block(0, (0, 1), 0)
        block(BK, (1,), 1)
    else:
        hi0, hi1 = rng[HI0], rng[HI1]
        sweep(lo0, jnp.minimum(lo1, hi0), (0,))
        common(lo1, hi0, (0, 1))
        sweep(jnp.maximum(hi0, lo1), hi1, (1,))
    return dq_scr[...].T * 0.125


def norm_rows(hidden):
    center = hidden - jnp.mean(hidden, axis=-1, keepdims=True)
    spread = lax.rsqrt(jnp.mean(center * center, axis=-1, keepdims=True) + EPSILON)
    return center * spread, spread


def norm_rows_back(upstream, normed, spread, gain):
    scaled = upstream * gain
    return spread * (
        scaled
        - jnp.mean(scaled, axis=-1, keepdims=True)
        - normed * jnp.mean(scaled * normed, axis=-1, keepdims=True)
    )


def put_block(both, m, rows, value):
    both[m % 2, m // 2, rows] = value


def put_far(both, m, rows, value):
    both[m // 2, m % 2, rows] = value


def row_of(ref, i):
    return ref[i : i + 1, :].astype(F32)


def self_body(rng, held, results, qh, s_even, s_odd, mx_even, mx_odd, acc, kt, a_low):
    x0, win, pb, x1, x2, x3, fq, fkt, wout, wq, gain, shift = held
    q, k, v, o, lse, a, n_out, r_out, q2_out, xt, at_out = results
    length, width = x0.ref.shape
    shard = rng[SHARD]
    eighth = jnp.asarray(0.125, BF16)
    x_ref, win_ref, pb_ref = x0.get(), win.get(), pb.get()
    start_all(held)
    q.ref[...] = (dot(x_ref[...], win_ref[:, :width]) + row_of(pb_ref, 0)).astype(BF16) * eighth
    q.send()
    for m, x in enumerate((x0, x1, x2, x3)):
        x_m = x.get()

        def fill(m=m, x_m=x_m):
            x = x_m[...]
            rows = slice(m * length, (m + 1) * length)
            for c in range(0, width, 256):
                cols = slice(c, c + 256)
                k_new = dot(x, win_ref[:, width + c : width + c + 256]).astype(BF16)
                k.ref[rows, cols] = k_new
                kt[cols, rows] = k_new.T
                v_new = dot(x, win_ref[:, 2 * width + c : 2 * width + c + 256])
                v.ref[rows, cols] = (v_new + pb_ref[1:2, cols].astype(F32)).astype(BF16)
            xt.ref[:, rows] = x.T

        if m == 0:
            fill()
        else:
            pl.when((shard ^ m) < shard)(fill)
    k.send()
    v.send()
    xt.send()
    attend(rng, q.ref, fq.get(), kt, v.ref, fkt.get(), o.ref, lse.ref, qh, s_even, s_odd, mx_even, mx_odd, acc, True)
    o.send()
    lse.send()
    wout_ref, wq_ref, gain_ref, shift_ref = wout.get(), wq.get(), gain.get(), shift.get()
    for c in range(0, width, 256):
        cols = slice(c, c + 256)
        h = x_ref[:, cols].astype(F32) + dot(o.ref[...], wout_ref[:, cols])
        n_out.ref[:, cols] = h + pb_ref[2:3, cols].astype(F32)
    for r in range(0, length, 128):
        rows = slice(r, r + 128)
        n, spread = norm_rows(n_out.ref[rows])
        a_new = n * row_of(gain_ref, 0) + row_of(shift_ref, 0)
        n_out.ref[rows] = n
        r_out.ref[rows] = jnp.broadcast_to(spread, (128, 128))
        a.ref[rows] = a_new
        a_low[rows] = a_new.astype(BF16)
    n_out.send()
    a.send()
    at_out.ref[...] = a_low[...].T
    for c in range(0, width, 256):
        cols = slice(c, c + 256)
        q2 = dot(a_low[...], wq_ref[:, cols]) + pb_ref[3:4, cols].astype(F32)
        q2_out.ref[:, cols] = q2.astype(BF16) * eighth


def self_forward(rng, parts, fq, fkt, win, wout, wq, pb, gain, shift):
    length, width = parts[0].shape
    full = len(parts) * length
    return call(
        self_body,
        rng,
        [parts[0], win, pb, *parts[1:], fq, fkt, wout, wq, gain, shift],
        [
            ((length, width), BF16), ((full, width), BF16), ((full, width), BF16),
            ((length, width), BF16), ((width // 128, length, 128), F32), ((length, width), F32),
            ((length, width), F32), ((length, 128), F32), ((length, width), BF16), ((width, full), BF16),
            ((width, length), BF16),
        ],
        attend_scratch(length, full) + [((width, full), BF16), ((length, width), BF16)],
        flops=10**7,
        vmem=40,
        loose=parts[1:],
        early=6,
    )


GELU_A = 0.7978845608028654
GELU_B = 0.044715


def cross_body(rng, held, results, qh, s_even, s_odd, mx_even, mx_odd, acc, kt, n1, r1, a2, a2_low, act, y_scr, dy_scr):
    wkv, pb, y0, y1, y2, y3, q, fq, fkt, wout, a1, gain, shift, w1, w2, eb, cot = held
    k, v, o, lse, out, do, dh, keep, send, deb, small, yt = results
    length, width = q.ref.shape
    shard = rng[SHARD]
    wkv_ref, pb_ref = wkv.get(), pb.get()
    for m, y in enumerate((y0, y1, y2, y3)):
        y_ref = y.get()
        if m == 1:
            start_all(held)
        x = y_ref[...]
        rows = slice(m * length, (m + 1) * length)
        for c in range(0, width, 256):
            cols = slice(c, c + 256)
            k_new = dot(x, wkv_ref[:, cols]).astype(BF16)
            k.ref[rows, cols] = k_new
            kt[cols, rows] = k_new.T
            v_new = dot(x, wkv_ref[:, width + c : width + c + 256])
            v.ref[rows, cols] = (v_new + pb_ref[4:5, cols].astype(F32)).astype(BF16)
        yt.ref[:, rows] = x.T
    k.send()
    v.send()
    yt.send()
    attend(rng, q.get(), fq.get(), kt, v.ref, fkt.get(), o.ref, lse.ref, qh, s_even, s_odd, mx_even, mx_odd, acc, False)
    o.send()
    lse.send()
    wout_ref, a1_ref, gain_ref, shift_ref = wout.get(), a1.get(), gain.get(), shift.get()
    for c in range(0, width, 256):
        cols = slice(c, c + 256)
        y_scr[:, cols] = a1_ref[:, cols] + (dot(o.ref[...], wout_ref[:, cols]) + pb_ref[5:6, cols].astype(F32))
    for r in range(0, length, 128):
        rows = slice(r, r + 128)
        n, spread = norm_rows(y_scr[rows])
        n1[rows] = n
        r1[rows] = jnp.broadcast_to(spread, (128, 128))
        a2[rows] = n * row_of(gain_ref, 1) + row_of(shift_ref, 1)
    y_scr[...] = jnp.zeros_like(y_scr)
    a2_low[...] = a2[...].astype(BF16)
    kt[:, 0:length] = a2_low[...].T
    w1_ref, w2_ref, eb_ref, cot_ref = w1.get(), w2.get(), eb.get(), cot.get()
    inner = w1_ref.shape[1]
    chunks = inner // width

    def expand(c):
        cols = slice(c * width, (c + 1) * width)
        for t in range(0, width, 256):
            half_cols = slice(c * width + t, c * width + t + 256)
            u = dot(a2_low[...], w1_ref[:, half_cols]) + eb_ref[0:1, half_cols].astype(F32)
            square = u * u
            th = jnp.tanh(u * (GELU_A + (GELU_A * GELU_B) * square))
            half = 0.5 * th + 0.5
            act[c, :, t : t + 256] = (u * half).astype(BF16)
            slope = (u - u * (th * th)) * (0.5 * GELU_A + (1.5 * GELU_A * GELU_B) * square)
            s_even[t // 256, c] = half + slope
        y_scr[...] += dot(act[c], w2_ref[cols, :])

    for c in range(chunks):
        expand(c)
    zero = jnp.zeros((1, width), F32)
    db5, db6, dg1, ds1, dg2, ds2 = (zero,) * 6
    for r in range(0, length, 128):
        rows = slice(r, r + 128)
        n, spread = norm_rows(a2[rows] + y_scr[rows] + row_of(pb_ref, 6))
        out.ref[rows] = (n * row_of(gain_ref, 2) + row_of(shift_ref, 2)).astype(BF16)
        position = shard * length + r + lax.broadcasted_iota(jnp.int32, (128, 1), 0)
        g = jnp.where(position < rng[VALID], cot_ref[rows].astype(F32), 0.0)
        dg2 += jnp.sum(g * n, axis=0, keepdims=True)
        ds2 += jnp.sum(g, axis=0, keepdims=True)
        dh3 = norm_rows_back(g, n, spread, row_of(gain_ref, 2))
        dy3 = dh3.astype(BF16)
        db6 += jnp.sum(dy3.astype(F32), axis=0, keepdims=True)
        dy_scr[rows] = dy3
        y_scr[rows] = dh3
    out.send()

    parts = width // 128

    def contract(c):
        cols = slice(c * width, (c + 1) * width)
        dus = []
        for t in range(0, width, 256):
            half_cols = slice(c * width + t, c * width + t + 256)
            du = (s_even[t // 256, c] * dot(dy_scr[...], w2_ref[half_cols, :], NT)).astype(BF16)
            deb.ref[0:1, half_cols] = jnp.sum(du.astype(F32), axis=0, keepdims=True)
            dus.append(du)
        du = jnp.concatenate(dus, axis=1)
        y_scr[...] += dot(du, w1_ref[:, cols], NT)
        g1 = dot(kt[:, 0:length], du)
        for j in range(parts):
            put_block(
                keep.both, c ^ shard, slice(inner + j * width, inner + (j + 1) * width),
                g1[:, j * 128 : (j + 1) * 128].astype(BF16),
            )
        g2 = dot(act[c], dy_scr[...], TN)
        at = slice(c * width, (c + 1) * width)
        for b in range(4):
            put_block(keep.both, shard ^ b, at, g2[:, b * 128 : (b + 1) * 128].astype(BF16))

    for c in range(chunks):
        contract(c)
    for r in range(0, length, 128):
        rows = slice(r, r + 128)
        up = y_scr[rows]
        n = n1[rows]
        dg1 += jnp.sum(up * n, axis=0, keepdims=True)
        ds1 += jnp.sum(up, axis=0, keepdims=True)
        dh2 = norm_rows_back(up, n, r1[rows, 0:1], row_of(gain_ref, 1))
        dh.ref[rows] = dh2
        dy2 = dh2.astype(BF16)
        dy_scr[rows] = dy2
        db5 += jnp.sum(dy2.astype(F32), axis=0, keepdims=True)
    dh.send()
    for c in range(0, width, 256):
        cols = slice(c, c + 256)
        do.ref[:, cols] = dot(dy_scr[...], wout_ref[cols, :], NT).astype(BF16)
    do.send()
    g3 = dot(o.ref[...], dy_scr[...], TN)
    for b in range(4):
        put_block(
            keep.both, shard ^ b, slice(2 * inner, 2 * inner + width),
            g3[:, b * 128 : (b + 1) * 128].astype(BF16),
        )
    for i, value in enumerate((db5, db6, dg1, dg2, ds1, ds2)):
        small.ref[i : i + 1, :] = value
    small.ref[6:8, :] = jnp.zeros((2, width), F32)


def cross_forward(rng, parts, fq, fkt, q, a1, cot, wkv, wout, w1, w2, eb, pb, gain, shift):
    length, width = q.shape
    full, inner = len(parts) * length, w1.shape[1]
    return call(
        cross_body,
        rng,
        [wkv, pb, *parts, q, fq, fkt, wout, a1, gain, shift, w1, w2, eb, cot],
        [
            ((full, width), BF16), ((full, width), BF16), ((length, width), BF16),
            ((width // 128, length, 128), F32), ((length, width), BF16), ((length, width), BF16),
            ((length, width), F32), ((2, 2 * inner + width, 128), BF16, 2), ((1, inner), F32),
            ((8, width), F32), ((width, full), BF16),
        ],
        attend_scratch(length, full)
        + [
            ((width, full), BF16),
            ((length, width), F32), ((length, 128), F32), ((length, width), F32), ((length, width), BF16),
            ((inner // width, length, width), BF16),
            ((length, width), F32), ((length, width), BF16),
        ],
        flops=10**7,
        vmem=57,
        loose=parts[1:],
        early=6,
    )


def back_body(rng, held, results, qh, doh, qm, dom, dq_scr, w_scr, c_scr, *more_scr, causal, pack, pairs):
    first, second, shared = held[:8], held[8 : 6 * pairs + 2], held[6 * pairs + 2 :]
    xq, xt = shared[:2]
    fq, fk = held[1], held[7]
    shard = rng[SHARD]
    groups = [(held[0], held[2], held[3], held[4], held[5], held[6])]
    if pairs == 2:
        groups.append(tuple(second))
    for i, (q, lse, do, o, k, v) in enumerate(groups):
        dq_out, dkv, w, small = results[4 * i : 4 * i + 4]
        length = q.ref.shape[0]
        dkv.ref[...] = jnp.zeros_like(dkv.ref)
        own = [x.get() for x in (q, fq, lse, do, o)]
        start_all(held)
        dq = attend_back(rng, *own, (k, v, fk), dkv.ref, qh, doh, qm, dom, dq_scr, causal).astype(BF16)
        dkv.send()
        dq_out.ref[...] = dq
        dq_out.send()
        w.ref[0] = dot(xq.get()[...], dq).astype(BF16)
        w_scr[...] = jnp.zeros_like(w_scr)
        c_scr[...] = jnp.zeros_like(c_scr)
        xt_ref = xt.get()
        for m in range(xt_ref.shape[1] // length):

            def more(m=m):
                span = slice(m * length, (m + 1) * length)
                part = dkv.ref[span, :]
                w_scr[...] += dot(xt_ref[:, span], part)
                c_scr[...] += jnp.sum(part[:, 128:].astype(F32), axis=0, keepdims=True)

            if causal and m:
                pl.when((shard ^ m) < shard)(more)
            else:
                more()
        w.ref[1] = w_scr[:, :128].astype(BF16)
        w.ref[2] = w_scr[:, 128:].astype(BF16)
        small.ref[0:1, :] = jnp.sum(dq.astype(F32), axis=0, keepdims=True)
        small.ref[1:2, :] = c_scr[0:1]
        small.ref[2:8, :] = jnp.zeros((6, 128), F32)
        w.send()
    if pack is not None:
        own = [[x.ref for x in results[4 * i : 4 * i + 4]] for i in range(pairs)]
        pack(rng, shared[2:], own, results[4 * pairs :], *more_scr)


def pack_memory(rng, others, own, outs, dy_scr):
    wkv, dkv0, dkv1, dq0, dq1, u0, u1, wq, dh2, n0, r0, gain, wout, o = others
    mem_keep, mem_send, dh, do, keep, send, small = outs
    parts = [dkv0.get(), dkv1.get(), own[0][1], own[1][1]]
    shard = rng[SHARD]
    for m in (1, 3, 0, 2):
        spread_block(parts, wkv.get(), 0, m, (mem_keep, mem_send)[m % 2].ref)
    mem_keep.send()
    mem_send.send()
    length, width = dh2.ref.shape
    pairs = width // 128
    zero = jnp.zeros((1, width), F32)
    db2, dg0, ds0 = zero, zero, zero
    dq_refs = [dq0.get(), dq1.get(), own[0][0], own[1][0]]
    dq = jnp.concatenate([d[...] for d in dq_refs], axis=1)
    wq_ref, dh2_ref, n_ref, r_ref, gain_ref, wout_ref = (x.get() for x in (wq, dh2, n0, r0, gain, wout))
    for c in range(0, width, 256):
        cols = slice(c, c + 256)
        dh.ref[:, cols] = dh2_ref[:, cols] + dot(dq, wq_ref[cols, :], NT)
    for r in range(0, length, 128):
        rows = slice(r, r + 128)
        up = dh.ref[rows]
        n = n_ref[rows]
        dg0 += jnp.sum(up * n, axis=0, keepdims=True)
        ds0 += jnp.sum(up, axis=0, keepdims=True)
        new = norm_rows_back(up, n, r_ref[rows, 0:1], row_of(gain_ref, 0))
        dh.ref[rows] = new
        dy = new.astype(BF16)
        dy_scr[rows] = dy
        db2 += jnp.sum(dy.astype(F32), axis=0, keepdims=True)
    dh.send()
    for c in range(0, width, 256):
        cols = slice(c, c + 256)
        do.ref[:, cols] = dot(dy_scr[...], wout_ref[cols, :], NT).astype(BF16)
    do.send()
    g = dot(o.get()[...], dy_scr[...], TN)
    for b in range(4):
        put_block(keep.both, shard ^ b, slice(0, width), g[:, b * 128 : (b + 1) * 128].astype(BF16))
    units = [u0.get(), u1.get(), own[0][2], own[1][2]]
    for b in range(4):
        put_block(keep.both, shard ^ b, slice(width, 2 * width), units[b][0])
    for i in range(2 * pairs):
        b, at = i // 2, 2 + i % 2
        put_block(keep.both, shard ^ b, slice(at * width, (at + 1) * width), units[i % pairs][1 + i // pairs])
    for i, value in enumerate((db2, dg0, ds0)):
        small.ref[i : i + 1, :] = value
    small.ref[3:8, :] = jnp.zeros((5, width), F32)


def pack_early(rng, others, own, outs):
    w0, w1 = (x.get() for x in others)
    w = own[0][2]
    both = outs[0].both
    width = w.shape[1]
    for b, columns in enumerate(((w0[0], w1[0]), (w0[1], w1[1]), (w[1], w0[2]), (w1[2], w[2]))):
        for at, value in enumerate(columns):
            put_far(both, rng[SHARD] ^ b, slice(at * width, (at + 1) * width), value)


def pack_late(rng, others, own, outs):
    w2, a0, a1, a2, b0, b1, b2, b3, s0_ref, s2_ref, deb_ref = (x.get() for x in others)
    w, small = own[0][2:]
    both = outs[0].both
    width = w.shape[1]
    own_small, other = (a0, a1, a2, small), (b0, b1, b2, b3)
    for b, value in enumerate((w2[0], w[0], w[1], w[2])):
        put_block(both, rng[SHARD] ^ b, slice(0, width), value)
    pad = both.shape[2] - width
    for b in range(4):
        cols = slice(b * 128, (b + 1) * 128)
        rows = [deb_ref[0:1, b * width + j * 128 : b * width + (j + 1) * 128] for j in range(width // 128)]
        rows += [own_small[b][0:1], own_small[b][1:2], s0_ref[0:1, cols], other[b][0:1], other[b][1:2]]
        rows += [s2_ref[0:1, cols], s2_ref[1:2, cols]]
        rows += [s0_ref[1:2, cols], s2_ref[2:3, cols], s2_ref[3:4, cols]]
        rows += [s0_ref[2:3, cols], s2_ref[4:5, cols], s2_ref[5:6, cols]]
        rows.append(jnp.zeros((pad - len(rows), 128), F32))
        put_block(both, rng[SHARD] ^ b, slice(width, width + pad), jnp.concatenate(rows, axis=0).astype(BF16))


def attend_backward(rng, pairs, q, fq, lse, do, o, fk, k, v, xq, xt, causal, pack=None, extra=(), packed=(), more=(), vmem=22):
    length, width = q.shape
    full = k.shape[0]
    ins, outs = [], []
    for i, p in enumerate(pairs):
        cut = pl.ds(p * 128, 128)
        if i == 0:
            ins += [(q, cut), fq, (lse, p), (do, cut), (o, cut), (k, cut), (v, cut), fk]
        else:
            ins += [(q, cut), (lse, p), (do, cut), (o, cut), (k, cut), (v, cut)]
        outs += [((length, 128), BF16), ((full, 256), BF16), ((3, width, 128), BF16), ((8, 128), F32)]
    if pack is not None:
        outs += list(packed)
    out = call(
        functools.partial(back_body, causal=causal, pack=pack, pairs=len(pairs)),
        rng,
        [*ins, (xq, pl.ds(0, length)), xt, *extra],
        outs,
        [((2, 128, length), BF16)] * 2
        + [((2, length, 128), BF16)] * 2
        + [((128, length), F32), ((width, 256), F32), ((8, 128), F32), *more],
        flops=10**7,
        vmem=vmem,
        early=8,
    )
    return [out[4 * i : 4 * i + 4] for i in range(len(pairs))] + [out[4 * len(pairs) :]]


def spread_block(parts, w_ref, offset, m, ref):
    length, width = ref.shape[1:]
    rows = slice(m * length, (m + 1) * length)
    dk = jnp.concatenate([d[rows, :128] for d in parts], axis=1)
    dv = jnp.concatenate([d[rows, 128:] for d in parts], axis=1)
    for c in range(0, width, 256):
        cols = slice(c, c + 256)
        total = dot(dk, w_ref[cols, offset : offset + width], NT)
        total += dot(dv, w_ref[cols, offset + width : offset + 2 * width], NT)
        ref[m // 2, :, cols] = total.astype(BF16)


def spread_body(rng, held, results, *, causal, offset):
    keep, send = results
    shard = rng[SHARD]
    refs = [x.get() for x in held]
    w_ref, parts = refs[0], refs[1:]
    for m in (1, 3, 0, 2):
        ref = (keep.ref, send.ref)[m % 2]

        def fill(m=m, ref=ref):
            spread_block(parts, w_ref, offset, m, ref)

        def clear(m=m, ref=ref):
            ref[m // 2] = jnp.zeros_like(ref[m // 2])

        if causal and m:
            pl.when((shard ^ m) < shard)(fill)
            pl.when((shard ^ m) > shard)(clear)
        else:
            fill()
        if m == 3:
            send.send()


def spread_keys(rng, dkvs, w, length, causal, offset):
    width = w.shape[0]
    return call(
        functools.partial(spread_body, causal=causal, offset=offset),
        rng,
        [w, *dkvs],
        [((2, length, width), BF16), ((2, length, width), BF16)],
        [],
        flops=10**7,
    )


def partial_body(rng, held, results):
    wq, dq0, dq1, dq2, dq3, dh, near, got = held
    total = results[0].ref
    width = total.shape[1]
    dq = jnp.concatenate([x.get()[...] for x in (dq0, dq1, dq2, dq3)], axis=1)
    wq_ref, dh_ref, near_ref, got_ref = (x.get() for x in (wq, dh, near, got))
    for c in range(0, width, 256):
        cols = slice(c, c + 256)
        total[:, cols] = (
            dh_ref[:, cols]
            + dot(dq, wq_ref[cols, :], NT)
            + (near_ref[:, cols].astype(F32) + got_ref[:, cols].astype(F32))
        )


def target_partial(rng, win, dqs, dh, near, got):
    length, width = dh.shape
    return call(
        partial_body,
        rng,
        [(win, pl.ds(0, width)), *dqs, dh, (near, 0), (got, 0)],
        [((length, width), F32)],
        [],
        flops=20 * 10**9,
        loose=[got],
    )[0]


def outputs_body(rng, held, results):
    part, far_t, near, got, far_m, sums = held
    target_grad, memory_grad, expand, reduce, outproj = results
    part_ref, far_ref = part.get(), far_t.get()
    target_grad.ref[...] = part_ref[...] + far_ref[...].astype(F32)
    target_grad.send()
    near_ref, got_ref, far_ref = near.get(), got.get(), far_m.get()
    memory_grad.ref[...] = near_ref[...].astype(F32) + got_ref[...].astype(F32) + far_ref[...].astype(F32)
    memory_grad.send()
    sums_ref = sums.get()
    inner = reduce.ref.shape[0]
    width = expand.ref.shape[0]
    reduce.ref[...] = sums_ref[0:inner].astype(F32)
    reduce.send()
    for j in range(expand.ref.shape[1] // 128):
        rows = slice(inner + j * width, inner + (j + 1) * width)
        expand.ref[:, j * 128 : (j + 1) * 128] = sums_ref[rows].astype(F32)
    expand.send()
    outproj.ref[...] = sums_ref[2 * inner : 2 * inner + width].astype(F32)


def first_outputs(rng, part, far_t, near, got, far_m, sums, inner, shards):
    length, width = part.shape
    return call(
        outputs_body,
        rng,
        [part, far_t, (near, 0), (got, 0), far_m, sums],
        [
            ((length, width), F32), ((length, width), F32), ((width, inner // shards), F32), ((inner, 128), F32),
            ((width, 128), F32),
        ],
        [],
        flops=20 * 10**9,
        loose=[far_t, got, far_m, sums],
    )


def finish_body(rng, held, results):
    sums = held[1].get()
    w, outproj, query, keyval, eb, pb, gain, shift = (r.ref for r in results)
    width = w.shape[0]
    shard = rng[SHARD]
    outproj[...] = sums[0:width].astype(F32)
    query[...] = sums[width : 2 * width].astype(F32)
    for j in range(keyval.shape[1] // 128):
        keyval[:, j * 128 : (j + 1) * 128] = sums[(2 + j) * width : (3 + j) * width].astype(F32)
    for x in results[1:4]:
        x.send()
    total = held[0].get()
    second = jnp.where(shard == 1, 0, jnp.where(shard == 2, 2, 1))
    third = jnp.where((shard == 1) | (shard == 2), 1, 2)
    for j, at in enumerate((jnp.where(shard == 1, 2, 0), second, third)):
        rows = pl.ds(pl.multiple_of(at * width, width), width)
        w[:, j * 128 : (j + 1) * 128] = total[rows].astype(F32)
    results[0].send()
    rest = total[3 * width : 3 * width + 32].astype(F32)
    for j in range(width // 128):
        eb[0:1, j * 128 : (j + 1) * 128] = rest[j : j + 1]
    pb[...] = rest[4:11]
    gain[...] = rest[11:14]
    shift[...] = rest[14:17]


def finish(rng, total, sums, width):
    return call(
        finish_body,
        rng,
        [total, sums],
        [
            ((width, 384), F32), ((width, 128), F32), ((width, 128), F32), ((width, 256), F32), ((1, width), F32),
            ((7, 128), F32), ((3, 128), F32), ((3, 128), F32),
        ],
        [],
        loose=[total, sums],
    )


def first_body(rng, held, results):
    keep_far, got_far, keep_rest, got_rest = held
    far, rest = results
    far.ref[...] = (keep_far.get()[...].astype(F32) + got_far.get()[...].astype(F32)).astype(BF16)
    far.send()
    half = rest.ref.shape[1]
    keep_ref, got_ref = keep_rest.get(), got_rest.get()
    rows = pl.ds(pl.multiple_of((1 - rng[6]) * half, 128), half)
    for m in range(2):
        rest.ref[m] = (keep_ref[m, rows].astype(F32) + got_ref[m, rows].astype(F32)).astype(BF16)


def first_sums(rng, keep, got):
    half = keep.shape[1] // 2
    low = lambda ref: ref.at[1, 0:half]
    high = lambda ref: ref.at[:, half : 2 * half]
    return call(
        first_body,
        rng,
        [(keep, low, (half, 128)), (got, low, (half, 128)), (keep, high, (2, half, 128)), (got, high, (2, half, 128))],
        [((half, 128), BF16), ((2, half // 2, 128), BF16)],
        [],
        loose=[got],
    )


def partner(x, axis, mask):
    n = lax.axis_size(axis)
    return lax.ppermute(x, axis, [(i, i ^ mask) for i in range(n)])


def add(a, b):
    return (a.astype(F32) + b.astype(F32)).astype(BF16)


def after(x, *deps):
    return lax.optimization_barrier((x, *deps))[0]


def half_of(x, bit):
    half = x.shape[0] // 2
    return lax.dynamic_slice_in_dim(x, bit * half, half, 0)


def dp_bit(j):
    return (lax.axis_index("dp") >> j) & 1


class Flow:
    def __init__(self, keep, send):
        bits = lax.axis_size("dp").bit_length() - 1
        self.steps = [("core", 0), ("chip", 0)]
        self.steps += [("fold", j) for j in range(bits)]
        self.steps += [("join", j) for j in reversed(range(bits))]
        self.keep, self.out, self.cur, self.got = keep, send, None, None

    def done(self):
        return not self.steps

    def begin(self):
        if self.done():
            return
        kind, j = self.steps[0]
        if kind == "core":
            self.got = partner(self.out, "seq", 1)
        elif kind == "chip":
            self.got = partner(self.out, "seq", 2)
        elif kind == "fold":
            self.got = partner(half_of(self.cur, 1 - dp_bit(j)), "dp", 1 << j)
        else:
            self.got = partner(self.cur, "dp", 1 << j)

    def end(self, *deps):
        if self.done():
            return
        kind, j = self.steps.pop(0)
        got = after(self.got, *deps) if deps else self.got
        if kind == "core":
            self.out = add(self.keep[1], got[1])
            self.cur = add(self.keep[0], got[0])
        elif kind == "chip":
            self.cur = add(self.cur, got)
        elif kind == "fold":
            self.cur = add(half_of(self.cur, dp_bit(j)), got)
        else:
            low = dp_bit(j) == 0
            self.cur = jnp.where(low, jnp.concatenate([self.cur, got]), jnp.concatenate([got, self.cur]))

    def state(self):
        return self.out if self.steps and self.steps[0][0] == "chip" else self.cur


class SplitFlow:
    def __init__(self, rng, keep, got):
        half = keep.shape[1] // 2
        self.keep, self.arrived, self.half = keep, got, half
        self.far, self.other = first_sums(rng, keep, got)
        bits = lax.axis_size("dp").bit_length() - 1
        self.steps = ["cross", "back"] + [("fold", j) for j in range(1, bits)]
        self.steps += [("join", j) for j in reversed(range(1, bits))] + ["last"]
        self.cur = self.got = None

    def done(self):
        return not self.steps

    def begin(self):
        if self.done():
            return
        step = self.steps[0]
        if step == "cross":
            self.got = (partner(self.far, "seq", 2), partner(self.other, "dp", 1))
        elif step == "back":
            self.got = (partner(half_of(self.low, 1 - dp_bit(0)), "dp", 1), partner(self.high[1], "seq", 2))
        elif step == "last":
            self.got = partner(self.cur, "dp", 1)
        elif step[0] == "fold":
            self.got = partner(half_of(self.cur, 1 - dp_bit(step[1])), "dp", 1 << step[1])
        else:
            self.got = partner(self.cur, "dp", 1 << step[1])

    def end(self, *deps):
        if self.done():
            return
        step = self.steps.pop(0)
        if step in ("cross", "back"):
            one, two = after(self.got[0], *deps), after(self.got[1], *deps)
        else:
            got = after(self.got, *deps)
        if step == "cross":
            keep, got, half = after(self.keep, *deps), after(self.arrived, *deps), self.half
            self.low = add(keep[0, :half].astype(F32) + got[0, :half].astype(F32), one)
            at = half + dp_bit(0) * (half // 2)
            mine = [lax.dynamic_slice_in_dim(x, at, half // 2, 1).astype(F32) for x in (keep, got)]
            self.high = add(mine[0] + mine[1], two)
        elif step == "back":
            self.cur = jnp.concatenate([add(half_of(self.low, dp_bit(0)), one), add(self.high[0], two)])
        elif step == "last":
            low = dp_bit(0) == 0
            a, b = jnp.where(low, self.cur, got), jnp.where(low, got, self.cur)
            half = a.shape[0] // 2
            self.cur = jnp.concatenate([a[:half], b[:half], a[half:], b[half:]])
        elif step[0] == "fold":
            self.cur = add(half_of(self.cur, dp_bit(step[1])), got)
        else:
            low = dp_bit(step[1]) == 0
            self.cur = jnp.where(low, jnp.concatenate([self.cur, got]), jnp.concatenate([got, self.cur]))

    def state(self):
        if self.cur is not None:
            return (self.cur,)
        return (self.far, self.other) if self.steps[0] == "cross" else (self.low, self.high)


def local(
    target, memory, cotangent, target_segments, source_segments, target_lengths, source_lengths,
    self_inproj, self_outproj, cross_query, cross_keyval, cross_outproj, ffn_expand, ffn_reduce,
    expand_bias, proj_bias, norm_gain, norm_shift,
):
    target, memory, cotangent = target[0], memory[0], cotangent[0]
    length, width = target.shape
    shards = lax.axis_size("seq")
    shard = lax.axis_index("seq").astype(jnp.int32)
    unit = 16 * lax.axis_size("dp")

    t2 = partner(target, "seq", 2)
    t1 = partner(target, "seq", 1)
    m1 = partner(memory, "seq", 1)
    self_rng, cross_rng, fq, self_fk, cross_fk, self_fkt, cross_fkt = prepare(
        shard, target_lengths, source_lengths, target_segments, source_segments, length
    )
    t2 = after(t2, self_rng)
    t3 = partner(t2, "seq", 1)
    m2 = partner(after(memory, t2), "seq", 2)
    target_parts = [target, t1, t2, t3]

    q1, k1, v1, o1, lse1, a1, n0, r0, q2, target_t, a1_t = self_forward(
        self_rng, target_parts, fq, self_fkt, self_inproj, self_outproj, cross_query, proj_bias,
        norm_gain, norm_shift,
    )
    m2 = after(m2, q2)
    memory_parts = [memory, m1, m2, partner(m2, "seq", 1)]
    k2, v2, o2, lse2, layer_out, do2, dh2, keep_a, send_a, deb, small2, memory_t = cross_forward(
        cross_rng, memory_parts, fq, cross_fkt, q2, a1, cotangent, cross_keyval, cross_outproj,
        ffn_expand, ffn_reduce, expand_bias, proj_bias, norm_gain, norm_shift,
    )
    got_a = partner(send_a, "seq", 1)

    def cross_back(pairs, *deps, **pack):
        rng = after(cross_rng, *deps) if deps else cross_rng
        return attend_backward(
            rng, pairs, q2, fq, lse2, do2, o2, cross_fk, k2, v2, a1_t, memory_t, False, **pack
        )

    def self_back(p, *deps, **pack):
        rng = after(self_rng, *deps) if deps else self_rng
        return attend_backward(
            rng, [p], q1, fq, lse1, do1, o1, self_fk, k1, v1, target_t, target_t, True, **pack
        )

    c0, c1, _ = cross_back([0, 1])
    got_a = after(got_a, c1[0])
    flow_a = SplitFlow(cross_rng, keep_a, got_a)
    flow_a.begin()
    rows_b = ((2, 4 * width, 128), BF16, 2)
    half = ((2, length, width), BF16)
    c2, c3, (mem_keep, mem_send, dh1, do1, keep_b, send_b, small0) = cross_back(
        [2, 3], c1[0], *flow_a.state(), pack=pack_memory,
        extra=(
            cross_keyval, c0[1], c1[1], c0[0], c1[0], c0[2], c1[2], cross_query, dh2, n0, r0, norm_gain,
            self_outproj, o1,
        ),
        packed=(
            half, half, ((length, width), F32), ((length, width), BF16), rows_b, ((8, width), F32),
        ),
        more=[((length, width), BF16)],
        vmem=36,
    )
    cross = (c0, c1, c2, c3)
    mem_got = partner(mem_send, "seq", 1)
    flow_b = Flow(keep_b, send_b)
    flow_b.begin()
    flow_a.end(do1)
    flow_a.begin()
    s0 = self_back(0, *flow_a.state(), do1)[0]
    mem_far = add(mem_keep[1], after(mem_got, s0[0])[1])
    mem_get = partner(mem_far, "seq", 2)
    flow_a.end(s0[0])
    flow_b.end(s0[0])
    flow_a.begin()
    flow_b.begin()
    s1 = self_back(1, *flow_a.state(), flow_b.state(), mem_far, s0[0])[0]
    flow_a.end(s1[0])
    flow_b.end(s1[0])
    flow_a.begin()
    flow_b.begin()
    s2, (keep_c, send_c) = self_back(
        2, *flow_a.state(), flow_b.state(), s1[0], pack=pack_early, extra=(s0[2], s1[2]), packed=[((2, 2 * width, 128), BF16, 2)],
    )
    got_c = partner(send_c, "seq", 2)
    flow_a.end(s2[0])
    flow_b.end(s2[0])
    flow_a.begin()
    flow_b.begin()
    s3, (keep_d, send_d) = self_back(
        3, *flow_a.state(), flow_b.state(), s2[0], pack=pack_late,
        extra=(s2[2], s0[3], s1[3], s2[3], c0[3], c1[3], c2[3], c3[3], small0, small2, deb),
        packed=[((2, width + unit, 128), BF16, 2)],
    )
    selfs = (s0, s1, s2, s3)
    got_d = partner(send_d, "seq", 1)
    two_c = add(keep_c, after(got_c, s3[0]))
    core_c = partner(two_c[1], "seq", 1)
    flow_a.end(s3[0])
    flow_b.end(s3[0])
    flow_a.begin()
    flow_b.begin()
    far_d, near_d = add(keep_d[1], got_d[1]), add(keep_d[0], got_d[0])
    get_d = partner(far_d, "seq", 2)
    tgt_keep, tgt_send = spread_keys(
        after(self_rng, far_d, two_c, *flow_a.state(), flow_b.state()), [s[1] for s in selfs], self_inproj,
        length, True, width,
    )
    get_d, core_c = after(get_d, tgt_keep), after(core_c, tgt_keep)
    tgt_got = partner(tgt_send, "seq", 1)
    flow_a.end(tgt_keep)
    flow_b.end(tgt_keep)
    flow_a.begin()
    flow_b.begin()
    block = jnp.concatenate([add(two_c[0], core_c), add(near_d, get_d)])
    tgt_far = add(tgt_keep[1], tgt_got[1])
    tgt_get = partner(tgt_far, "seq", 2)
    block = after(block, tgt_far)
    devices = lax.axis_size("dp")
    parts = lax.all_to_all(block.reshape(devices, -1, 128), "dp", 0, 0, tiled=True)
    partial = target_partial(
        after(self_rng, block), self_inproj, [s[0] for s in selfs], dh1, tgt_keep, tgt_got
    )
    flow_b.end(partial)
    flow_b.begin()
    parts = after(parts, partial, flow_b.state(), tgt_get)
    part = jnp.sum(parts.astype(F32), axis=0).astype(BF16)
    flow_b.end(part)
    flow_b.begin()
    spread_part = after(jnp.broadcast_to(part[None], parts.shape), flow_b.state())
    whole = lax.all_to_all(spread_part, "dp", 0, 0, tiled=True).reshape(-1, 128)
    flow_a.end(part)
    while not flow_a.done():
        flow_a.begin()
        flow_a.end()
    target_grad, memory_grad, expand_grad, reduce_grad, outproj_grad = first_outputs(
        after(self_rng, spread_part), partial, tgt_get, mem_keep, mem_got, mem_get, flow_a.cur,
        ffn_expand.shape[1], shards,
    )
    flow_b.end(target_grad)
    while not flow_b.done():
        flow_b.begin()
        flow_b.end()
    self_in, self_out_grad, query_grad, keyval_grad, eb_grad, pb_grad, gain_grad, shift_grad = finish(
        self_rng, after(whole, target_grad), flow_b.cur, width
    )
    return (
        layer_out[None],
        target_grad[None],
        memory_grad[None],
        self_in,
        self_out_grad,
        query_grad,
        keyval_grad,
        outproj_grad,
        expand_grad,
        reduce_grad,
        eb_grad,
        pb_grad,
        gain_grad,
        shift_grad,
    )


def solution(mesh):
    rows, shard = P("dp", "seq", None), P(None, "seq")
    in_specs = (rows, rows, rows, P("dp", None), P("dp", None), P("dp"), P("dp")) + (P(),) * 11
    out_specs = (rows, rows, rows) + (shard,) * 11
    return jax.shard_map(local, mesh=mesh, in_specs=in_specs, out_specs=out_specs, check_vma=False)
```

```python
import functools
import jax
import jax.numpy as jnp
from jax import lax
from jax.experimental import pallas as pl
from jax.experimental.pallas import tpu as pltpu
from jax.sharding import PartitionSpec as P

BF16 = jnp.bfloat16
F32 = jnp.float32
EPSILON = 1e-05
BK = 256
RT = 256
NT = (((1,), (1,)), ((), ()))
NN = (((1,), (0,)), ((), ()))
TN = (((0,), (0,)), ((), ()))


def dot(a, b, dims=NN):
    return lax.dot_general(a, b, dims, preferred_element_type=F32)


class Held:
    def __init__(self, copy, ref):
        self.copy, self.ref, self.started, self.waited = copy, ref, False, False

    def start(self):
        if not self.started:
            self.copy.start()
            self.started = True

    def get(self):
        self.start()
        if not self.waited:
            self.copy.wait()
            self.waited = True
        return self.ref


class Result:
    def __init__(self, copy, ref, both=None):
        self.copy, self.ref, self.both, self.started = copy, ref, both, False

    def send(self):
        self.copy.start()
        self.started = True


def call(body, rng, ins, outs, scratch, flops=10**7, vmem=24, loose=(), early=None):
    arrays, columns = [], []
    shapes = []
    for x in ins:
        x, cut, *shape = x if isinstance(x, tuple) else (x, None)
        arrays.append(x)
        columns.append(cut)
        if shape:
            shapes.append(shape[0])
        elif cut is None:
            shapes.append(x.shape)
        else:
            shapes.append(x.shape[1:] if isinstance(cut, int) else x.shape[:-1] + (cut.size,))
    pairs = [len(out) == 3 for out in outs]
    buffers = [((2, *out[0]) if pair else out[0], out[1]) for out, pair in zip(outs, pairs)]
    outs = [out[:2] for out, pair in zip(outs, pairs) for _ in range(1 + pair)]
    n_in, n_out, n_buf, n_scr = len(ins), len(outs), len(buffers), len(scratch)

    def kernel(rng_ref, *refs):
        hbm_in, refs = refs[:n_in], refs[n_in:]
        hbm_out, refs = refs[:n_out], refs[n_out:]
        vm_in, refs = refs[:n_in], refs[n_in:]
        vm_buf, refs = refs[:n_buf], refs[n_buf:]
        scr, refs = refs[:n_scr], refs[n_scr:]
        sem_in, sem_out = refs
        held = []
        for i, (src, dst, cut) in enumerate(zip(hbm_in, vm_in, columns)):
            if callable(cut):
                src = cut(src)
            elif isinstance(cut, int):
                src = src.at[cut]
            elif cut is not None:
                src = src.at[(slice(None),) * (len(src.shape) - 1) + (cut,)]
            held.append(Held(pltpu.make_async_copy(src, dst, sem_in.at[i]), dst))
        for x in held[:early]:
            x.start()
        parts = []
        for ref, pair in zip(vm_buf, pairs):
            parts += [(ref.at[0], ref), (ref.at[1], ref)] if pair else [(ref, None)]
        results = [
            Result(pltpu.make_async_copy(src, dst, sem_out.at[i]), src, both)
            for i, ((src, both), dst) in enumerate(zip(parts, hbm_out))
        ]
        body(rng_ref, held, results, *scr)
        for x in held:
            x.get()
        for x in results:
            if not x.started:
                x.send()
        for x in results:
            x.copy.wait()

    hbm = pl.BlockSpec(memory_space=pltpu.HBM)
    return pl.pallas_call(
        kernel,
        out_shape=tuple(pltpu.HBM(s, d) for s, d in outs),
        in_specs=[pl.BlockSpec(memory_space=pltpu.SMEM)] + [hbm] * n_in,
        out_specs=(hbm,) * n_out,
        scratch_shapes=[pltpu.VMEM(s, x.dtype) for s, x in zip(shapes, arrays)]
        + [pltpu.VMEM(s, d) for s, d in buffers]
        + [pltpu.VMEM(s, d) for s, d in scratch]
        + [pltpu.SemaphoreType.DMA((n_in,)), pltpu.SemaphoreType.DMA((n_out,))],
        compiler_params=pltpu.CompilerParams(vmem_limit_bytes=vmem * 2**20),
        cost_estimate=pl.CostEstimate(flops=flops, bytes_accessed=2**20, transcendentals=0),
    )(
        rng,
        *[
            x if any(x is y for y in loose) else pltpu.with_memory_space_constraint(x, pltpu.HBM)
            for x in arrays
        ],
    )


LO0, HI0, LO1, HI1, SHARD, VALID = range(6)


def prepare_body(
    info, lengths, t_smem, t_ref, s_ref, self_rng, cross_rng, fq_ref, self_fk, cross_fk, self_fkt, cross_fkt
):
    length = fq_ref.shape[0]
    shard = info[0]
    valid, count = lengths[0], lengths[1]
    full = t_ref.shape[1]
    t_row, s_row = t_ref[...], s_ref[...]

    def number(mask):
        return jnp.sum(jnp.where(mask, 1.0, 0.0)).astype(jnp.int32)

    for half in range(2):
        first = t_smem[0, shard * length + half * RT]
        last = t_smem[0, shard * length + half * RT + RT - 1]
        self_rng[LO0 + 2 * half] = lax.div(number(t_row < first), BK)
        self_rng[HI0 + 2 * half] = 0
        cross_rng[LO0 + 2 * half] = lax.div(number(s_row < first), BK)
        end = jnp.minimum(number(s_row <= last), count)
        cross_rng[HI0 + 2 * half] = lax.div(end + BK - 1, BK)
    for ref in (self_rng, cross_rng):
        ref[SHARD] = shard
        ref[VALID] = valid
        ref[6] = info[1]
        ref[7] = 0
    f = lax.broadcasted_iota(jnp.int32, (128, 128), 1) % 64

    def column(ref, at):
        return jnp.broadcast_to(ref[0:1, pl.ds(pl.multiple_of(at, 128), 128)], (128, 128)).T

    row = lax.broadcasted_iota(jnp.int32, (128, 128), 0)
    for m in range(full // length):
        for t in range(0, length, 128):
            at = (shard ^ m) * length + t
            for ref, total, out, out_t in ((t_ref, valid, self_fk, self_fkt), (s_ref, count, cross_fk, cross_fkt)):
                seg = column(ref, at)
                seen = (seg == f) & (row + at < total)
                feature = jnp.where(
                    f < 8, jnp.where(seen, 0.0, -1e30), jnp.where(f < 11, 1.0, 0.0)
                )
                out[m * length + t : m * length + t + 128] = feature.astype(BF16)
                out_t[:, m * length + t : m * length + t + 128] = feature.astype(BF16).T[0:64]
                if m == 0 and out is self_fk:
                    fq_ref[t : t + 128] = jnp.where(seg == f, 1.0, 0.0).astype(BF16)


def prepare(shard, target_length, source_length, target_segments, source_segments, length):
    full = target_segments.shape[1]
    sd = jax.ShapeDtypeStruct
    smem, vm = pl.BlockSpec(memory_space=pltpu.SMEM), pl.BlockSpec(memory_space=pltpu.VMEM)
    return pl.pallas_call(
        prepare_body,
        out_shape=(
            sd((8,), jnp.int32), sd((8,), jnp.int32), sd((length, 128), BF16), sd((full, 128), BF16),
            sd((full, 128), BF16), sd((64, full), BF16), sd((64, full), BF16),
        ),
        in_specs=[smem, smem, smem, vm, vm],
        out_specs=(smem, smem, vm, vm, vm, vm, vm),
    )(
        jnp.stack([shard, lax.axis_index("dp").astype(jnp.int32) & 1]),
        jnp.concatenate([target_length, source_length]), target_segments,
        target_segments, source_segments,
    )


def start_all(held):
    for x in held:
        x.start()


def half_masks():
    lane = lax.broadcasted_iota(jnp.int32, (1, 128), 1)
    return (lane < 64, lane >= 64), lane % 64


def relative_offset(block, shard, per_shard):
    owner = lax.div(block, per_shard)
    return pl.multiple_of(((owner ^ shard) * per_shard + lax.rem(block, per_shard)) * BK, BK)


def triangle(transposed):
    a = lax.broadcasted_iota(jnp.int32, (BK, BK), 0)
    b = lax.broadcasted_iota(jnp.int32, (BK, BK), 1)
    return a <= b if transposed else b <= a


def attend(rng, q_ref, fq_ref, kt, v_ref, fkt_ref, o_ref, lse_ref, qh, s_even, s_odd, mx_even, mx_odd, acc, causal):
    length, width = q_ref.shape
    per = length // BK
    pairs = width // 128
    shard = rng[SHARD]
    conds, _ = half_masks()
    lo0, hi0, lo1, hi1 = rng[LO0], rng[HI0], rng[LO1], rng[HI1]
    both, upper, lower = slice(0, length), slice(0, RT), slice(RT, length)
    s_bank, mx_bank = (s_even, s_odd), (mx_even, mx_odd)

    def scores(g, off, slot, rows, diagonal):
        s_scr, mx = s_bank[g % 2], mx_bank[g % 2]
        mask = fkt_ref[0:64, pl.ds(off, BK)]
        for h in range(2):
            at = g * 128 + 64 * h
            mine = kt[at : at + 64, pl.ds(off, BK)]
            w = jnp.concatenate([mine, mask] if h == 0 else [mask, mine], axis=0)
            s = dot(qh[h, rows], w)
            if diagonal:
                n = rows.stop - rows.start
                a = lax.broadcasted_iota(jnp.int32, (n, BK), 0)
                b = lax.broadcasted_iota(jnp.int32, (n, BK), 1)
                s = jnp.where(b <= a, s, -1e30)
            s_scr[h, slot, rows] = s
            m = mx[h, rows]
            for t in range(0, BK, 128):
                m = jnp.maximum(m, s[:, t : t + 128])
            mx[h, rows] = m

    def values(g, off, slot, rows):
        s_scr, mx = s_bank[g % 2], mx_bank[g % 2]
        for h in range(2):
            vp = v_ref[pl.ds(off, BK), g * 128 : g * 128 + 128]
            vh = jnp.where(conds[h], vp, jnp.ones_like(vp))
            m = mx[h, rows]
            p = jnp.concatenate(
                [
                    jnp.exp(s_scr[h, slot, rows, t : t + 128] - m).astype(BF16)
                    for t in range(0, BK, 128)
                ],
                axis=1,
            )
            acc[h, rows] += dot(p, vh)

    def sweep(f):
        def span(lo, hi, rows, unroll=1):
            def step(kb, carry):
                f(relative_offset(kb, shard, per), kb, rows, False)
                return carry

            def steps(i, carry):
                for j in range(unroll):
                    step(lo + unroll * i + j, carry)
                return carry

            if unroll > 1:
                turns = lax.div(jnp.maximum(hi - lo, 0), unroll)
                lax.fori_loop(0, turns, steps, 0)
                lo = lo + unroll * turns
            lax.fori_loop(lo, hi, step, 0)

        if causal:
            own = shard * per
            span(lo0, jnp.minimum(lo1, own), upper, 2)
            span(lo1, own, both, 2)
            f(0, own, both, True)
            f(BK, own + 1, lower, True)
        else:
            span(lo0, jnp.minimum(lo1, hi0), upper)
            span(lo1, hi0, both, 2)
            span(jnp.maximum(hi0, lo1), hi1, lower)

    def start(g):
        mx = mx_bank[g % 2]
        cols = slice(g * 128, g * 128 + 128)
        for h in range(2):
            qh[h] = jnp.where(conds[h], q_ref[:, cols], fq_ref[...])
            mx[h] = jnp.full((length, 128), -3e38, F32)

    def turn(g):
        mx = mx_bank[g % 2]
        for h in range(2):
            for r in range(0, length, 128):
                rows = slice(r, r + 128)
                top = jnp.max(mx[h, rows], axis=-1, keepdims=True)
                mx[h, rows] = jnp.broadcast_to(top, (128, 128))
                acc[h, rows] = jnp.zeros((128, 128), F32)

    def finish(g):
        mx = mx_bank[g % 2]
        cols = slice(g * 128, g * 128 + 128)
        for r in range(0, length, 128):
            rows = slice(r, r + 128)
            a0, a1 = acc[0, rows], acc[1, rows]
            num = jnp.where(conds[0], a0, a1)
            den = jnp.where(conds[0], a1, a0)
            o_ref[rows, cols] = (num / pltpu.roll(den, 64, 1)).astype(BF16)
            lse_ref[g, rows] = jnp.where(conds[0], mx[1, rows], mx[0, rows]) + jnp.log(den)

    start(0)
    sweep(lambda off, slot, rows, edge: scores(0, off, slot, rows, edge))

    for g in range(1, pairs):
        turn(g - 1)
        start(g)

        def pair(off, slot, rows, edge, g=g):
            scores(g, off, slot, rows, edge)
            values(g - 1, off, slot, rows)

        sweep(pair)
        finish(g - 1)
    turn(pairs - 1)
    sweep(lambda off, slot, rows, edge: values(pairs - 1, off, slot, rows))
    finish(pairs - 1)


def attend_scratch(length, full):
    return [
        ((2, length, 128), BF16),
        ((2, full // BK, length, BK), F32),
        ((2, full // BK, length, BK), F32),
        ((2, length, 128), F32),
        ((2, length, 128), F32),
        ((2, length, 128), F32),
    ]


def attend_back(rng, q, fq, logsum, do, o, keys, dkv_ref, qh, doh, qm, dom, dq_scr, causal):
    length = q.shape[0]
    per = length // BK
    shard = rng[SHARD]
    conds, l64 = half_masks()

    def negated_parts(x):
        high = x.astype(BF16).astype(F32)
        rest = x - high
        mid = rest.astype(BF16).astype(F32)
        low = rest - mid
        return -jnp.where(
            l64 == 8, high, jnp.where(l64 == 9, mid, jnp.where(l64 == 10, low, 0.0))
        )

    for r in range(0, length, 128):
        rows = slice(r, r + 128)
        q_r, do_r = q[rows], do[rows]
        prod = do_r.astype(F32) * o[rows].astype(F32)
        delta = jnp.where(
            conds[0],
            jnp.sum(jnp.where(conds[1], prod, 0.0), axis=-1, keepdims=True),
            jnp.sum(jnp.where(conds[0], prod, 0.0), axis=-1, keepdims=True),
        )
        fl = (negated_parts(logsum[rows]) + fq[rows].astype(F32)).astype(BF16)
        fd = negated_parts(delta).astype(BF16)
        zero = jnp.zeros_like(q_r)
        for h in range(2):
            qh[h, :, rows] = jnp.where(conds[h], q_r, fl).T
            doh[h, :, rows] = jnp.where(conds[h], do_r, fd).T
            qm[h, rows] = jnp.where(conds[h], q_r, zero)
            dom[h, rows] = jnp.where(conds[h], do_r, zero)
    dq_scr[...] = jnp.zeros_like(dq_scr)
    ones = jnp.where((l64 >= 8) & (l64 <= 10), 1.0, 0.0).astype(BF16)
    k_ref, v_ref, fk_ref = (x.get() for x in keys)

    def block(off, halves, diagonal=None, size=BK):
        kp = k_ref[pl.ds(off, size), :]
        vp = v_ref[pl.ds(off, size), :]
        fk = fk_ref[pl.ds(off, size), :]
        ones_block = jnp.broadcast_to(ones, vp.shape)
        kt = kp.T
        dk = jnp.zeros((size, 128), F32)
        dv = jnp.zeros((size, 128), F32)
        for h in range(2):
            kh = jnp.where(conds[h], kp, fk)
            vh = jnp.where(conds[h], vp, ones_block)
            rows = slice(64 * h, 64 * h + 64)
            for half in halves:
                r = half * RT
                s = dot(kh, qh[h, :, r : r + RT])
                if diagonal == half:
                    s = jnp.where(triangle(True), s, -1e30)
                p = jnp.exp(s)
                dp = dot(vh, doh[h, :, r : r + RT])
                ds = (p * dp).astype(BF16)
                dv += dot(p.astype(BF16), dom[h, r : r + RT])
                dk += dot(ds, qm[h, r : r + RT])
                dq_scr[rows, r : r + RT] += dot(kt[rows], ds)
        dkv_ref[pl.ds(off, size), 0:128] = dk.astype(BF16)
        dkv_ref[pl.ds(off, size), 128:256] = dv.astype(BF16)

    def sweep(lo, hi, halves):
        def step(kb, carry):
            block(relative_offset(kb, shard, per), halves)
            return carry

        lax.fori_loop(lo, hi, step, 0)

    def sweep_two(lo, hi, halves):
        first = lax.div(lo + 1, 2)
        last = lax.div(hi, 2)

        def step(kb, carry):
            block(relative_offset(2 * kb, shard, per), halves, size=2 * BK)
            return carry

        lax.fori_loop(first, last, step, 0)
        sweep(lo, jnp.minimum(2 * first, hi), halves)
        sweep(jnp.maximum(2 * last, 2 * first), hi, halves)

    lo0, lo1 = rng[LO0], rng[LO1]
    common = sweep_two
    if causal:
        own = shard * per
        sweep_two(lo0, jnp.minimum(lo1, own), (0,))
        common(lo1, own, (0, 1))
        block(0, (0, 1), 0)
        block(BK, (1,), 1)
    else:
        hi0, hi1 = rng[HI0], rng[HI1]
        sweep(lo0, jnp.minimum(lo1, hi0), (0,))
        common(lo1, hi0, (0, 1))
        sweep(jnp.maximum(hi0, lo1), hi1, (1,))
    return dq_scr[...].T * 0.125


def norm_rows(hidden):
    center = hidden - jnp.mean(hidden, axis=-1, keepdims=True)
    spread = lax.rsqrt(jnp.mean(center * center, axis=-1, keepdims=True) + EPSILON)
    return center * spread, spread


def norm_rows_back(upstream, normed, spread, gain):
    scaled = upstream * gain
    return spread * (
        scaled
        - jnp.mean(scaled, axis=-1, keepdims=True)
        - normed * jnp.mean(scaled * normed, axis=-1, keepdims=True)
    )


def put_block(both, m, rows, value):
    both[m % 2, m // 2, rows] = value


def put_far(both, m, rows, value):
    both[m // 2, m % 2, rows] = value


def row_of(ref, i):
    return ref[i : i + 1, :].astype(F32)


def self_body(rng, held, results, qh, s_even, s_odd, mx_even, mx_odd, acc, kt, a_low):
    x0, win, pb, x1, x2, x3, fq, fkt, wout, wq, gain, shift = held
    q, k, v, o, lse, a, n_out, r_out, q2_out, xt, at_out = results
    length, width = x0.ref.shape
    shard = rng[SHARD]
    eighth = jnp.asarray(0.125, BF16)
    x_ref, win_ref, pb_ref = x0.get(), win.get(), pb.get()
    start_all(held)
    q.ref[...] = (dot(x_ref[...], win_ref[:, :width]) + row_of(pb_ref, 0)).astype(BF16) * eighth
    q.send()
    for m, x in enumerate((x0, x1, x2, x3)):
        x_m = x.get()

        def fill(m=m, x_m=x_m):
            x = x_m[...]
            rows = slice(m * length, (m + 1) * length)
            for c in range(0, width, 256):
                cols = slice(c, c + 256)
                k_new = dot(x, win_ref[:, width + c : width + c + 256]).astype(BF16)
                k.ref[rows, cols] = k_new
                kt[cols, rows] = k_new.T
                v_new = dot(x, win_ref[:, 2 * width + c : 2 * width + c + 256])
                v.ref[rows, cols] = (v_new + pb_ref[1:2, cols].astype(F32)).astype(BF16)
            xt.ref[:, rows] = x.T

        if m == 0:
            fill()
        else:
            pl.when((shard ^ m) < shard)(fill)
    k.send()
    v.send()
    xt.send()
    attend(rng, q.ref, fq.get(), kt, v.ref, fkt.get(), o.ref, lse.ref, qh, s_even, s_odd, mx_even, mx_odd, acc, True)
    o.send()
    lse.send()
    wout_ref, wq_ref, gain_ref, shift_ref = wout.get(), wq.get(), gain.get(), shift.get()
    for c in range(0, width, 256):
        cols = slice(c, c + 256)
        h = x_ref[:, cols].astype(F32) + dot(o.ref[...], wout_ref[:, cols])
        n_out.ref[:, cols] = h + pb_ref[2:3, cols].astype(F32)
    for r in range(0, length, 128):
        rows = slice(r, r + 128)
        n, spread = norm_rows(n_out.ref[rows])
        a_new = n * row_of(gain_ref, 0) + row_of(shift_ref, 0)
        n_out.ref[rows] = n
        r_out.ref[rows] = jnp.broadcast_to(spread, (128, 128))
        a.ref[rows] = a_new
        a_low[rows] = a_new.astype(BF16)
    n_out.send()
    a.send()
    at_out.ref[...] = a_low[...].T
    for c in range(0, width, 256):
        cols = slice(c, c + 256)
        q2 = dot(a_low[...], wq_ref[:, cols]) + pb_ref[3:4, cols].astype(F32)
        q2_out.ref[:, cols] = q2.astype(BF16) * eighth


def self_forward(rng, parts, fq, fkt, win, wout, wq, pb, gain, shift):
    length, width = parts[0].shape
    full = len(parts) * length
    return call(
        self_body,
        rng,
        [parts[0], win, pb, *parts[1:], fq, fkt, wout, wq, gain, shift],
        [
            ((length, width), BF16), ((full, width), BF16), ((full, width), BF16),
            ((length, width), BF16), ((width // 128, length, 128), F32), ((length, width), F32),
            ((length, width), F32), ((length, 128), F32), ((length, width), BF16), ((width, full), BF16),
            ((width, length), BF16),
        ],
        attend_scratch(length, full) + [((width, full), BF16), ((length, width), BF16)],
        flops=10**7,
        vmem=40,
        loose=parts[1:],
        early=6,
    )


GELU_A = 0.7978845608028654
GELU_B = 0.044715


def cross_body(rng, held, results, qh, s_even, s_odd, mx_even, mx_odd, acc, kt, n1, r1, a2, a2_low, act, y_scr, dy_scr):
    wkv, pb, y0, y1, y2, y3, q, fq, fkt, wout, a1, gain, shift, w1, w2, eb, cot = held
    k, v, o, lse, out, do, dh, keep, send, deb, small, yt = results
    length, width = q.ref.shape
    shard = rng[SHARD]
    wkv_ref, pb_ref = wkv.get(), pb.get()
    for m, y in enumerate((y0, y1, y2, y3)):
        y_ref = y.get()
        if m == 1:
            start_all(held)
        x = y_ref[...]
        rows = slice(m * length, (m + 1) * length)
        for c in range(0, width, 256):
            cols = slice(c, c + 256)
            k_new = dot(x, wkv_ref[:, cols]).astype(BF16)
            k.ref[rows, cols] = k_new
            kt[cols, rows] = k_new.T
            v_new = dot(x, wkv_ref[:, width + c : width + c + 256])
            v.ref[rows, cols] = (v_new + pb_ref[4:5, cols].astype(F32)).astype(BF16)
        yt.ref[:, rows] = x.T
    k.send()
    v.send()
    yt.send()
    attend(rng, q.get(), fq.get(), kt, v.ref, fkt.get(), o.ref, lse.ref, qh, s_even, s_odd, mx_even, mx_odd, acc, False)
    o.send()
    lse.send()
    wout_ref, a1_ref, gain_ref, shift_ref = wout.get(), a1.get(), gain.get(), shift.get()
    for c in range(0, width, 256):
        cols = slice(c, c + 256)
        y_scr[:, cols] = a1_ref[:, cols] + (dot(o.ref[...], wout_ref[:, cols]) + pb_ref[5:6, cols].astype(F32))
    for r in range(0, length, 128):
        rows = slice(r, r + 128)
        n, spread = norm_rows(y_scr[rows])
        n1[rows] = n
        r1[rows] = jnp.broadcast_to(spread, (128, 128))
        a2[rows] = n * row_of(gain_ref, 1) + row_of(shift_ref, 1)
    y_scr[...] = jnp.zeros_like(y_scr)
    a2_low[...] = a2[...].astype(BF16)
    kt[:, 0:length] = a2_low[...].T
    w1_ref, w2_ref, eb_ref, cot_ref = w1.get(), w2.get(), eb.get(), cot.get()
    inner = w1_ref.shape[1]
    chunks = inner // width

    def expand(c):
        cols = slice(c * width, (c + 1) * width)
        for t in range(0, width, 256):
            half_cols = slice(c * width + t, c * width + t + 256)
            u = dot(a2_low[...], w1_ref[:, half_cols]) + eb_ref[0:1, half_cols].astype(F32)
            square = u * u
            th = jnp.tanh(u * (GELU_A + (GELU_A * GELU_B) * square))
            half = 0.5 * th + 0.5
            act[c, :, t : t + 256] = (u * half).astype(BF16)
            slope = (u - u * (th * th)) * (0.5 * GELU_A + (1.5 * GELU_A * GELU_B) * square)
            s_even[t // 256, c] = half + slope
        y_scr[...] += dot(act[c], w2_ref[cols, :])

    for c in range(chunks):
        expand(c)
    zero = jnp.zeros((1, width), F32)
    db5, db6, dg1, ds1, dg2, ds2 = (zero,) * 6
    for r in range(0, length, 128):
        rows = slice(r, r + 128)
        n, spread = norm_rows(a2[rows] + y_scr[rows] + row_of(pb_ref, 6))
        out.ref[rows] = (n * row_of(gain_ref, 2) + row_of(shift_ref, 2)).astype(BF16)
        position = shard * length + r + lax.broadcasted_iota(jnp.int32, (128, 1), 0)
        g = jnp.where(position < rng[VALID], cot_ref[rows].astype(F32), 0.0)
        dg2 += jnp.sum(g * n, axis=0, keepdims=True)
        ds2 += jnp.sum(g, axis=0, keepdims=True)
        dh3 = norm_rows_back(g, n, spread, row_of(gain_ref, 2))
        dy3 = dh3.astype(BF16)
        db6 += jnp.sum(dy3.astype(F32), axis=0, keepdims=True)
        dy_scr[rows] = dy3
        y_scr[rows] = dh3
    out.send()

    parts = width // 128

    def contract(c):
        cols = slice(c * width, (c + 1) * width)
        dus = []
        for t in range(0, width, 256):
            half_cols = slice(c * width + t, c * width + t + 256)
            du = (s_even[t // 256, c] * dot(dy_scr[...], w2_ref[half_cols, :], NT)).astype(BF16)
            deb.ref[0:1, half_cols] = jnp.sum(du.astype(F32), axis=0, keepdims=True)
            dus.append(du)
        du = jnp.concatenate(dus, axis=1)
        y_scr[...] += dot(du, w1_ref[:, cols], NT)
        g1 = dot(kt[:, 0:length], du)
        for j in range(parts):
            put_block(
                keep.both, c ^ shard, slice(inner + j * width, inner + (j + 1) * width),
                g1[:, j * 128 : (j + 1) * 128].astype(BF16),
            )
        g2 = dot(act[c], dy_scr[...], TN)
        at = slice(c * width, (c + 1) * width)
        for b in range(4):
            put_block(keep.both, shard ^ b, at, g2[:, b * 128 : (b + 1) * 128].astype(BF16))

    for c in range(chunks):
        contract(c)
    for r in range(0, length, 128):
        rows = slice(r, r + 128)
        up = y_scr[rows]
        n = n1[rows]
        dg1 += jnp.sum(up * n, axis=0, keepdims=True)
        ds1 += jnp.sum(up, axis=0, keepdims=True)
        dh2 = norm_rows_back(up, n, r1[rows, 0:1], row_of(gain_ref, 1))
        dh.ref[rows] = dh2
        dy2 = dh2.astype(BF16)
        dy_scr[rows] = dy2
        db5 += jnp.sum(dy2.astype(F32), axis=0, keepdims=True)
    dh.send()
    for c in range(0, width, 256):
        cols = slice(c, c + 256)
        do.ref[:, cols] = dot(dy_scr[...], wout_ref[cols, :], NT).astype(BF16)
    do.send()
    g3 = dot(o.ref[...], dy_scr[...], TN)
    for b in range(4):
        put_block(
            keep.both, shard ^ b, slice(2 * inner, 2 * inner + width),
            g3[:, b * 128 : (b + 1) * 128].astype(BF16),
        )
    for i, value in enumerate((db5, db6, dg1, dg2, ds1, ds2)):
        small.ref[i : i + 1, :] = value
    small.ref[6:8, :] = jnp.zeros((2, width), F32)


def cross_forward(rng, parts, fq, fkt, q, a1, cot, wkv, wout, w1, w2, eb, pb, gain, shift):
    length, width = q.shape
    full, inner = len(parts) * length, w1.shape[1]
    return call(
        cross_body,
        rng,
        [wkv, pb, *parts, q, fq, fkt, wout, a1, gain, shift, w1, w2, eb, cot],
        [
            ((full, width), BF16), ((full, width), BF16), ((length, width), BF16),
            ((width // 128, length, 128), F32), ((length, width), BF16), ((length, width), BF16),
            ((length, width), F32), ((2, 2 * inner + width, 128), BF16, 2), ((1, inner), F32),
            ((8, width), F32), ((width, full), BF16),
        ],
        attend_scratch(length, full)
        + [
            ((width, full), BF16),
            ((length, width), F32), ((length, 128), F32), ((length, width), F32), ((length, width), BF16),
            ((inner // width, length, width), BF16),
            ((length, width), F32), ((length, width), BF16),
        ],
        flops=10**7,
        vmem=57,
        loose=parts[1:],
        early=6,
    )


def back_body(rng, held, results, qh, doh, qm, dom, dq_scr, w_scr, c_scr, *more_scr, causal, pack, pairs):
    first, second, shared = held[:8], held[8 : 6 * pairs + 2], held[6 * pairs + 2 :]
    xq, xt = shared[:2]
    fq, fk = held[1], held[7]
    shard = rng[SHARD]
    groups = [(held[0], held[2], held[3], held[4], held[5], held[6])]
    if pairs == 2:
        groups.append(tuple(second))
    for i, (q, lse, do, o, k, v) in enumerate(groups):
        dq_out, dkv, w, small = results[4 * i : 4 * i + 4]
        length = q.ref.shape[0]
        dkv.ref[...] = jnp.zeros_like(dkv.ref)
        own = [x.get() for x in (q, fq, lse, do, o)]
        start_all(held)
        dq = attend_back(rng, *own, (k, v, fk), dkv.ref, qh, doh, qm, dom, dq_scr, causal).astype(BF16)
        dkv.send()
        dq_out.ref[...] = dq
        dq_out.send()
        w.ref[0] = dot(xq.get()[...], dq).astype(BF16)
        w_scr[...] = jnp.zeros_like(w_scr)
        c_scr[...] = jnp.zeros_like(c_scr)
        xt_ref = xt.get()
        for m in range(xt_ref.shape[1] // length):

            def more(m=m):
                span = slice(m * length, (m + 1) * length)
                part = dkv.ref[span, :]
                w_scr[...] += dot(xt_ref[:, span], part)
                c_scr[...] += jnp.sum(part[:, 128:].astype(F32), axis=0, keepdims=True)

            if causal and m:
                pl.when((shard ^ m) < shard)(more)
            else:
                more()
        w.ref[1] = w_scr[:, :128].astype(BF16)
        w.ref[2] = w_scr[:, 128:].astype(BF16)
        small.ref[0:1, :] = jnp.sum(dq.astype(F32), axis=0, keepdims=True)
        small.ref[1:2, :] = c_scr[0:1]
        small.ref[2:8, :] = jnp.zeros((6, 128), F32)
        w.send()
    if pack is not None:
        own = [[x.ref for x in results[4 * i : 4 * i + 4]] for i in range(pairs)]
        pack(rng, shared[2:], own, results[4 * pairs :], *more_scr)


def pack_memory(rng, others, own, outs, dy_scr):
    wkv, dkv0, dkv1, dq0, dq1, u0, u1, wq, dh2, n0, r0, gain, wout, o = others
    mem_keep, mem_send, dh, do, keep, send, small = outs
    parts = [dkv0.get(), dkv1.get(), own[0][1], own[1][1]]
    shard = rng[SHARD]
    for m in (1, 3, 0, 2):
        spread_block(parts, wkv.get(), 0, m, (mem_keep, mem_send)[m % 2].ref)
    mem_keep.send()
    mem_send.send()
    length, width = dh2.ref.shape
    pairs = width // 128
    zero = jnp.zeros((1, width), F32)
    db2, dg0, ds0 = zero, zero, zero
    dq_refs = [dq0.get(), dq1.get(), own[0][0], own[1][0]]
    dq = jnp.concatenate([d[...] for d in dq_refs], axis=1)
    wq_ref, dh2_ref, n_ref, r_ref, gain_ref, wout_ref = (x.get() for x in (wq, dh2, n0, r0, gain, wout))
    for c in range(0, width, 256):
        cols = slice(c, c + 256)
        dh.ref[:, cols] = dh2_ref[:, cols] + dot(dq, wq_ref[cols, :], NT)
    for r in range(0, length, 128):
        rows = slice(r, r + 128)
        up = dh.ref[rows]
        n = n_ref[rows]
        dg0 += jnp.sum(up * n, axis=0, keepdims=True)
        ds0 += jnp.sum(up, axis=0, keepdims=True)
        new = norm_rows_back(up, n, r_ref[rows, 0:1], row_of(gain_ref, 0))
        dh.ref[rows] = new
        dy = new.astype(BF16)
        dy_scr[rows] = dy
        db2 += jnp.sum(dy.astype(F32), axis=0, keepdims=True)
    dh.send()
    for c in range(0, width, 256):
        cols = slice(c, c + 256)
        do.ref[:, cols] = dot(dy_scr[...], wout_ref[cols, :], NT).astype(BF16)
    do.send()
    g = dot(o.get()[...], dy_scr[...], TN)
    for b in range(4):
        put_block(keep.both, shard ^ b, slice(0, width), g[:, b * 128 : (b + 1) * 128].astype(BF16))
    units = [u0.get(), u1.get(), own[0][2], own[1][2]]
    for b in range(4):
        put_block(keep.both, shard ^ b, slice(width, 2 * width), units[b][0])
    for i in range(2 * pairs):
        b, at = i // 2, 2 + i % 2
        put_block(keep.both, shard ^ b, slice(at * width, (at + 1) * width), units[i % pairs][1 + i // pairs])
    for i, value in enumerate((db2, dg0, ds0)):
        small.ref[i : i + 1, :] = value
    small.ref[3:8, :] = jnp.zeros((5, width), F32)


def pack_early(rng, others, own, outs):
    w0, w1 = (x.get() for x in others)
    w = own[0][2]
    both = outs[0].both
    width = w.shape[1]
    for b, columns in enumerate(((w0[0], w1[0]), (w0[1], w1[1]), (w[1], w0[2]), (w1[2], w[2]))):
        for at, value in enumerate(columns):
            put_far(both, rng[SHARD] ^ b, slice(at * width, (at + 1) * width), value)


def pack_late(rng, others, own, outs):
    w2, a0, a1, a2, b0, b1, b2, b3, s0_ref, s2_ref, deb_ref = (x.get() for x in others)
    w, small = own[0][2:]
    both = outs[0].both
    width = w.shape[1]
    own_small, other = (a0, a1, a2, small), (b0, b1, b2, b3)
    for b, value in enumerate((w2[0], w[0], w[1], w[2])):
        put_block(both, rng[SHARD] ^ b, slice(0, width), value)
    pad = both.shape[2] - width
    for b in range(4):
        cols = slice(b * 128, (b + 1) * 128)
        rows = [deb_ref[0:1, b * width + j * 128 : b * width + (j + 1) * 128] for j in range(width // 128)]
        rows += [own_small[b][0:1], own_small[b][1:2], s0_ref[0:1, cols], other[b][0:1], other[b][1:2]]
        rows += [s2_ref[0:1, cols], s2_ref[1:2, cols]]
        rows += [s0_ref[1:2, cols], s2_ref[2:3, cols], s2_ref[3:4, cols]]
        rows += [s0_ref[2:3, cols], s2_ref[4:5, cols], s2_ref[5:6, cols]]
        rows.append(jnp.zeros((pad - len(rows), 128), F32))
        put_block(both, rng[SHARD] ^ b, slice(width, width + pad), jnp.concatenate(rows, axis=0).astype(BF16))


def attend_backward(rng, pairs, q, fq, lse, do, o, fk, k, v, xq, xt, causal, pack=None, extra=(), packed=(), more=(), vmem=22):
    length, width = q.shape
    full = k.shape[0]
    ins, outs = [], []
    for i, p in enumerate(pairs):
        cut = pl.ds(p * 128, 128)
        if i == 0:
            ins += [(q, cut), fq, (lse, p), (do, cut), (o, cut), (k, cut), (v, cut), fk]
        else:
            ins += [(q, cut), (lse, p), (do, cut), (o, cut), (k, cut), (v, cut)]
        outs += [((length, 128), BF16), ((full, 256), BF16), ((3, width, 128), BF16), ((8, 128), F32)]
    if pack is not None:
        outs += list(packed)
    out = call(
        functools.partial(back_body, causal=causal, pack=pack, pairs=len(pairs)),
        rng,
        [*ins, (xq, pl.ds(0, length)), xt, *extra],
        outs,
        [((2, 128, length), BF16)] * 2
        + [((2, length, 128), BF16)] * 2
        + [((128, length), F32), ((width, 256), F32), ((8, 128), F32), *more],
        flops=10**7,
        vmem=vmem,
        early=8,
    )
    return [out[4 * i : 4 * i + 4] for i in range(len(pairs))] + [out[4 * len(pairs) :]]


def spread_block(parts, w_ref, offset, m, ref):
    length, width = ref.shape[1:]
    rows = slice(m * length, (m + 1) * length)
    dk = jnp.concatenate([d[rows, :128] for d in parts], axis=1)
    dv = jnp.concatenate([d[rows, 128:] for d in parts], axis=1)
    for c in range(0, width, 256):
        cols = slice(c, c + 256)
        total = dot(dk, w_ref[cols, offset : offset + width], NT)
        total += dot(dv, w_ref[cols, offset + width : offset + 2 * width], NT)
        ref[m // 2, :, cols] = total.astype(BF16)


def spread_body(rng, held, results, *, causal, offset):
    keep, send = results
    shard = rng[SHARD]
    refs = [x.get() for x in held]
    w_ref, parts = refs[0], refs[1:]
    for m in (1, 3, 0, 2):
        ref = (keep.ref, send.ref)[m % 2]

        def fill(m=m, ref=ref):
            spread_block(parts, w_ref, offset, m, ref)

        def clear(m=m, ref=ref):
            ref[m // 2] = jnp.zeros_like(ref[m // 2])

        if causal and m:
            pl.when((shard ^ m) < shard)(fill)
            pl.when((shard ^ m) > shard)(clear)
        else:
            fill()
        if m == 3:
            send.send()


def spread_keys(rng, dkvs, w, length, causal, offset):
    width = w.shape[0]
    return call(
        functools.partial(spread_body, causal=causal, offset=offset),
        rng,
        [w, *dkvs],
        [((2, length, width), BF16), ((2, length, width), BF16)],
        [],
        flops=10**7,
    )


def partial_body(rng, held, results):
    wq, dq0, dq1, dq2, dq3, dh, near, got = held
    total = results[0].ref
    width = total.shape[1]
    dq = jnp.concatenate([x.get()[...] for x in (dq0, dq1, dq2, dq3)], axis=1)
    wq_ref, dh_ref, near_ref, got_ref = (x.get() for x in (wq, dh, near, got))
    for c in range(0, width, 256):
        cols = slice(c, c + 256)
        total[:, cols] = (
            dh_ref[:, cols]
            + dot(dq, wq_ref[cols, :], NT)
            + (near_ref[:, cols].astype(F32) + got_ref[:, cols].astype(F32))
        )


def target_partial(rng, win, dqs, dh, near, got):
    length, width = dh.shape
    return call(
        partial_body,
        rng,
        [(win, pl.ds(0, width)), *dqs, dh, (near, 0), (got, 0)],
        [((length, width), F32)],
        [],
        flops=20 * 10**9,
        loose=[got],
    )[0]


def outputs_body(rng, held, results):
    part, far_t, near, got, far_m, sums = held
    target_grad, memory_grad, expand, reduce, outproj = results
    part_ref, far_ref = part.get(), far_t.get()
    target_grad.ref[...] = part_ref[...] + far_ref[...].astype(F32)
    target_grad.send()
    near_ref, got_ref, far_ref = near.get(), got.get(), far_m.get()
    memory_grad.ref[...] = near_ref[...].astype(F32) + got_ref[...].astype(F32) + far_ref[...].astype(F32)
    memory_grad.send()
    sums_ref = sums.get()
    inner = reduce.ref.shape[0]
    width = expand.ref.shape[0]
    reduce.ref[...] = sums_ref[0:inner].astype(F32)
    reduce.send()
    for j in range(expand.ref.shape[1] // 128):
        rows = slice(inner + j * width, inner + (j + 1) * width)
        expand.ref[:, j * 128 : (j + 1) * 128] = sums_ref[rows].astype(F32)
    expand.send()
    outproj.ref[...] = sums_ref[2 * inner : 2 * inner + width].astype(F32)


def first_outputs(rng, part, far_t, near, got, far_m, sums, inner, shards):
    length, width = part.shape
    return call(
        outputs_body,
        rng,
        [part, far_t, (near, 0), (got, 0), far_m, sums],
        [
            ((length, width), F32), ((length, width), F32), ((width, inner // shards), F32), ((inner, 128), F32),
            ((width, 128), F32),
        ],
        [],
        flops=20 * 10**9,
        loose=[far_t, got, far_m, sums],
    )


def finish_body(rng, held, results):
    sums = held[1].get()
    w, outproj, query, keyval, eb, pb, gain, shift = (r.ref for r in results)
    width = w.shape[0]
    shard = rng[SHARD]
    outproj[...] = sums[0:width].astype(F32)
    query[...] = sums[width : 2 * width].astype(F32)
    for j in range(keyval.shape[1] // 128):
        keyval[:, j * 128 : (j + 1) * 128] = sums[(2 + j) * width : (3 + j) * width].astype(F32)
    for x in results[1:4]:
        x.send()
    total = held[0].get()
    second = jnp.where(shard == 1, 0, jnp.where(shard == 2, 2, 1))
    third = jnp.where((shard == 1) | (shard == 2), 1, 2)
    for j, at in enumerate((jnp.where(shard == 1, 2, 0), second, third)):
        rows = pl.ds(pl.multiple_of(at * width, width), width)
        w[:, j * 128 : (j + 1) * 128] = total[rows].astype(F32)
    results[0].send()
    rest = total[3 * width : 3 * width + 32].astype(F32)
    for j in range(width // 128):
        eb[0:1, j * 128 : (j + 1) * 128] = rest[j : j + 1]
    pb[...] = rest[4:11]
    gain[...] = rest[11:14]
    shift[...] = rest[14:17]


def finish(rng, total, sums, width):
    return call(
        finish_body,
        rng,
        [total, sums],
        [
            ((width, 384), F32), ((width, 128), F32), ((width, 128), F32), ((width, 256), F32), ((1, width), F32),
            ((7, 128), F32), ((3, 128), F32), ((3, 128), F32),
        ],
        [],
        loose=[total, sums],
    )


def first_body(rng, held, results):
    keep_far, got_far, keep_rest, got_rest = held
    far, rest = results
    far.ref[...] = (keep_far.get()[...].astype(F32) + got_far.get()[...].astype(F32)).astype(BF16)
    far.send()
    half = rest.ref.shape[1]
    keep_ref, got_ref = keep_rest.get(), got_rest.get()
    rows = pl.ds(pl.multiple_of((1 - rng[6]) * half, 128), half)
    for m in range(2):
        rest.ref[m] = (keep_ref[m, rows].astype(F32) + got_ref[m, rows].astype(F32)).astype(BF16)


def first_sums(rng, keep, got):
    half = keep.shape[1] // 2
    low = lambda ref: ref.at[1, 0:half]
    high = lambda ref: ref.at[:, half : 2 * half]
    return call(
        first_body,
        rng,
        [(keep, low, (half, 128)), (got, low, (half, 128)), (keep, high, (2, half, 128)), (got, high, (2, half, 128))],
        [((half, 128), BF16), ((2, half // 2, 128), BF16)],
        [],
        loose=[got],
    )


def partner(x, axis, mask):
    n = lax.axis_size(axis)
    return lax.ppermute(x, axis, [(i, i ^ mask) for i in range(n)])


def add(a, b):
    return (a.astype(F32) + b.astype(F32)).astype(BF16)


def after(x, *deps):
    return lax.optimization_barrier((x, *deps))[0]


def half_of(x, bit):
    half = x.shape[0] // 2
    return lax.dynamic_slice_in_dim(x, bit * half, half, 0)


def dp_bit(j):
    return (lax.axis_index("dp") >> j) & 1


class Flow:
    def __init__(self, keep, send):
        bits = lax.axis_size("dp").bit_length() - 1
        self.steps = [("core", 0), ("chip", 0)]
        self.steps += [("fold", j) for j in range(bits)]
        self.steps += [("join", j) for j in reversed(range(bits))]
        self.keep, self.out, self.cur, self.got = keep, send, None, None

    def done(self):
        return not self.steps

    def begin(self):
        if self.done():
            return
        kind, j = self.steps[0]
        if kind == "core":
            self.got = partner(self.out, "seq", 1)
        elif kind == "chip":
            self.got = partner(self.out, "seq", 2)
        elif kind == "fold":
            self.got = partner(half_of(self.cur, 1 - dp_bit(j)), "dp", 1 << j)
        else:
            self.got = partner(self.cur, "dp", 1 << j)

    def end(self, *deps):
        if self.done():
            return
        kind, j = self.steps.pop(0)
        got = after(self.got, *deps) if deps else self.got
        if kind == "core":
            self.out = add(self.keep[1], got[1])
            self.cur = add(self.keep[0], got[0])
        elif kind == "chip":
            self.cur = add(self.cur, got)
        elif kind == "fold":
            self.cur = add(half_of(self.cur, dp_bit(j)), got)
        else:
            low = dp_bit(j) == 0
            self.cur = jnp.where(low, jnp.concatenate([self.cur, got]), jnp.concatenate([got, self.cur]))

    def state(self):
        return self.out if self.steps and self.steps[0][0] == "chip" else self.cur


class SplitFlow:
    def __init__(self, rng, keep, got):
        half = keep.shape[1] // 2
        self.keep, self.arrived, self.half = keep, got, half
        self.far, self.other = first_sums(rng, keep, got)
        bits = lax.axis_size("dp").bit_length() - 1
        self.steps = ["cross", "back"] + [("fold", j) for j in range(1, bits)]
        self.steps += [("join", j) for j in reversed(range(1, bits))] + ["last"]
        self.cur = self.got = None

    def done(self):
        return not self.steps

    def begin(self):
        if self.done():
            return
        step = self.steps[0]
        if step == "cross":
            self.got = (partner(self.far, "seq", 2), partner(self.other, "dp", 1))
        elif step == "back":
            self.got = (partner(half_of(self.low, 1 - dp_bit(0)), "dp", 1), partner(self.high[1], "seq", 2))
        elif step == "last":
            self.got = partner(self.cur, "dp", 1)
        elif step[0] == "fold":
            self.got = partner(half_of(self.cur, 1 - dp_bit(step[1])), "dp", 1 << step[1])
        else:
            self.got = partner(self.cur, "dp", 1 << step[1])

    def end(self, *deps):
        if self.done():
            return
        step = self.steps.pop(0)
        if step in ("cross", "back"):
            one, two = after(self.got[0], *deps), after(self.got[1], *deps)
        else:
            got = after(self.got, *deps)
        if step == "cross":
            keep, got, half = after(self.keep, *deps), after(self.arrived, *deps), self.half
            self.low = add(keep[0, :half].astype(F32) + got[0, :half].astype(F32), one)
            at = half + dp_bit(0) * (half // 2)
            mine = [lax.dynamic_slice_in_dim(x, at, half // 2, 1).astype(F32) for x in (keep, got)]
            self.high = add(mine[0] + mine[1], two)
        elif step == "back":
            self.cur = jnp.concatenate([add(half_of(self.low, dp_bit(0)), one), add(self.high[0], two)])
        elif step == "last":
            low = dp_bit(0) == 0
            a, b = jnp.where(low, self.cur, got), jnp.where(low, got, self.cur)
            half = a.shape[0] // 2
            self.cur = jnp.concatenate([a[:half], b[:half], a[half:], b[half:]])
        elif step[0] == "fold":
            self.cur = add(half_of(self.cur, dp_bit(step[1])), got)
        else:
            low = dp_bit(step[1]) == 0
            self.cur = jnp.where(low, jnp.concatenate([self.cur, got]), jnp.concatenate([got, self.cur]))

    def state(self):
        if self.cur is not None:
            return (self.cur,)
        return (self.far, self.other) if self.steps[0] == "cross" else (self.low, self.high)


def local(
    target, memory, cotangent, target_segments, source_segments, target_lengths, source_lengths,
    self_inproj, self_outproj, cross_query, cross_keyval, cross_outproj, ffn_expand, ffn_reduce,
    expand_bias, proj_bias, norm_gain, norm_shift,
):
    target, memory, cotangent = target[0], memory[0], cotangent[0]
    length, width = target.shape
    shards = lax.axis_size("seq")
    shard = lax.axis_index("seq").astype(jnp.int32)
    unit = 16 * lax.axis_size("dp")

    def eight(x):
        return jnp.pad(x.astype(F32), ((0, 8 - x.shape[0]), (0, 0)))

    expand_bias, proj_bias = eight(expand_bias), eight(proj_bias)
    norm_gain, norm_shift = eight(norm_gain), eight(norm_shift)
    t2 = partner(target, "seq", 2)
    t1 = partner(target, "seq", 1)
    m1 = partner(memory, "seq", 1)
    self_rng, cross_rng, fq, self_fk, cross_fk, self_fkt, cross_fkt = prepare(
        shard, target_lengths, source_lengths, target_segments, source_segments, length
    )
    t2 = after(t2, self_rng, expand_bias, proj_bias, norm_gain, norm_shift)
    t3 = partner(t2, "seq", 1)
    m2 = partner(after(memory, t2), "seq", 2)
    target_parts = [target, t1, t2, t3]

    q1, k1, v1, o1, lse1, a1, n0, r0, q2, target_t, a1_t = self_forward(
        self_rng, target_parts, fq, self_fkt, self_inproj, self_outproj, cross_query, proj_bias,
        norm_gain, norm_shift,
    )
    m2 = after(m2, q2)
    memory_parts = [memory, m1, m2, partner(m2, "seq", 1)]
    k2, v2, o2, lse2, layer_out, do2, dh2, keep_a, send_a, deb, small2, memory_t = cross_forward(
        cross_rng, memory_parts, fq, cross_fkt, q2, a1, cotangent, cross_keyval, cross_outproj,
        ffn_expand, ffn_reduce, expand_bias, proj_bias, norm_gain, norm_shift,
    )
    got_a = partner(send_a, "seq", 1)

    def cross_back(pairs, *deps, **pack):
        rng = after(cross_rng, *deps) if deps else cross_rng
        return attend_backward(
            rng, pairs, q2, fq, lse2, do2, o2, cross_fk, k2, v2, a1_t, memory_t, False, **pack
        )

    def self_back(p, *deps, **pack):
        rng = after(self_rng, *deps) if deps else self_rng
        return attend_backward(
            rng, [p], q1, fq, lse1, do1, o1, self_fk, k1, v1, target_t, target_t, True, **pack
        )

    c0, c1, _ = cross_back([0, 1])
    got_a = after(got_a, c1[0])
    flow_a = SplitFlow(cross_rng, keep_a, got_a)
    flow_a.begin()
    rows_b = ((2, 4 * width, 128), BF16, 2)
    half = ((2, length, width), BF16)
    c2, c3, (mem_keep, mem_send, dh1, do1, keep_b, send_b, small0) = cross_back(
        [2, 3], c1[0], *flow_a.state(), pack=pack_memory,
        extra=(
            cross_keyval, c0[1], c1[1], c0[0], c1[0], c0[2], c1[2], cross_query, dh2, n0, r0, norm_gain,
            self_outproj, o1,
        ),
        packed=(
            half, half, ((length, width), F32), ((length, width), BF16), rows_b, ((8, width), F32),
        ),
        more=[((length, width), BF16)],
        vmem=36,
    )
    cross = (c0, c1, c2, c3)
    mem_got = partner(mem_send, "seq", 1)
    flow_b = Flow(keep_b, send_b)
    flow_b.begin()
    flow_a.end(do1)
    flow_a.begin()
    s0 = self_back(0, *flow_a.state(), do1)[0]
    mem_far = add(mem_keep[1], after(mem_got, s0[0])[1])
    mem_get = partner(mem_far, "seq", 2)
    flow_a.end(s0[0])
    flow_b.end(s0[0])
    flow_a.begin()
    flow_b.begin()
    s1 = self_back(1, *flow_a.state(), flow_b.state(), mem_far, s0[0])[0]
    flow_a.end(s1[0])
    flow_b.end(s1[0])
    flow_a.begin()
    flow_b.begin()
    s2, (keep_c, send_c) = self_back(
        2, *flow_a.state(), flow_b.state(), s1[0], pack=pack_early, extra=(s0[2], s1[2]), packed=[((2, 2 * width, 128), BF16, 2)],
    )
    got_c = partner(send_c, "seq", 2)
    flow_a.end(s2[0])
    flow_b.end(s2[0])
    flow_a.begin()
    flow_b.begin()
    s3, (keep_d, send_d) = self_back(
        3, *flow_a.state(), flow_b.state(), s2[0], pack=pack_late,
        extra=(s2[2], s0[3], s1[3], s2[3], c0[3], c1[3], c2[3], c3[3], small0, small2, deb),
        packed=[((2, width + unit, 128), BF16, 2)],
    )
    selfs = (s0, s1, s2, s3)
    got_d = partner(send_d, "seq", 1)
    two_c = add(keep_c, after(got_c, s3[0]))
    core_c = partner(two_c[1], "seq", 1)
    flow_a.end(s3[0])
    flow_b.end(s3[0])
    flow_a.begin()
    flow_b.begin()
    far_d, near_d = add(keep_d[1], got_d[1]), add(keep_d[0], got_d[0])
    get_d = partner(far_d, "seq", 2)
    tgt_keep, tgt_send = spread_keys(
        after(self_rng, far_d, two_c, *flow_a.state(), flow_b.state()), [s[1] for s in selfs], self_inproj,
        length, True, width,
    )
    get_d, core_c = after(get_d, tgt_keep), after(core_c, tgt_keep)
    tgt_got = partner(tgt_send, "seq", 1)
    flow_a.end(tgt_keep)
    flow_b.end(tgt_keep)
    flow_a.begin()
    flow_b.begin()
    block = jnp.concatenate([add(two_c[0], core_c), add(near_d, get_d)])
    tgt_far = add(tgt_keep[1], tgt_got[1])
    tgt_get = partner(tgt_far, "seq", 2)
    block = after(block, tgt_far)
    devices = lax.axis_size("dp")
    parts = lax.all_to_all(block.reshape(devices, -1, 128), "dp", 0, 0, tiled=True)
    partial = target_partial(
        after(self_rng, block), self_inproj, [s[0] for s in selfs], dh1, tgt_keep, tgt_got
    )
    flow_b.end(partial)
    flow_b.begin()
    parts = after(parts, partial, flow_b.state(), tgt_get)
    part = jnp.sum(parts.astype(F32), axis=0).astype(BF16)
    flow_b.end(part)
    flow_b.begin()
    spread_part = after(jnp.broadcast_to(part[None], parts.shape), flow_b.state())
    whole = lax.all_to_all(spread_part, "dp", 0, 0, tiled=True).reshape(-1, 128)
    flow_a.end(part)
    while not flow_a.done():
        flow_a.begin()
        flow_a.end()
    target_grad, memory_grad, expand_grad, reduce_grad, outproj_grad = first_outputs(
        after(self_rng, spread_part), partial, tgt_get, mem_keep, mem_got, mem_get, flow_a.cur,
        ffn_expand.shape[1], shards,
    )
    flow_b.end(target_grad)
    while not flow_b.done():
        flow_b.begin()
        flow_b.end()
    self_in, self_out_grad, query_grad, keyval_grad, eb_grad, pb_grad, gain_grad, shift_grad = finish(
        self_rng, after(whole, target_grad), flow_b.cur, width
    )
    return (
        layer_out[None],
        target_grad[None],
        memory_grad[None],
        self_in,
        self_out_grad,
        query_grad,
        keyval_grad,
        outproj_grad,
        expand_grad,
        reduce_grad,
        eb_grad,
        pb_grad,
        gain_grad,
        shift_grad,
    )


def solution(mesh):
    rows, shard = P("dp", "seq", None), P(None, "seq")
    in_specs = (rows, rows, rows, P("dp", None), P("dp", None), P("dp"), P("dp")) + (P(),) * 11
    out_specs = (rows, rows, rows) + (shard,) * 11
    return jax.shard_map(local, mesh=mesh, in_specs=in_specs, out_specs=out_specs, check_vma=False)
```
